32 devices in a mesh: section: 2 (over core), seq: 4 (over z), head: 4 (over y, x).
Axes of the slice: x: 2, y: 2, z: 4, core: 2. Of those that a mesh axis runs over, the one named last changes fastest.
Arguments:
- hidden_in: float32 [4, 1024, 1024], P(None, 'seq'), may hold values from -6 to 6
- cotangent: float32 [4, 1024, 1024], P(None, 'seq'), may hold values from -6 to 6
- segments: int32 [4, 1024], P(None, 'seq'), may hold values from 0 to 6, as said below
- padding: int32 [4, 1024], P(None, 'seq'), may hold values from 0 to 1, as said below
- norm_gain: float32 [2, 1024], P('section'), may hold values from 0.5 to 1.5
- w_zx: bfloat16 [2, 1024, 2, 2048], P('section', None, None, 'head'), may hold values from -0.1875 to 0.1875
- w_bc: bfloat16 [2, 1024, 256], P('section'), may hold values from -0.1875 to 0.1875
- w_dt: bfloat16 [2, 1024, 32], P('section', None, 'head'), may hold values from -0.1875 to 0.1875
- conv_x: float32 [2, 4, 2048], P('section', None, 'head'), may hold values from -3 to 3
- conv_x_bias: float32 [2, 2048], P('section', 'head'), may hold values from -3 to 3
- conv_bc: float32 [2, 4, 256], P('section'), may hold values from -3 to 3
- conv_bc_bias: float32 [2, 256], P('section'), may hold values from -3 to 3
- dt_bias: float32 [2, 32], P('section', 'head'), may hold values from -9 to -2
- a_log: float32 [2, 32], P('section', 'head'), may hold values from -3 to 1
- skip_d: float32 [2, 32], P('section', 'head'), may hold values from 0.5 to 1.5
- gate_gain: float32 [2, 2048], P('section', 'head'), may hold values from 0.5 to 1.5
- w_out: bfloat16 [2, 2048, 1024], P('section', 'head'), may hold values from -0.125 to 0.125
Outputs:
- layer_out: float32 [2, 4, 1024, 1024], P('section', None, 'seq')
- input_grad: float32 [2, 4, 1024, 1024], P('section', None, 'seq')
- rms: float32 [2, 2], P('section')
- grad_norm_gain: float32 [2, 1024], P('section')
- grad_w_zx: float32 [2, 1024, 2, 2048], P('section', None, None, 'head')
- grad_w_bc: float32 [2, 1024, 256], P('section')
- grad_w_dt: float32 [2, 1024, 32], P('section', None, 'head')
- grad_conv_x: float32 [2, 4, 2048], P('section', None, 'head')
- grad_conv_x_bias: float32 [2, 2048], P('section', 'head')
- grad_conv_bc: float32 [2, 4, 256], P('section')
- grad_conv_bc_bias: float32 [2, 256], P('section')
- grad_dt_bias: float32 [2, 32], P('section', 'head')
- grad_a_log: float32 [2, 32], P('section', 'head')
- grad_skip_d: float32 [2, 32], P('section', 'head')
- grad_gate_gain: float32 [2, 2048], P('section', 'head')
- grad_w_out: float32 [2, 2048, 1024], P('section', 'head')
The draws below stay inside these ranges and needn't reach their ends.
Inputs may be any that keep to these rules, and one draw needn't show every extreme that they name: `segments`: along each row non-decreasing from 0; documents hold 200 to 2000 tokens, except the last one before the padding, which may be shorter; in one row drawn from the seed a single document fills every token before the padding; in another row drawn from the seed every document but the last holds exactly 200 tokens and the padding is a single token; the padding of a row is one final segment of its own. `padding`: each row is 1 on a prefix and 0 on its last 1 to 199 tokens.
All inputs are finite; a program needn't handle non-finite values.
Results may differ from the reference program's by a relative error of at most 0.018.
Values may be sent and summed in bfloat16 or wider, within the bound.
A program may use at most 192 MiB of HBM per device.

```python
import jax
import jax.numpy as jnp
from jax import lax

D = 1024
DI = 2048
NH = 32
HP = 64
DS = 128
KC = 4
SPAN = 256
MICRO = 4
DOC_MIN = 200
DOC_MAX = 2000
SEQ_LEN = 1024


def packing(key):
    key_pad, key_row, key_len, key_dense = jax.random.split(key, 4)
    chosen = jax.random.randint(key_row, (), 0, MICRO)
    dense = (chosen + jax.random.randint(key_dense, (), 1, MICRO)) % MICRO
    row_index = jnp.arange(MICRO)
    pad_length = jax.random.randint(key_pad, (MICRO,), 1, DOC_MIN)
    pad_length = jnp.where(row_index == dense, 1, pad_length)
    doc_slots = SEQ_LEN // DOC_MIN + 1
    lengths = jax.random.randint(key_len, (MICRO, doc_slots), DOC_MIN, DOC_MAX + 1)
    lengths = jnp.where((row_index == dense)[:, None], DOC_MIN, lengths)
    doc_ends = jnp.cumsum(lengths, axis=1)
    positions = jnp.arange(SEQ_LEN)
    seg_ids = jnp.sum((doc_ends[:, None, :] <= positions[None, :, None]).astype(jnp.int32), axis=2)
    is_live = positions[None, :] < (SEQ_LEN - pad_length)[:, None]
    last_live = jnp.take_along_axis(seg_ids, (SEQ_LEN - pad_length - 1)[:, None], axis=1)
    seg_ids = jnp.where(is_live, seg_ids, last_live + 1)
    single = jnp.where(is_live, 0, 1)
    seg_ids = jnp.where((row_index == chosen)[:, None], single, seg_ids)
    return (seg_ids.astype(jnp.int32), is_live.astype(jnp.int32))


def draw_segments(key, part):
    return packing(key)[0]


def draw_padding(key, part):
    return packing(key)[1]


def block_levels(key, shape, cuts, least, largest):
    def one(dim, parts):
        draws = jax.random.uniform(jax.random.fold_in(jax.random.fold_in(key, 6), dim), (parts,), jnp.float32, least / len(cuts), largest / len(cuts))
        return jnp.repeat(jnp.exp(draws), shape[dim] // parts).reshape((-1,) + (1,) * (len(shape) - dim - 1))

    gain = one(*cuts[0])
    for cut in cuts[1:]:
        gain = gain * one(*cut)
    return gain


def bell_draw(key, extent, deviation, reach, cuts=(), kind=jnp.bfloat16):
    result = jax.random.normal(key, extent, jnp.float32) * deviation
    if len(cuts) > 0:
        result = block_levels(key, extent, cuts, -0.22, 0.18) * result
    return jnp.clip(result, min=-reach, max=reach).astype(kind)


def setup_inputs(seed: int = 0) -> dict:
    seeds = jax.random.split(jax.random.key(seed), 18)
    hidden_in = bell_draw(seeds[0], (MICRO, SEQ_LEN, D), 1.0, 6.0, ((1, 4),), jnp.float32)
    cotangent = bell_draw(seeds[1], (MICRO, SEQ_LEN, D), 1.0, 6.0, ((1, 4),), jnp.float32)
    segments = draw_segments(jax.random.fold_in(seeds[17], 71), 0)
    padding = draw_padding(jax.random.fold_in(seeds[17], 71), 0)
    norm_gain = jnp.clip(1.0 + 0.1 * jax.random.normal(seeds[4], (2, D), jnp.float32), 0.5, 1.5)
    w_zx = bell_draw(seeds[5], (2, D, 2, DI), D ** -0.5, 0.1875, ((0, 2), (3, 4)))
    w_bc = bell_draw(seeds[6], (2, D, 2 * DS), D ** -0.5, 0.1875, ((0, 2),))
    w_dt = bell_draw(seeds[7], (2, D, NH), D ** -0.5, 0.1875, ((0, 2), (2, 4)))
    conv_x = bell_draw(seeds[8], (2, KC, DI), KC ** -0.5, 3.0, ((0, 2), (2, 4)), jnp.float32)
    conv_x_bias = bell_draw(seeds[9], (2, DI), 0.5, 3.0, ((0, 2), (1, 4)), jnp.float32)
    conv_bc = bell_draw(seeds[10], (2, KC, 2 * DS), KC ** -0.5, 3.0, ((0, 2),), jnp.float32)
    conv_bc_bias = bell_draw(seeds[11], (2, 2 * DS), 0.5, 3.0, ((0, 2),), jnp.float32)
    dt_bias = jnp.clip(-9.0 + 7.0 * jax.random.uniform(seeds[12], (2, NH), jnp.float32) ** block_levels(seeds[12], (2, NH), ((0, 2), (1, 4)), -0.2, 0.2), -9.0, -2.0)
    a_log = jnp.clip(-3.0 + 4.0 * jax.random.uniform(seeds[13], (2, NH), jnp.float32) ** block_levels(seeds[13], (2, NH), ((0, 2), (1, 4)), -0.2, 0.2), -3.0, 1.0)
    skip_d = jnp.clip(0.5 + 1.0 * jax.random.uniform(seeds[14], (2, NH), jnp.float32) ** block_levels(seeds[14], (2, NH), ((0, 2), (1, 4)), -0.2, 0.2), 0.5, 1.5)
    gate_gain = jnp.clip(1.0 + 0.1 * jax.random.normal(seeds[15], (2, DI), jnp.float32), 0.5, 1.5)
    w_out = bell_draw(seeds[16], (2, DI, D), DI ** -0.5, 0.125, ((0, 2), (1, 4)))
    return {"hidden_in": hidden_in, "cotangent": cotangent, "segments": segments, "padding": padding, "norm_gain": norm_gain, "w_zx": w_zx, "w_bc": w_bc, "w_dt": w_dt, "conv_x": conv_x, "conv_x_bias": conv_x_bias, "conv_bc": conv_bc, "conv_bc_bias": conv_bc_bias, "dt_bias": dt_bias, "a_log": a_log, "skip_d": skip_d, "gate_gain": gate_gain, "w_out": w_out}


epsilon = 1e-05
highest = lax.Precision.HIGHEST

@jax.custom_vjp
def low(v):
    return lax.optimization_barrier(v.astype(jnp.bfloat16)).astype(jnp.float32)

@jax.custom_vjp
def low_back(v):
    return v

def low_keep(v):
    return (low(v), None)

def low_pass(kept, grad):
    return (grad,)

def back_keep(v):
    return (v, None)

def back_low(kept, grad):
    return (low(grad),)
low.defvjp(low_keep, low_pass)
low_back.defvjp(back_keep, back_low)

def convolve(values, kernel, bias_row, segment):
    length = values.shape[0]
    padded = jnp.concatenate([jnp.zeros((KC - 1, values.shape[1]), jnp.float32), values], axis=0)
    padded_ids = jnp.concatenate([jnp.full((KC - 1,), -1, jnp.int32), segment])
    running = jnp.zeros_like(values) + bias_row
    for offset in range(KC):
        same_seg = (padded_ids[offset:offset + length] == segment).astype(jnp.float32)
        running = running + kernel[offset] * padded[offset:offset + length] * same_seg[:, None]
    return running

def ssd_block(carry, pieces):
    carried, before = carry
    values, input_b, input_c, steps_dt, rates, seg_ids = pieces
    cumulative = jnp.cumsum(rates, axis=0)
    positions = jnp.arange(seg_ids.shape[0])
    causal = (seg_ids[:, None] == seg_ids[None, :]) & (positions[:, None] >= positions[None, :])
    causal_heads = causal[None]
    spread = cumulative.T[:, :, None] - cumulative.T[:, None, :]
    decay_mat = jnp.where(causal_heads, jnp.exp(jnp.where(causal_heads, spread, 0.0)), 0.0)
    inner_cb = jnp.dot(input_c, input_b.T, precision=highest)
    mixing = low(inner_cb[None] * decay_mat * steps_dt.T[:, None, :])
    local_y = jnp.einsum('hts,shp->thp', mixing, values, precision=highest)
    entry_gain = jnp.exp(cumulative) * (seg_ids == before).astype(jnp.float32)[:, None]
    readout = jnp.einsum('tn,hpn->thp', input_c, carried, precision=highest)
    last_id = seg_ids[-1]
    toward = jnp.exp(cumulative[-1][None, :] - cumulative) * (seg_ids == last_id).astype(jnp.float32)[:, None] * steps_dt
    contrib = jnp.einsum('shp,sn->hpn', values * toward[:, :, None], input_b, precision=highest)
    carry_decay = jnp.exp(cumulative[-1]) * (last_id == before).astype(jnp.float32)
    new_state = carry_decay[:, None, None] * carried + contrib
    return ((new_state, last_id), local_y + entry_gain[:, :, None] * readout)

def one_layer(weights, hidden, segment):
    norm_gain, w_zx, w_bc, w_dt, conv_x, conv_x_bias, conv_bc, conv_bc_bias, dt_bias, a_log, skip_d, gate_gain, w_out = weights
    length = hidden.shape[0]
    blocks = length // SPAN
    scale_in = lax.rsqrt(lax.optimization_barrier(jnp.mean(hidden * hidden, axis=1, keepdims=True)) + epsilon)
    normed = low(hidden * scale_in * norm_gain)
    project = low_back(jnp.einsum('td,dki->tki', normed, w_zx, precision=highest))
    gate_z = project[:, 0]
    raw_x = low(project[:, 1])
    raw_bc = low(low_back(jnp.dot(normed, w_bc, precision=highest)))
    raw_dt = low_back(jnp.dot(normed, w_dt, precision=highest))
    conv_values = low(jax.nn.silu(convolve(raw_x, conv_x, conv_x_bias, segment)))
    conv_shared = low(jax.nn.silu(convolve(raw_bc, conv_bc, conv_bc_bias, segment)))
    steps_dt = jax.nn.softplus(raw_dt + dt_bias)
    rates = steps_dt * -jnp.exp(a_log)
    values = conv_values.reshape(blocks, SPAN, NH, HP)
    input_b = conv_shared[:, :DS].reshape(blocks, SPAN, DS)
    input_c = conv_shared[:, DS:].reshape(blocks, SPAN, DS)
    start_carry = (jnp.zeros((NH, HP, DS), jnp.float32), jnp.array(-1, jnp.int32))
    end_carry, mixed_y = lax.scan(jax.checkpoint(ssd_block), start_carry, (values, input_b, input_c, steps_dt.reshape(blocks, SPAN, NH), rates.reshape(blocks, SPAN, NH), segment.reshape(blocks, SPAN)))
    ssd_out = low_back(mixed_y + skip_d[None, None, :, None] * values).reshape(length, DI)
    gated = ssd_out * jax.nn.silu(gate_z)
    gate_scale = lax.rsqrt(lax.optimization_barrier(jnp.mean(gated * gated, axis=1, keepdims=True)) + epsilon)
    normed_gate = low(gated * gate_scale * gate_gain)
    branch = low_back(jnp.dot(normed_gate, w_out, precision=highest))
    return (hidden + branch, branch)

def reference(hidden_in, cotangent, segments, padding, norm_gain, w_zx, w_bc, w_dt, conv_x, conv_x_bias, conv_bc, conv_bc_bias, dt_bias, a_log, skip_d, gate_gain, w_out):
    stacked = (norm_gain, w_zx, w_bc, w_dt, conv_x, conv_x_bias, conv_bc, conv_bc_bias, dt_bias, a_log, skip_d, gate_gain, w_out)
    weights_one = tuple((piece[0].astype(jnp.float32) for piece in stacked))
    weights_two = tuple((piece[1].astype(jnp.float32) for piece in stacked))

    def per_batch(totals, batch_rows):
        sum_one, sum_two, squares = totals
        source, upstream, segment, keep_mask = batch_rows
        keep_f = keep_mask.astype(jnp.float32)

        def apply_layer(weights, hidden):
            return one_layer(weights, hidden, segment)
        (middle, branch_one), pull_one = jax.vjp(apply_layer, weights_one, source)
        (final_out, branch_two), pull_two = jax.vjp(apply_layer, weights_two, middle)
        grad_two, grad_middle = pull_two((upstream * keep_f[:, None], jnp.zeros_like(branch_two)))
        grad_one, grad_source = pull_one((grad_middle, jnp.zeros_like(branch_one)))
        sum_one = tuple((first_sum + first_new for first_sum, first_new in zip(sum_one, grad_one)))
        sum_two = tuple((second_sum + second_new for second_sum, second_new in zip(sum_two, grad_two)))
        row_sums = jnp.stack([jnp.sum(keep_f * lax.optimization_barrier(jnp.sum(middle * middle, axis=1))), jnp.sum(keep_f * lax.optimization_barrier(jnp.sum(branch_one * branch_one, axis=1))), jnp.sum(keep_f * lax.optimization_barrier(jnp.sum(final_out * final_out, axis=1))), jnp.sum(keep_f * lax.optimization_barrier(jnp.sum(branch_two * branch_two, axis=1))), jnp.sum(keep_f)])
        return ((sum_one, sum_two, squares + row_sums), (middle, final_out, grad_source, grad_middle))
    start_totals = (tuple((jnp.zeros_like(piece) for piece in weights_one)), tuple((jnp.zeros_like(piece) for piece in weights_two)), jnp.zeros((5,), jnp.float32))
    (sum_one, sum_two, squares), (middles, finals, grad_sources, grad_middles) = lax.scan(per_batch, start_totals, (hidden_in, cotangent, segments, padding))
    rms = jnp.sqrt(jnp.stack([squares[0:2], squares[2:4]]) / (squares[4] * D))
    layer_out = jnp.stack([middles, finals])
    input_grad = jnp.stack([grad_sources, grad_middles])
    grads = tuple((jnp.stack([piece_one, piece_two]) for piece_one, piece_two in zip(sum_one, sum_two)))
    return (layer_out, input_grad, rms, grads[0], grads[1], grads[2], grads[3], grads[4], grads[5], grads[6], grads[7], grads[8], grads[9], grads[10], grads[11], grads[12])
```

```python
import functools

import jax
import jax.numpy as jnp
from jax import lax
from jax.experimental import pallas as pl
from jax.experimental.pallas import tpu as pltpu
from jax.sharding import PartitionSpec as P

SEC, SEQ, HEAD = "section", "seq", "head"
F32, BF = jnp.float32, jnp.bfloat16
MESH = pl.DeviceIdType.MESH
HIGH = lax.Precision.HIGHEST
EPS = 1e-05
KC = 4
HALO = 16
LANES = 128
HEAD_SHIFT = 6
LIMIT = 58 << 20
CHUNK = 32
SKEW = 2
TOTAL_T = jnp.bfloat16


def mm(a, b, precision=None):
    return lax.dot_general(
        a, b, (((1,), (0,)), ((), ())), precision=precision, preferred_element_type=F32
    )


def mm_nt(a, b):
    return lax.dot_general(a, b, (((1,), (1,)), ((), ())), preferred_element_type=F32)


def mm_tn(a, b, precision=None):
    return lax.dot_general(
        a, b, (((0,), (0,)), ((), ())), precision=precision, preferred_element_type=F32
    )


def iota(shape, dim):
    return lax.broadcasted_iota(jnp.int32, shape, dim)


def spread_matrix(width):
    shape = (LANES, width)
    return (iota(shape, 0) == jnp.right_shift(iota(shape, 1), HEAD_SHIFT)).astype(BF)


def split(x):
    high = x.astype(BF)
    return high, (x - high.astype(F32)).astype(BF)


def expand(x, matrix):
    high, low = split(x)
    return mm(high, matrix) + mm(low, matrix)


def head_sums(x, matrix):
    high, low = split(x)
    return mm_nt(high, matrix) + mm_nt(low, matrix)


def fine(product, a, b):
    high, low = split(a)
    return product(high, b) + product(low, b)


def two_lanes(column):
    high = column.astype(BF).astype(F32)
    lane = iota((column.shape[0], LANES), 1)
    return jnp.where(lane == 0, high, jnp.where(lane == 1, column - high, 0.0)).astype(BF)


def sigmoid(v):
    return 1.0 / (1.0 + jnp.exp(-v))


def lower(size):
    return (iota((size, size), 0) >= iota((size, size), 1)).astype(F32)


def same_rows(seg_ref, mb, tokens):
    mine = seg_ref[mb, HALO:]
    first = HALO - KC + 1
    return [
        (seg_ref[mb, first + k : first + k + tokens] == mine).astype(F32) for k in range(KC)
    ]


def convolved(raw_f, same, prm, col, tokens):
    first = HALO - KC + 1
    cols = slice(col, col + LANES)
    pre = jnp.zeros((tokens, LANES), F32) + prm[5:6, cols]
    for k in range(KC):
        pre = pre + prm[1 + k : 2 + k, cols] * raw_f[first + k : first + k + tokens, cols] * same[k]
    return pre


def gains(cum, seg_ref, mb):
    mine = seg_ref[mb, HALO:]
    before = seg_ref[mb, HALO - 1 : HALO]
    last = mine[-1:]
    entry = jnp.exp(cum) * (mine == before).astype(F32)
    decay_end = jnp.exp(cum[-1:] - cum) * (mine == last).astype(F32)
    return entry, decay_end


def place():
    return lax.axis_index(SEC), lax.axis_index(SEQ), lax.axis_index(HEAD)


def remote(src, dst, send, recv, device):
    return pltpu.make_async_remote_copy(
        src_ref=src, dst_ref=dst, send_sem=send, recv_sem=recv, device_id=device,
        device_id_type=MESH,
    )


def greet(device):
    pl.semaphore_signal(
        pltpu.get_barrier_semaphore(), inc=1, device_id=device, device_id_type=MESH
    )


def await_greets(count):
    pl.semaphore_wait(pltpu.get_barrier_semaphore(), count)


def one_if(condition):
    return condition.astype(jnp.int32)


def comm(kernel, ins, outs, scratch, ident, name, in_hbm=0, from_hbm=0):
    sources = [pl.ANY] * from_hbm + [pltpu.VMEM] * (len(ins) - from_hbm)
    spaces = [pltpu.VMEM] * (len(outs) - in_hbm) + [pl.ANY] * in_hbm
    return pl.pallas_call(
        kernel,
        in_specs=[pl.BlockSpec(memory_space=space) for space in sources],
        out_specs=[pl.BlockSpec(memory_space=space) for space in spaces],
        out_shape=[jax.ShapeDtypeStruct(s, d) for s, d in outs],
        scratch_shapes=scratch,
        compiler_params=pltpu.CompilerParams(
            collective_id=ident, has_side_effects=True, vmem_limit_bytes=LIMIT
        ),
        name=name,
    )(*ins)


DMA = pltpu.SemaphoreType.DMA


def swap_kernel(seqs, wc, wo, pr, edge, wc_o, wo_o, pr_o, edge_o, send, recv):
    s, q, h = place()
    other = (1 - s, q, h)
    greet(other)

    @pl.when(q > 0)
    def _():
        greet((s, q - 1, h))

    await_greets(1 + one_if(q < seqs - 1))

    pairs = ((wc, wc_o), (wo, wo_o), (pr, pr_o))
    sends = [
        remote(a, b.at[s], send.at[i], recv.at[i], other) for i, (a, b) in enumerate(pairs)
    ]
    for c in sends:
        c.start()
    edge_copy = remote(edge, edge_o, send.at[3], recv.at[3], (s, q + 1, h))

    @pl.when(q < seqs - 1)
    def _():
        edge_copy.start()

    for a, b in pairs:
        b[s] = a[...]
    for c in sends:
        c.wait_send()
    for i, (a, b) in enumerate(pairs):
        remote(a, b.at[1 - s], send.at[i], recv.at[i], other).wait_recv()

    @pl.when(q < seqs - 1)
    def _():
        edge_copy.wait_send()

    @pl.when(q > 0)
    def _():
        edge_copy.wait_recv()


def finer(a, b):
    a_high, a_low = split(a)
    b_high, b_low = split(b)
    return mm(a_high, b_high) + mm(a_low, b_high) + mm(a_high, b_low)


def wide_copy(x, width):
    return jnp.concatenate([x] * (width // LANES), axis=1)


def causal_mask(seg_ref, srow_ref, mb, tokens, transposed):
    row = iota((tokens, tokens), 0)
    col = iota((tokens, tokens), 1)
    same = wide_copy(seg_ref[mb, HALO:], tokens) == srow_ref[mb, 0:1]
    return same & ((row <= col) if transposed else (row >= col))


def when(condition):
    return pl.when(condition)


def both(a, b):
    return jnp.logical_and(a, b)


def fwd_kernel(seqs, n, hid, halo, seg, srow, pad, wc, wo, pr,
               normed, raw, z, dtp, dt, cum, co, st, car, yn, gsc, stats, lo,
               h1, raw_f, con, sbuf, gated_s, part0, part, rbuf0, rbuf, ssend, srecv, lo1,
               c_s, c_r, q_s, q_r, s_s, s_r, g_s, g_r, h_s, h_r, l_c, l_s, l_r):
    s, q, h = place()
    count, tokens, model = hid.shape
    inner = wo.shape[1]
    wide = raw.shape[2]
    heads = inner >> HEAD_SHIFT
    rows = tokens // n
    units = 2 * count
    full = inner * n
    half = inner // 2
    other = (1 - s, q, h)
    first_q, last_q = q == 0, q == seqs - 1
    edge_owner = both(h == n - 1, q < seqs - 1)
    peers = [lax.rem(h + j, n) for j in range(1, n)]
    froms = [lax.rem(h + n - j, n) for j in range(1, n)]
    matrix = spread_matrix(inner)
    for p in peers:
        greet((s, q, p))
    greet(other)

    @when(q > 0)
    def _():
        greet((s, q - 1, n - 1))

    @when(both(q > 0, h < n - 1))
    def _():
        greet((s, q - 1, h))

    await_greets(n + one_if(q < seqs - 1) * (1 + (n - 1) * one_if(h == n - 1)))

    def at_rows(owner):
        return pl.ds(pl.multiple_of(owner * rows, rows), rows)

    def slot_rows(owner):
        return pl.ds(pl.multiple_of(HALO + owner * rows, HALO), rows)

    def chain(u, k):
        cut = pl.ds(k * half, half)
        return remote(
            sbuf.at[u, cut], st.at[u, cut], c_s.at[u, k], c_r.at[u, k], (s, q + 1, h)
        )

    def squares(u, j):
        return remote(
            ssend.at[u], srecv.at[u, j], q_s.at[u, j], q_r.at[u, j], (s, q, peers[j])
        )

    def scatter(u, j, layer):
        src, dst = (part, rbuf) if layer else (part0, rbuf0)
        mb = u - layer * count
        return remote(
            src.at[mb, at_rows(peers[j])], dst.at[mb, j], s_s.at[u, j], s_r.at[u, j],
            (s, q, peers[j]),
        )

    def gather(u, j, owner):
        where = (u + count, slot_rows(owner))
        return remote(
            normed.at[where], normed.at[where], g_s.at[u, j], g_r.at[u, j], (s, q, peers[j])
        )

    def edge(u, head):
        return remote(
            normed.at[u + count, pl.ds(tokens, HALO)], normed.at[u + count, pl.ds(0, HALO)],
            h_s.at[u, head], h_r.at[u], (s, q + 1, head),
        )

    def ship_local(src, mb, layer):
        return pltpu.make_async_copy(src.at[mb], lo.at[s * count + mb], l_c.at[mb])

    def ship(src, mb):
        return remote(src.at[mb], lo.at[s * count + mb], l_s.at[mb], l_r.at[mb], other)

    def send_out(src, mb, layer):
        @when(s == layer)
        def _():
            ship_local(src, mb, layer).start()

        @when(s != layer)
        def _():
            ship(src, mb).start()

    def add_stats(layer, mb, h_new, branch):
        live = pad[mb]
        stats[layer, 0:1] += jnp.sum(
            jnp.sum(h_new * h_new, axis=1, keepdims=True) * live, axis=0, keepdims=True
        )
        stats[layer, 1:2] += jnp.sum(
            jnp.sum(branch * branch, axis=1, keepdims=True) * live, axis=0, keepdims=True
        )
        stats[layer, 2:3] += jnp.sum(live, axis=0, keepdims=True)

    def pass_state(u):
        for k in range(2):
            @when(q > 0)
            def _():
                chain(u, k).wait_recv()

            @when(first_q)
            def _():
                st[u, k * half : (k + 1) * half] = jnp.zeros((half, LANES), F32)

            @when(q < seqs - 1)
            def _():
                per = inner // heads
                for i in range(k * heads // 2, (k + 1) * heads // 2):
                    cut = slice(i * per, (i + 1) * per)
                    sbuf[u, cut] = car[u, i : i + 1] * st[u, cut] + con[cut]
                chain(u, k).start()

    def in_norm(mb, _):
        hx = jnp.concatenate([halo[mb], hid[mb]], axis=0)
        scale = lax.rsqrt(jnp.mean(hx * hx, axis=1, keepdims=True) + EPS)
        normed[mb, :, :model] = (hx * scale * pr[0, 0:1]).astype(BF)
        normed[mb, :, model:] = two_lanes(scale)

        @when(first_q)
        def _():
            normed[mb + count, :HALO] = jnp.zeros((HALO, model + LANES), BF)

        return 0

    stats[...] = jnp.zeros_like(stats)
    lax.fori_loop(0, count, in_norm, 0)

    def local_part(u):
        layer = u // count
        mb = lax.rem(u, count)
        prm = pr[layer]
        x = normed[u, :, :model]
        new_raw = mm(x, wc[layer, :, inner : inner + wide]).astype(BF)
        raw[u] = new_raw
        raw_f[...] = new_raw.astype(F32)
        x = x[HALO:]
        z[u] = mm(x, wc[layer, :, :inner])
        new_dtp = mm(x, wc[layer, :, inner + wide :]) + prm[6:7, :LANES]
        dtp[u] = new_dtp
        new_dt = jax.nn.softplus(new_dtp)
        dt[u] = new_dt
        new_cum = mm(lower(tokens), new_dt * prm[7:8, :LANES], HIGH)
        cum[u] = new_cum
        cum_t = new_cum.T
        dt_t = new_dt.T
        same = same_rows(seg, mb, tokens)
        pieces = []
        for col in range(0, wide, LANES):
            pre = convolved(raw_f, same, prm, col, tokens)
            piece = (pre * sigmoid(pre)).astype(BF)
            co[u, :, col : col + LANES] = piece
            pieces.append(piece)
        values = jnp.concatenate(pieces[: inner // LANES], axis=1)
        in_b, in_c = pieces[-2], pieces[-1]
        entry, decay_end = gains(new_cum, seg, mb)
        toward = expand(decay_end * new_dt, matrix)
        con[...] = fine(mm_tn, values.astype(F32) * toward, in_b)
        mine = seg[mb, HALO:]
        same_before = (mine[-1:, :] == seg[mb, HALO - 1 : HALO]).astype(F32)
        car[u] = jnp.exp(cum_t[:heads, tokens - 1 :]) * same_before

        @when(first_q)
        def _():
            pass_state(u)

        inner_cb = jnp.where(
            causal_mask(seg, srow, mb, tokens, False), mm_nt(in_c, in_b), 0.0
        )
        lane = iota((tokens, LANES), 1)
        for pair in range(heads // 2):
            cols = slice(pair * LANES, (pair + 1) * LANES)
            acc = jnp.zeros((tokens, LANES), F32)
            for j in range(2):
                one = slice(2 * pair + j, 2 * pair + j + 1)
                decay = jnp.exp(jnp.minimum(new_cum[:, one] - cum_t[one, :], 0.0))
                mask = jnp.right_shift(lane, HEAD_SHIFT) == j
                value = jnp.where(mask, values[:, cols], jnp.zeros((), BF))
                acc = acc + mm((inner_cb * decay * dt_t[one, :]).astype(BF), value)
            yn[u, :, cols] = acc

    def gate_part(u):
        layer = u // count
        mb = lax.rem(u, count)
        entry, _ = gains(cum[u], seg, mb)
        in_c = co[u, :, inner + LANES :]
        readout = fine(lambda a, b: mm_nt(b, a), st[u], in_c)
        y = yn[u] + expand(entry, matrix) * readout
        yn[u] = y
        ssd = y + pr[layer, 8:9, :inner] * co[u, :, :inner].astype(F32)
        gate = z[u]
        gated = ssd * (gate * sigmoid(gate))
        gated_s[...] = gated
        ones = jnp.ones((8, inner), BF)
        ssend[u] = fine(lambda a, b: mm_nt(b, a), gated * gated, ones)

    def out_part(u):
        layer = u // count
        total = ssend[u]
        for j in range(n - 1):
            squares(u, j).wait_recv()
            total = total + srecv[u, j]
        scale_row = lax.rsqrt(total / full + EPS)
        scale = mm_tn(scale_row * 0.125, jnp.ones((8, LANES), F32), HIGH)
        gsc[u] = scale
        x = (gated_s[...] * wide_copy(scale, inner) * pr[layer, 9:10, :inner]).astype(BF)
        product = mm(x, wo[layer])

        @when(u < count)
        def _():
            part0[u] = product.astype(BF)
            for j in range(n - 1):
                scatter(u, j, 0).start()

        @when(u >= count)
        def _():
            part[u - count] = product.astype(BF)
            for j in range(n - 1):
                scatter(u, j, 1).start()

    def finish(u):
        @when(u < count)
        def _():
            total = part0[u, at_rows(h)].astype(F32)
            for j in range(n - 1):
                scatter(u, j, 0).wait_recv()
                total = total + rbuf0[u, j].astype(F32)
            h_new = hid[u, at_rows(h)] + total
            scale = lax.rsqrt(jnp.mean(h_new * h_new, axis=1, keepdims=True) + EPS)
            normed[u + count, slot_rows(h), :model] = (h_new * scale * pr[1, 0:1]).astype(BF)
            normed[u + count, slot_rows(h), model:] = two_lanes(scale)

        @when(u >= count)
        def _():
            total = part[u - count, at_rows(h)].astype(F32)
            for j in range(n - 1):
                scatter(u, j, 1).wait_recv()
                total = total + rbuf[u - count, j].astype(F32)
            normed[u + count, slot_rows(h), :model] = total.astype(BF)
            normed[u + count, slot_rows(h), model:] = jnp.zeros((rows, LANES), BF)

        for j in range(n - 1):
            gather(u, j, h).start()

        @when(both(u < count, edge_owner))
        def _():
            for head in range(n):
                edge(u, head).start()

    def arrived(u):
        for j in range(n - 1):
            gather(u, j, froms[j]).wait_recv()

    def step(u, _):
        @when(both(u >= count, u < units))
        def _():
            mb = u - count
            arrived(mb)

            @when(q > 0)
            def _():
                edge(mb, 0).wait_recv()

            scale = jnp.sum(normed[u, HALO:, model:].astype(F32), axis=1, keepdims=True)
            h_new = normed[u, HALO:, :model].astype(F32) / (scale * pr[1, 0:1])
            h1[mb] = h_new
            send_out(h1, mb, 0)
            add_stats(0, mb, h_new, h_new - hid[mb])

        @when(u < units)
        def _():
            local_part(u)

            @when(q > 0)
            def _():
                pass_state(u)

            gate_part(u)
            for j in range(n - 1):
                squares(u, j).start()

        @when(u > 0)
        def _():
            finish(u - 1)

        @when(u < units)
        def _():
            out_part(u)

        return 0

    lax.fori_loop(0, units + 1, step, 0)

    def last_out(mb, _):
        arrived(mb + count)
        branch = normed[mb + units, HALO:, :model].astype(F32)
        h_new = h1[mb] + branch
        lo1[mb] = h_new
        send_out(lo1, mb, 1)
        add_stats(1, mb, h_new, branch)
        return 0

    lax.fori_loop(0, count, last_out, 0)

    def drain(u, _):
        for j in range(n - 1):
            squares(u, j).wait_send()
            gather(u, j, h).wait_send()

        @when(u < count)
        def _():
            for j in range(n - 1):
                scatter(u, j, 0).wait_send()

        @when(u >= count)
        def _():
            for j in range(n - 1):
                scatter(u, j, 1).wait_send()

        @when(q < seqs - 1)
        def _():
            for k in range(2):
                chain(u, k).wait_send()

        @when(both(u < count, edge_owner))
        def _():
            for head in range(n):
                edge(u, head).wait_send()

        return 0

    lax.fori_loop(0, units, drain, 0)

    def drain_out(mb, _):
        ship_local(h1, mb, 0).wait()
        ship(h1, mb).wait_send()
        remote(
            h1.at[mb], lo.at[(1 - s) * count + mb], l_s.at[mb], l_r.at[mb], other
        ).wait_recv()
        return 0

    lax.fori_loop(0, count, drain_out, 0)


def bwd_kernel(seqs, n, cot, hid, kept, pad, raw, z, dtp, dt, cum, co, st, car, yn, gsc,
               stats, seg, srow, wc, wo, pr,
               big, table, ig,
               gin, normed, raw_f, shift, gconv, gext, gz, gy_s, ng, ob, gdr, back, nxt, sbuf,
               part, hpart, rbuf, hbuf, acc, ag, gwb, small, srecv, ggn, dsend, drecv,
               c_s, c_r, s_s, s_r, g_s, g_r, h_s, h_r, m_s, m_r, l_c, l_s, l_r, in_s,
               d_s, d_r):
    s, q, h = place()
    count, tokens, model = hid.shape
    inner = wo.shape[1]
    state = LANES
    wide = raw.shape[2]
    heads = inner >> HEAD_SHIFT
    rows = tokens // n
    ext = tokens + HALO
    steps = 2 * count
    full = inner * n
    half = inner // 2
    other = (1 - s, q, h)
    edge_owner = both(h == n - 1, q < seqs - 1)
    peers = [lax.rem(h + j, n) for j in range(1, n)]
    froms = [lax.rem(h + n - j, n) for j in range(1, n)]
    matrix = spread_matrix(inner)
    for p in peers:
        greet((s, q, p))
    greet(other)

    @when(q < seqs - 1)
    def _():
        greet((s, q + 1, h))

    @when(edge_owner)
    def _():
        for head in range(n - 1):
            greet((s, q + 1, head))

    await_greets(n + one_if(q > 0) * (1 + one_if(h < n - 1)))

    def at_rows(owner):
        return pl.ds(pl.multiple_of(owner * rows, rows), rows)

    def slot(w):
        return lax.rem(w, count)

    def chain(w, k):
        cut = pl.ds(k * half, half)
        return remote(
            sbuf.at[slot(w), cut], nxt.at[w, cut], c_s.at[w, k], c_r.at[w, k], (s, q - 1, h)
        )

    def scatter(w, j):
        return remote(
            part.at[slot(w), at_rows(peers[j])], rbuf.at[slot(w), j], s_s.at[w, j],
            s_r.at[w, j], (s, q, peers[j]),
        )

    def gather(w, j, owner):
        where = (slot(w), at_rows(owner))
        return remote(
            ag.at[where], ag.at[where], g_s.at[w, j], g_r.at[w, j], (s, q, peers[j])
        )

    def edge(w, head):
        return remote(
            hpart.at[w], hbuf.at[w, head], h_s.at[w], h_r.at[w, head], (s, q - 1, n - 1)
        )

    def little(layer, j):
        return remote(
            small.at[layer], srecv.at[layer, j], m_s.at[layer, j], m_r.at[layer, j],
            (s, q, peers[j]),
        )

    def ship_local(v):
        mb = lax.rem(v, count)
        return pltpu.make_async_copy(gin.at[v], ig.at[s * count + mb], l_c.at[mb])

    def ship(v):
        mb = lax.rem(v, count)
        return remote(gin.at[v], ig.at[s * count + mb], l_s.at[mb], l_r.at[mb], other)

    def norm_part(v):
        layer = 1 - v // count
        mb = lax.rem(v, count)
        u = layer * count + mb
        for j in range(n - 1):
            gather(v, j, froms[j]).wait_recv()
        gn = ag[mb, :, :model].astype(F32)
        scale = jnp.sum(normed[u, HALO:, model:].astype(F32), axis=1, keepdims=True)
        gain = pr[layer, 0:1]

        def rest(h_in, grad_out):
            x = gn * gain
            dots = jnp.sum(x * h_in, axis=1, keepdims=True)
            gin[v] = grad_out + x * scale - h_in * (scale * scale * scale * dots / model)
            table[layer, 0:1] += jnp.sum(gn * h_in * scale, axis=0, keepdims=True)

        @when(layer == 1)
        def _():
            rest(
                normed[u, HALO:, :model].astype(F32) / (scale * gain),
                gin[mb] * wide_copy(pad[mb], model),
            )

        @when(layer == 0)
        def _():
            rest(gin[v], gin[mb])

        @when(s == layer)
        def _():
            ship_local(v).start()

        @when(s != layer)
        def _():
            ship(v).start()

        grad_w = mm_tn(normed[u, HALO:, :model], ag[mb, :, model:])

        @when(mb == 0)
        def _():
            gwb[...] = grad_w

        @when(mb > 0)
        def _():
            gwb[...] += grad_w

        @when(mb == count - 1)
        def _():
            base = model + inner
            deep = 2 * state
            for k in range(model // deep):
                cut = slice(k * deep, (k + 1) * deep)
                big[layer, base : base + deep, cut] = gwb[cut].astype(TOTAL_T)

    def dots(w, j):
        return remote(
            dsend.at[w], drecv.at[w, j], d_s.at[w, j], d_r.at[w, j], (s, q, peers[j])
        )

    def gate_forward(u, layer):
        gate = z[u]
        sig = sigmoid(gate)
        silu = gate * sig
        ssd = yn[u] + pr[layer, 8:9, :inner] * co[u, :, :inner].astype(F32)
        return gate, sig, silu, ssd, ssd * silu

    def gate_first(w):
        layer = 1 - w // count
        mb = lax.rem(w, count)
        u = layer * count + mb

        @when(layer == 1)
        def _():
            ob[mb] = (gin[mb] * wide_copy(pad[mb], model)).astype(BF)

        @when(layer == 0)
        def _():
            ob[mb] = gin[mb].astype(BF)

        grad_gn = mm_nt(ob[mb], wo[layer])
        ggn[...] = grad_gn
        gated = gate_forward(u, layer)[-1]
        ones = jnp.ones((8, inner), BF)
        dsend[w] = fine(
            lambda a, b: mm_nt(b, a), grad_gn * gated * pr[layer, 9:10, :inner], ones
        )
        for j in range(n - 1):
            dots(w, j).start()

    def gate_part(w):
        layer = 1 - w // count
        mb = lax.rem(w, count)
        u = layer * count + mb
        total = dsend[w]
        for j in range(n - 1):
            dots(w, j).wait_recv()
            total = total + drecv[w, j]
        across = mm_tn(total * 0.125, jnp.ones((8, LANES), F32), HIGH)
        scale = gsc[u]
        scale_x = wide_copy(scale, inner)
        gate, sig, silu, ssd, gated = gate_forward(u, layer)
        grad_gn = ggn[...]
        values = co[u, :, :inner].astype(F32)
        gain = pr[layer, 9:10, :inner]
        scaled = gated * scale_x
        grad_gated = grad_gn * (gain * scale_x) - scaled * wide_copy(
            scale * scale * across / full, inner
        )
        gy = (grad_gated * silu).astype(BF)
        gy_s[...] = gy
        gz[mb] = (grad_gated * ssd * (sig * (1.0 + gate * (1.0 - sig)))).astype(BF)
        ng[mb] = (scaled * gain).astype(BF)
        gy_f = gy.astype(F32)
        table[layer, 8:9, :inner] += jnp.sum(grad_gn * scaled, axis=0, keepdims=True)
        table[layer, 9:10, :inner] += jnp.sum(gy_f * values, axis=0, keepdims=True)
        entry, _ = gains(cum[u], seg, mb)
        read = expand(entry, matrix) * gy_f
        back[...] = fine(mm_tn, read, co[u, :, inner + state :])
        per = inner // heads
        for k in range(2):
            @when(q < seqs - 1)
            def _():
                chain(w, k).wait_recv()

            @when(q == seqs - 1)
            def _():
                nxt[w, k * half : (k + 1) * half] = jnp.zeros((half, LANES), F32)

            @when(q > 0)
            def _():
                @when(w >= count)
                def _():
                    chain(w - count, k).wait_send()

                for i in range(k * heads // 2, (k + 1) * heads // 2):
                    cut = slice(i * per, (i + 1) * per)
                    sbuf[slot(w), cut] = car[u, i : i + 1] * nxt[w, cut] + back[cut]
                chain(w, k).start()

    def local_part(w):
        layer = 1 - w // count
        mb = lax.rem(w, count)
        u = layer * count + mb
        prm = pr[layer]
        cum_u, dt_u = cum[u], dt[u]
        cum_t = cum_u.T
        entry, decay_end = gains(cum_u, seg, mb)
        values = co[u, :, :inner]
        in_b = co[u, :, inner : inner + state]
        in_c = co[u, :, inner + state :]
        gy = gy_s[...]
        gy_f = gy.astype(F32)
        causal = causal_mask(seg, srow, mb, tokens, True)
        inner_bc = jnp.where(causal, mm_nt(in_b, in_c), 0.0)
        grad_inner = jnp.zeros((tokens, tokens), F32)
        lane = iota((tokens, LANES), 1)
        grad_dt = jnp.zeros((tokens, LANES), F32)
        locals_, rows_ = [], []
        for pair in range(heads // 2):
            cols = slice(pair * LANES, (pair + 1) * LANES)
            total = jnp.zeros((tokens, LANES), F32)
            for j in range(2):
                head = 2 * pair + j
                one = slice(head, head + 1)
                dt_col = dt_u[:, one]
                decay = jnp.exp(jnp.minimum(cum_t[one, :] - cum_u[:, one], 0.0))
                mask = jnp.right_shift(lane, HEAD_SHIFT) == j
                gy_one = jnp.where(mask, gy[:, cols], jnp.zeros((), BF))
                grad_mix = mm_nt(values[:, cols], gy_one)
                mixed = inner_bc * decay
                total = total + mm((mixed * dt_col).astype(BF), gy_one)
                grad_inner = grad_inner + grad_mix * (decay * dt_col)
                weighted = grad_mix * mixed
                sums = jnp.sum(weighted, axis=1, keepdims=True)
                grad_dt = jnp.where(lane == head, sums, grad_dt)
                rows_.append(jnp.sum(weighted * dt_col, axis=0, keepdims=True))
            locals_.append(total)
        grad_inner = jnp.where(causal, grad_inner, 0.0)
        toward = decay_end * dt_u
        toward_x = expand(toward, matrix)
        values_f = values.astype(F32)
        pulled = fine(lambda a, b: mm_nt(b, a), nxt[w], in_b)
        gconv[:, :inner] = (
            prm[8:9, :inner] * gy_f + jnp.concatenate(locals_, axis=1) + toward_x * pulled
        )
        read = expand(entry, matrix) * gy_f
        from_row = (iota((heads, LANES), 0) == iota((heads, LANES), 1)).astype(F32)
        grad_cum = (
            mm_tn(jnp.concatenate(rows_, axis=0), from_row, HIGH)
            - dt_u * grad_dt
            + head_sums(read * fine(lambda a, b: mm_nt(b, a), st[u], in_c), matrix)
        )
        pulled_sums = head_sums(values_f * pulled, matrix)
        grad_dt = grad_dt + pulled_sums * decay_end
        high, low = split(nxt[w] * st[u])
        carried = jnp.sum(
            lax.dot_general(high, matrix, (((0,), (1,)), ((), ())), preferred_element_type=F32)
            + lax.dot_general(low, matrix, (((0,), (1,)), ((), ())), preferred_element_type=F32),
            axis=0,
            keepdims=True,
        )
        ahead = (iota((tokens, tokens), 0) > iota((tokens, tokens), 1)).astype(F32)
        grad_rate = (
            mm_tn(lower(tokens), grad_cum, HIGH)
            + mm(ahead, pulled_sums * toward, HIGH)
            + carried * entry[-1:]
        )
        neg = prm[7:8, :LANES]
        grad_pre = (grad_dt + grad_rate * neg) * sigmoid(dtp[u])
        table[layer, 6:7, :LANES] += jnp.sum(grad_pre, axis=0, keepdims=True)
        table[layer, 7:8, :LANES] += jnp.sum(grad_rate * dt_u * neg, axis=0, keepdims=True)
        grad_raw_dt = grad_pre.astype(BF)
        gdr[mb] = grad_raw_dt
        gconv[:, inner : inner + state] = fine(mm, grad_inner, in_c) + finer(
            values_f * toward_x, nxt[w]
        )
        gconv[:, inner + state :] = fine(mm_tn, grad_inner, in_b) + finer(read, st[u])
        raw_f[...] = raw[u].astype(F32)
        same = same_rows(seg, mb, tokens)
        first = HALO - KC + 1
        shift[:HALO] = jnp.zeros((HALO, LANES), F32)
        shift[ext:] = jnp.zeros((HALO, LANES), F32)
        for col in range(0, wide, LANES):
            cols = slice(col, col + LANES)
            pre = convolved(raw_f, same, prm, col, tokens)
            sig = sigmoid(pre)
            grad = gconv[:, cols] * (sig * (1.0 + pre * (1.0 - sig)))
            target = table if col < inner else small
            off = col if col < inner else col - inner
            tc = slice(off, off + LANES)
            target[layer, 5:6, tc] += jnp.sum(grad, axis=0, keepdims=True)
            total = jnp.zeros((ext, LANES), F32)
            for k in range(KC):
                masked = grad * same[k]
                target[layer, 1 + k : 2 + k, tc] += jnp.sum(
                    masked * raw_f[first + k : first + k + tokens, cols], axis=0, keepdims=True
                )
                shift[HALO:ext] = masked * prm[1 + k : 2 + k, cols]
                total = total + shift[KC - 1 - k : KC - 1 - k + ext]
            gext[mb, :, cols] = total.astype(BF)
        grad_raw = gext[mb]
        main = mm_nt(gz[mb], wc[layer, :, :inner]) + mm_nt(
            grad_raw_dt, wc[layer, :, inner + wide :]
        )
        rest = mm_nt(grad_raw, wc[layer, :, inner : inner + wide])
        part[mb, :, :model] = (main + rest[HALO:]).astype(BF)
        hpart[w, :, :model] = rest[:HALO].astype(BF)
        part[mb, :, model:] = grad_raw[HALO:, inner:]
        hpart[w, :, model:] = grad_raw[:HALO, inner:]

    def finish(w):
        acc[...] = part[slot(w), at_rows(h)].astype(F32)
        for j in range(n - 1):
            scatter(w, j).wait_recv()
            acc[...] += rbuf[slot(w), j].astype(F32)

        @when(edge_owner)
        def _():
            for head in range(n):
                edge(w, head).wait_recv()
                acc[rows - HALO :] += hbuf[w, head].astype(F32)

        ag[slot(w), at_rows(h)] = acc[...].astype(BF)
        for j in range(n - 1):
            gather(w, j, h).start()

    def weights_part(layer):
        gate_w = jnp.zeros((inner, model), F32)
        z_w = jnp.zeros((model, inner), F32)
        x_w = jnp.zeros((model, inner), F32)
        dt_w = jnp.zeros((LANES, model), F32)
        for mb in range(count):
            x = normed[layer * count + mb, :, :model]
            gate_w = gate_w + mm_tn(ng[mb], ob[mb])
            z_w = z_w + mm_tn(x[HALO:], gz[mb])
            x_w = x_w + mm_tn(x, gext[mb, :, :inner])
            dt_w = dt_w + mm_tn(gdr[mb], x[HALO:])
        big[layer, :model, :inner] = z_w.astype(TOTAL_T)
        big[layer, :model, inner:] = x_w.astype(TOTAL_T)
        big[layer, model : model + inner] = gate_w.astype(TOTAL_T)
        table[layer, 16:24] = dt_w[:8]
        for j in range(n - 1):
            little(layer, j).start()

    loads = [
        pltpu.make_async_copy(cot, gin.at[pl.ds(0, count)], in_s.at[0]),
        pltpu.make_async_copy(hid, gin.at[pl.ds(count, count)], in_s.at[1]),
        pltpu.make_async_copy(kept.at[pl.ds(0, steps)], normed, in_s.at[2]),
    ]
    for load in loads:
        load.start()
    table[...] = jnp.zeros_like(table)
    small[...] = jnp.zeros_like(small)
    table[:, 24:32, :LANES] = stats[...]
    for load in loads:
        load.wait()

    def step(w, _):
        @when(w >= count)
        def _():
            norm_part(w - count)

        @when(w < steps)
        def _():
            gate_first(w)

        @when(both(w > 0, w <= steps))
        def _():
            finish(w - 1)

        @when(w < steps)
        def _():
            gate_part(w)

        @when(both(w >= count, w < steps))
        def _():
            for j in range(n - 1):
                scatter(w - count, j).wait_send()
                gather(w - count, j, h).wait_send()

        @when(w < steps)
        def _():
            local_part(w)

            @when(q > 0)
            def _():
                edge(w, h).start()

            for j in range(n - 1):
                scatter(w, j).start()

            @when(lax.rem(w, count) == count - 1)
            def _():
                weights_part(1 - w // count)

        return 0

    lax.fori_loop(0, steps + count, step, 0)

    def drain(w, _):
        @when(w >= count)
        def _():
            for j in range(n - 1):
                scatter(w, j).wait_send()
                gather(w, j, h).wait_send()

            @when(q > 0)
            def _():
                for k in range(2):
                    chain(w, k).wait_send()

        for j in range(n - 1):
            dots(w, j).wait_send()

        @when(q > 0)
        def _():
            edge(w, h).wait_send()

        return 0

    lax.fori_loop(0, steps, drain, 0)
    for layer in range(2):
        total = small[layer]
        for j in range(n - 1):
            little(layer, j).wait_recv()
            total = total + srecv[layer, j]
        for j in range(n - 1):
            little(layer, j).wait_send()
        table[layer, 1:6, inner : inner + 2 * state] = total[1:6]

    def drain_out(mb, _):
        ship_local(mb).wait()
        ship(mb).wait_send()
        remote(
            gin.at[mb], ig.at[(1 - s) * count + mb], l_s.at[mb], l_r.at[mb], other
        ).wait_recv()
        return 0

    lax.fori_loop(0, count, drain_out, 0)


def total_kernel(seqs, g, small, out, small_o, pbuf, rbuf, tbuf, ps, rs_, ts,
                 sp, rp, s1, r1, s2, r2, sx, rx):
    s, q, h = place()
    rows = out.shape[0]
    half = rows // 2
    chunks = half // CHUNK
    other = (1 - s, q, h)
    greet(other)

    @pl.when(q > 0)
    def _():
        greet((s, q - 1, h))

    @pl.when(q < seqs - 1)
    def _():
        greet((s, q + 1, h))

    await_greets(1 + one_if(q > 0) + one_if(q < seqs - 1))

    def span(side, c):
        return pl.ds(pl.multiple_of(side * half + c * CHUNK, CHUNK), CHUNK)

    def cross(side, c):
        k = side * chunks + c
        at = span(side, c)
        return remote(g.at[1 - s, at], pbuf.at[at], sp.at[k], rp.at[k], other)

    def along(side, c):
        k = side * chunks + c
        at = span(side, c)
        return remote(
            tbuf.at[at], rbuf.at[at], s1.at[k], r1.at[k], (s, q + 1 - 2 * side, h)
        )

    def back(side, c):
        k = side * chunks + c
        at = span(side, c)
        return remote(out.at[at], out.at[at], s2.at[k], r2.at[k], (s, q - 1 + 2 * side, h))

    small_cross = remote(small.at[1 - s], ps, sx.at[0], rx.at[0], other)
    small_along = remote(ts, rs_, sx.at[1], rx.at[1], (s, q + 1, h))
    small_back = remote(small_o, small_o, sx.at[2], rx.at[2], (s, q - 1, h))
    small_cross.start()

    def start_cross(c, _):
        cross(0, c).start()
        cross(1, c).start()
        return 0

    lax.fori_loop(0, chunks, start_cross, 0)
    small_cross.wait_recv()
    ts[...] = small[s] + ps[...]

    @pl.when(q > 0)
    def _():
        small_along.wait_recv()
        ts[...] += rs_[...]

    @pl.when(q < seqs - 1)
    def _():
        small_along.start()

    @pl.when(q == seqs - 1)
    def _():
        small_o[...] = ts[...]

        @pl.when(q > 0)
        def _():
            small_back.start()

    ends = [(q > 0, q < seqs - 1), (q < seqs - 1, q > 0)]
    ahead = [q, seqs - 1 - q]

    def reduce_step(t, _):
        @pl.when(jnp.logical_and(t == chunks, q < seqs - 1))
        def _():
            small_back.wait_recv()

            @pl.when(q > 0)
            def _():
                small_back.start()

        for side in range(2):
            has_prev, has_next = ends[side]
            c = t - SKEW * ahead[side]

            @pl.when(jnp.logical_and(c >= 0, c < chunks))
            def _():
                at = span(side, c)
                cross(side, c).wait_recv()
                tbuf[at] = (g[s, at].astype(F32) + pbuf[at].astype(F32)).astype(TOTAL_T)

                @pl.when(has_prev)
                def _():
                    along(side, c).wait_recv()
                    tbuf[at] = (
                        g[s, at].astype(F32) + pbuf[at].astype(F32) + rbuf[at].astype(F32)
                    ).astype(TOTAL_T)

                @pl.when(has_next)
                def _():
                    along(side, c).start()

                @pl.when(jnp.logical_not(has_next))
                def _():
                    out[at] = tbuf[at]

                    @pl.when(has_prev)
                    def _():
                        back(side, c).start()

            e = t - SKEW * (2 * (seqs - 1) - ahead[side])

            @pl.when(jnp.logical_and(has_next, jnp.logical_and(e >= 0, e < chunks)))
            def _():
                back(side, e).wait_recv()

                @pl.when(has_prev)
                def _():
                    back(side, e).start()

        return 0

    lax.fori_loop(0, chunks + 2 * SKEW * (seqs - 1), reduce_step, 0)

    def drain(c, _):
        for side in range(2):
            has_prev, has_next = ends[side]
            cross(side, c).wait_send()

            @pl.when(has_next)
            def _():
                along(side, c).wait_send()

            @pl.when(has_prev)
            def _():
                back(side, c).wait_send()

        return 0

    lax.fori_loop(0, chunks, drain, 0)
    small_cross.wait_send()

    @pl.when(q < seqs - 1)
    def _():
        small_along.wait_send()

    @pl.when(q > 0)
    def _():
        small_back.wait_send()


def total_grads(g, small, ident):
    _, rows, width = g.shape
    chunks = rows // CHUNK
    tiny = small.shape[1:]
    return comm(
        functools.partial(total_kernel, lax.axis_size(SEQ)),
        (g, small),
        (((rows, width), TOTAL_T), (tiny, F32)),
        [pltpu.VMEM((rows, width), TOTAL_T)] * 3
        + [pltpu.VMEM(tiny, F32)] * 3
        + [DMA((chunks,))] * 6
        + [DMA((3,))] * 2,
        ident,
        "total_grads",
    )


def pad_lanes(a, width):
    return jnp.pad(a, ((0, 0), (0, width - a.shape[1])))


def local(hidden_in, cotangent, segments, padding, norm_gain, w_zx, w_bc, w_dt, conv_x,
          conv_x_bias, conv_bc, conv_bc_bias, dt_bias, a_log, skip_d, gate_gain, w_out):
    s, q, h = place()
    seqs = lax.axis_size(SEQ)
    n = lax.axis_size(HEAD)
    sections = lax.axis_size(SEC)
    batches, tokens, model = hidden_in.shape
    count = batches // sections
    inner = w_out.shape[1]
    heads = w_dt.shape[2]
    per = inner // heads
    state = w_bc.shape[2] // 2
    wide = inner + 2 * state
    wc = jnp.concatenate(
        [w_zx[0, :, 0], w_zx[0, :, 1], w_bc[0], pad_lanes(w_dt[0], LANES)], axis=1
    )
    prm = jnp.concatenate(
        [
            norm_gain,
            pad_lanes(jnp.concatenate([conv_x[0], conv_bc[0]], axis=1), model),
            pad_lanes(jnp.concatenate([conv_x_bias, conv_bc_bias], axis=1), model),
            pad_lanes(dt_bias, model),
            pad_lanes(-jnp.exp(a_log), model),
            pad_lanes(jnp.repeat(skip_d, per, axis=1), model),
            pad_lanes(gate_gain, model),
            jnp.zeros((6, model), F32),
        ],
        axis=0,
    )

    def mine(a):
        return lax.dynamic_slice_in_dim(a, s * count, count, 0)

    hidden, upstream = mine(hidden_in), mine(cotangent)
    seg = mine(segments).astype(F32)
    pad = jnp.broadcast_to(mine(padding).astype(F32)[:, :, None], (count, tokens, LANES))
    seg_col = jnp.broadcast_to(seg[:, :, None], (count, tokens, LANES))
    srow = jnp.broadcast_to(seg[:, None, :], (count, 8, tokens))
    edge = jnp.concatenate([hidden[:, tokens - HALO :], seg_col[:, tokens - HALO :]], axis=2)
    wc, wo, pr, halo = comm(
        functools.partial(swap_kernel, seqs),
        (wc, w_out[0], prm, edge),
        (((2,) + wc.shape, BF), ((2,) + w_out.shape[1:], BF), ((2,) + prm.shape, F32),
         (edge.shape, F32)),
        [DMA((4,)), DMA((4,))],
        0, "swap",
    )
    inside = q > 0
    halo_h = jnp.where(inside, halo[:, :, :model], 0.0)
    halo_seg = jnp.where(inside, halo[:, :, model:], -1.0)
    seg_col = jnp.concatenate([halo_seg, seg_col], axis=1)
    units = 2 * count
    rows = tokens + HALO
    part_rows = tokens // n
    lane_shape = (units, tokens, LANES)
    inner_shape = (units, tokens, inner)
    state_shape = (units, inner, LANES)
    peer_sems = DMA((units, n - 1))
    out_shape = ((batches, tokens, model), F32)
    kept = comm(
        functools.partial(fwd_kernel, seqs, n),
        (hidden, halo_h, seg_col, srow, pad, wc, wo, pr),
        (
            ((units + count, rows, model + LANES), BF),
            ((units, rows, wide), BF),
            (inner_shape, F32),
            (lane_shape, F32),
            (lane_shape, F32),
            (lane_shape, F32),
            ((units, tokens, wide), BF),
            (state_shape, F32),
            ((units, heads, LANES), F32),
            (inner_shape, F32),
            (lane_shape, F32),
            ((2, 8, LANES), F32),
            out_shape,
        ),
        [
            pltpu.VMEM((count, tokens, model), F32),
            pltpu.VMEM((rows, wide), F32),
            pltpu.VMEM((inner, LANES), F32),
            pltpu.VMEM(state_shape, F32),
            pltpu.VMEM((tokens, inner), F32),
            pltpu.VMEM((count, tokens, model), BF),
            pltpu.VMEM((count, tokens, model), BF),
            pltpu.VMEM((count, n - 1, part_rows, model), BF),
            pltpu.VMEM((count, n - 1, part_rows, model), BF),
            pltpu.VMEM((units, 8, tokens), F32),
            pltpu.VMEM((units, n - 1, 8, tokens), F32),
            pltpu.VMEM((count, tokens, model), F32),
            DMA((units, 2)), DMA((units, 2)),
            peer_sems, peer_sems, peer_sems, peer_sems, peer_sems, peer_sems,
            DMA((count, n)), DMA((count,)),
            DMA((count,)), DMA((count,)), DMA((count,)),
        ],
        1, "fwd", 1,
    )
    normed, raw, z, dtp, dt, cum, co, st, car, yn, gsc, stats, layer_out = kept
    big, table, input_grad = comm(
        functools.partial(bwd_kernel, seqs, n),
        (upstream, hidden, normed, pad, raw, z, dtp, dt, cum, co, st, car, yn, gsc, stats,
         seg_col, srow, wc, wo, pr),
        (
            ((2, model + inner + 2 * state, model), TOTAL_T),
            ((2, 32, model), F32),
            out_shape,
        ),
        [
            pltpu.VMEM((units, tokens, model), F32),
            pltpu.VMEM((units, rows, model + LANES), BF),
            pltpu.VMEM((rows, wide), F32),
            pltpu.VMEM((rows + HALO, LANES), F32),
            pltpu.VMEM((tokens, wide), F32),
            pltpu.VMEM((count, rows, wide), BF),
            pltpu.VMEM((count, tokens, inner), BF),
            pltpu.VMEM((tokens, inner), BF),
            pltpu.VMEM((count, tokens, inner), BF),
            pltpu.VMEM((count, tokens, model), BF),
            pltpu.VMEM((count, tokens, LANES), BF),
            pltpu.VMEM((inner, LANES), F32),
            pltpu.VMEM(state_shape, F32),
            pltpu.VMEM((count, inner, LANES), F32),
            pltpu.VMEM((count, tokens, model + 2 * state), BF),
            pltpu.VMEM((units, HALO, model + 2 * state), BF),
            pltpu.VMEM((count, n - 1, part_rows, model + 2 * state), BF),
            pltpu.VMEM((units, n, HALO, model + 2 * state), BF),
            pltpu.VMEM((part_rows, model + 2 * state), F32),
            pltpu.VMEM((count, tokens, model + 2 * state), BF),
            pltpu.VMEM((model, 2 * state), F32),
            pltpu.VMEM((2, 8, 2 * state), F32),
            pltpu.VMEM((2, n - 1, 8, 2 * state), F32),
            pltpu.VMEM((tokens, inner), F32),
            pltpu.VMEM((units, 8, tokens), F32),
            pltpu.VMEM((units, n - 1, 8, tokens), F32),
            DMA((units, 2)), DMA((units, 2)),
            peer_sems, peer_sems, peer_sems, peer_sems,
            DMA((units,)), DMA((units, n)),
            DMA((2, n - 1)), DMA((2, n - 1)),
            DMA((count,)), DMA((count,)), DMA((count,)), DMA((3,)),
            peer_sems, peer_sems,
        ],
        2, "bwd", 1, 3,
    )
    big, table = total_grads(big, table, 3)
    big = big.astype(F32)
    stats = table[24:27, 0]
    rms = jnp.sqrt(stats[:2] / (stats[2] * model))[None, :]
    grad_zx = big[:model].reshape(model, 2, inner)
    grad_out = big[model : model + inner]
    deep = 2 * state
    grad_bc = big[model + inner :].reshape(deep, model // deep, deep)
    grad_bc = jnp.transpose(grad_bc, (1, 0, 2)).reshape(model, deep)
    return (
        layer_out[None],
        input_grad[None],
        rms,
        table[0:1],
        grad_zx[None],
        grad_bc[None],
        table[16:24].T[None],
        table[1:5, :inner][None],
        table[5:6, :inner],
        table[1:5, inner : inner + 2 * state][None],
        table[5:6, inner : inner + 2 * state],
        table[6:7, :heads],
        table[7:8, :heads],
        jnp.sum(table[9:10, :inner].reshape(1, heads, per), axis=2),
        table[8:9, :inner],
        grad_out[None],
    )


def solution(mesh):
    in_specs = (
        P(None, SEQ, None),
        P(None, SEQ, None),
        P(None, SEQ),
        P(None, SEQ),
        P(SEC, None),
        P(SEC, None, None, HEAD),
        P(SEC, None, None),
        P(SEC, None, HEAD),
        P(SEC, None, HEAD),
        P(SEC, HEAD),
        P(SEC, None, None),
        P(SEC, None),
        P(SEC, HEAD),
        P(SEC, HEAD),
        P(SEC, HEAD),
        P(SEC, HEAD),
        P(SEC, HEAD, None),
    )
    out_specs = (
        P(SEC, None, SEQ, None),
        P(SEC, None, SEQ, None),
        P(SEC, None),
        P(SEC, None),
        P(SEC, None, None, HEAD),
        P(SEC, None, None),
        P(SEC, None, HEAD),
        P(SEC, None, HEAD),
        P(SEC, HEAD),
        P(SEC, None, None),
        P(SEC, None),
        P(SEC, HEAD),
        P(SEC, HEAD),
        P(SEC, HEAD),
        P(SEC, HEAD),
        P(SEC, HEAD, None),
    )
    return jax.shard_map(local, mesh=mesh, in_specs=in_specs, out_specs=out_specs, check_vma=False)
```

```python
import functools

import jax
import jax.numpy as jnp
from jax import lax
from jax.experimental import pallas as pl
from jax.experimental.pallas import tpu as pltpu
from jax.sharding import PartitionSpec as P

SEC, SEQ, HEAD = "section", "seq", "head"
F32, BF = jnp.float32, jnp.bfloat16
MESH = pl.DeviceIdType.MESH
HIGH = lax.Precision.HIGHEST
EPS = 1e-05
KC = 4
HALO = 16
LANES = 128
HEAD_SHIFT = 6
LIMIT = 58 << 20
CHUNK = 32
SKEW = 2
TOTAL_T = jnp.bfloat16


def mm(a, b, precision=None):
    return lax.dot_general(
        a, b, (((1,), (0,)), ((), ())), precision=precision, preferred_element_type=F32
    )


def mm_nt(a, b):
    return lax.dot_general(a, b, (((1,), (1,)), ((), ())), preferred_element_type=F32)


def mm_tn(a, b, precision=None):
    return lax.dot_general(
        a, b, (((0,), (0,)), ((), ())), precision=precision, preferred_element_type=F32
    )


def iota(shape, dim):
    return lax.broadcasted_iota(jnp.int32, shape, dim)


def spread_matrix(width):
    shape = (LANES, width)
    return (iota(shape, 0) == jnp.right_shift(iota(shape, 1), HEAD_SHIFT)).astype(BF)


def split(x):
    high = x.astype(BF)
    return high, (x - high.astype(F32)).astype(BF)


def expand(x, matrix):
    high, low = split(x)
    return mm(high, matrix) + mm(low, matrix)


def head_sums(x, matrix):
    high, low = split(x)
    return mm_nt(high, matrix) + mm_nt(low, matrix)


def fine(product, a, b):
    high, low = split(a)
    return product(high, b) + product(low, b)


def two_lanes(column):
    high = column.astype(BF).astype(F32)
    lane = iota((column.shape[0], LANES), 1)
    return jnp.where(lane == 0, high, jnp.where(lane == 1, column - high, 0.0)).astype(BF)


def sigmoid(v):
    return 1.0 / (1.0 + jnp.exp(-v))


def lower(size):
    return (iota((size, size), 0) >= iota((size, size), 1)).astype(F32)


def same_rows(seg_ref, mb, tokens):
    mine = seg_ref[mb, HALO:]
    first = HALO - KC + 1
    return [
        (seg_ref[mb, first + k : first + k + tokens] == mine).astype(F32) for k in range(KC)
    ]


def convolved(raw_f, same, prm, col, tokens):
    first = HALO - KC + 1
    cols = slice(col, col + LANES)
    pre = jnp.zeros((tokens, LANES), F32) + prm[5:6, cols]
    for k in range(KC):
        pre = pre + prm[1 + k : 2 + k, cols] * raw_f[first + k : first + k + tokens, cols] * same[k]
    return pre


def gains(cum, seg_ref, mb):
    mine = seg_ref[mb, HALO:]
    before = seg_ref[mb, HALO - 1 : HALO]
    last = mine[-1:]
    entry = jnp.exp(cum) * (mine == before).astype(F32)
    decay_end = jnp.exp(cum[-1:] - cum) * (mine == last).astype(F32)
    return entry, decay_end


def place():
    return lax.axis_index(SEC), lax.axis_index(SEQ), lax.axis_index(HEAD)


def remote(src, dst, send, recv, device):
    return pltpu.make_async_remote_copy(
        src_ref=src, dst_ref=dst, send_sem=send, recv_sem=recv, device_id=device,
        device_id_type=MESH,
    )


def greet(device):
    pl.semaphore_signal(
        pltpu.get_barrier_semaphore(), inc=1, device_id=device, device_id_type=MESH
    )


def await_greets(count):
    pl.semaphore_wait(pltpu.get_barrier_semaphore(), count)


def one_if(condition):
    return condition.astype(jnp.int32)


def comm(kernel, ins, outs, scratch, ident, name, in_hbm=0, from_hbm=0):
    sources = [pl.ANY] * from_hbm + [pltpu.VMEM] * (len(ins) - from_hbm)
    spaces = [pltpu.VMEM] * (len(outs) - in_hbm) + [pl.ANY] * in_hbm
    return pl.pallas_call(
        kernel,
        in_specs=[pl.BlockSpec(memory_space=space) for space in sources],
        out_specs=[pl.BlockSpec(memory_space=space) for space in spaces],
        out_shape=[jax.ShapeDtypeStruct(s, d) for s, d in outs],
        scratch_shapes=scratch,
        compiler_params=pltpu.CompilerParams(
            collective_id=ident, has_side_effects=True, vmem_limit_bytes=LIMIT
        ),
        name=name,
    )(*ins)


DMA = pltpu.SemaphoreType.DMA


def finer(a, b):
    a_high, a_low = split(a)
    b_high, b_low = split(b)
    return mm(a_high, b_high) + mm(a_low, b_high) + mm(a_high, b_low)


def wide_copy(x, width):
    return jnp.concatenate([x] * (width // LANES), axis=1)


def causal_mask(seg_ref, srow_ref, mb, tokens, transposed):
    row = iota((tokens, tokens), 0)
    col = iota((tokens, tokens), 1)
    same = wide_copy(seg_ref[mb, HALO:], tokens) == srow_ref[mb, 0:1]
    return same & ((row <= col) if transposed else (row >= col))


def when(condition):
    return pl.when(condition)


def both(a, b):
    return jnp.logical_and(a, b)


def fwd_kernel(seqs, n, source, edge_in, seg_in, srow, pad, wc_in, wo_in, pr_in,
               normed, raw, z, dtp, dt, cum, co, st, car, yn, gsc, stats, wc, wo, pr, seg, lo,
               halo, hid, h1, raw_f, con, sbuf, gated_s, part0, part, rbuf0, rbuf, ssend, srecv, lo1,
               c_s, c_r, q_s, q_r, s_s, s_r, g_s, g_r, h_s, h_r, l_c, l_s, l_r, in_s, w_s, w_r):
    s, q, h = place()
    count, tokens, model = hid.shape
    inner = wo.shape[1]
    wide = raw.shape[2]
    heads = inner >> HEAD_SHIFT
    rows = tokens // n
    units = 2 * count
    full = inner * n
    half = inner // 2
    other = (1 - s, q, h)
    first_q, last_q = q == 0, q == seqs - 1
    edge_owner = both(h == n - 1, q < seqs - 1)
    peers = [lax.rem(h + j, n) for j in range(1, n)]
    froms = [lax.rem(h + n - j, n) for j in range(1, n)]
    matrix = spread_matrix(inner)
    load = pltpu.make_async_copy(source.at[pl.ds(s * count, count)], hid, in_s.at[0])
    load.start()
    for p in peers:
        greet((s, q, p))
    greet(other)

    @when(q > 0)
    def _():
        greet((s, q - 1, n - 1))

    @when(both(q > 0, h < n - 1))
    def _():
        greet((s, q - 1, h))

    await_greets(n + one_if(q < seqs - 1) * (1 + (n - 1) * one_if(h == n - 1)))

    def at_rows(owner):
        return pl.ds(pl.multiple_of(owner * rows, rows), rows)

    def slot_rows(owner):
        return pl.ds(pl.multiple_of(HALO + owner * rows, HALO), rows)

    def chain(u, k):
        cut = pl.ds(k * half, half)
        return remote(
            sbuf.at[u, cut], st.at[u, cut], c_s.at[u, k], c_r.at[u, k], (s, q + 1, h)
        )

    def squares(u, j):
        return remote(
            ssend.at[u], srecv.at[u, j], q_s.at[u, j], q_r.at[u, j], (s, q, peers[j])
        )

    def scatter(u, j, layer):
        src, dst = (part, rbuf) if layer else (part0, rbuf0)
        mb = u - layer * count
        return remote(
            src.at[mb, at_rows(peers[j])], dst.at[mb, j], s_s.at[u, j], s_r.at[u, j],
            (s, q, peers[j]),
        )

    def gather(u, j, owner):
        where = (u + count, slot_rows(owner))
        return remote(
            normed.at[where], normed.at[where], g_s.at[u, j], g_r.at[u, j], (s, q, peers[j])
        )

    def edge(u, head):
        return remote(
            normed.at[u + count, pl.ds(tokens, HALO)], normed.at[u + count, pl.ds(0, HALO)],
            h_s.at[u, head], h_r.at[u], (s, q + 1, head),
        )

    def ship_local(src, mb, layer):
        return pltpu.make_async_copy(src.at[mb], lo.at[s * count + mb], l_c.at[mb])

    def ship(src, mb):
        return remote(src.at[mb], lo.at[s * count + mb], l_s.at[mb], l_r.at[mb], other)

    def send_out(src, mb, layer):
        @when(s == layer)
        def _():
            ship_local(src, mb, layer).start()

        @when(s != layer)
        def _():
            ship(src, mb).start()

    def add_stats(layer, mb, h_new, branch):
        live = pad[mb]
        stats[layer, 0:1] += jnp.sum(
            jnp.sum(h_new * h_new, axis=1, keepdims=True) * live, axis=0, keepdims=True
        )
        stats[layer, 1:2] += jnp.sum(
            jnp.sum(branch * branch, axis=1, keepdims=True) * live, axis=0, keepdims=True
        )
        stats[layer, 2:3] += jnp.sum(live, axis=0, keepdims=True)

    def pass_state(u):
        for k in range(2):
            @when(q > 0)
            def _():
                chain(u, k).wait_recv()

            @when(first_q)
            def _():
                st[u, k * half : (k + 1) * half] = jnp.zeros((half, LANES), F32)

            @when(q < seqs - 1)
            def _():
                per = inner // heads
                for i in range(k * heads // 2, (k + 1) * heads // 2):
                    cut = slice(i * per, (i + 1) * per)
                    sbuf[u, cut] = car[u, i : i + 1] * st[u, cut] + con[cut]
                chain(u, k).start()

    def weight(i, layer):
        src, dst = ((pr_in, pr), (wc_in, wc), (wo_in, wo))[i]
        return remote(src, dst.at[layer], w_s.at[i], w_r.at[i], other)

    halo_copy = remote(edge_in, halo, w_s.at[3], w_r.at[3], (s, q + 1, h))
    weight(0, s).start()

    @when(q < seqs - 1)
    def _():
        halo_copy.start()

    weight(1, s).start()
    weight(2, s).start()
    pr[s] = pr_in[...]
    wc[s] = wc_in[...]
    wo[s] = wo_in[...]

    @when(q > 0)
    def _():
        halo_copy.wait_recv()

    @when(first_q)
    def _():
        halo[:, :, :model] = jnp.zeros((count, HALO, model), F32)
        halo[:, :, model:] = jnp.full((count, HALO, LANES), -1.0, F32)

    seg[:, :HALO] = halo[:, :, model:]
    seg[:, HALO:] = seg_in[...]
    weight(0, 1 - s).wait_recv()

    def needs_weights(u):
        return u == count * (1 - s)

    def in_norm(mb, _):
        hx = jnp.concatenate([halo[mb, :, :model], hid[mb]], axis=0)
        scale = lax.rsqrt(jnp.mean(hx * hx, axis=1, keepdims=True) + EPS)
        normed[mb, :, :model] = (hx * scale * pr[0, 0:1]).astype(BF)
        normed[mb, :, model:] = two_lanes(scale)

        @when(first_q)
        def _():
            normed[mb + count, :HALO] = jnp.zeros((HALO, model + LANES), BF)

        return 0

    load.wait()
    stats[...] = jnp.zeros_like(stats)
    lax.fori_loop(0, count, in_norm, 0)

    def local_part(u):
        layer = u // count
        mb = lax.rem(u, count)
        prm = pr[layer]
        x = normed[u, :, :model]
        new_raw = mm(x, wc[layer, :, inner : inner + wide]).astype(BF)
        raw[u] = new_raw
        raw_f[...] = new_raw.astype(F32)
        x = x[HALO:]
        z[u] = mm(x, wc[layer, :, :inner])
        new_dtp = mm(x, wc[layer, :, inner + wide :]) + prm[6:7, :LANES]
        dtp[u] = new_dtp
        new_dt = jax.nn.softplus(new_dtp)
        dt[u] = new_dt
        new_cum = mm(lower(tokens), new_dt * prm[7:8, :LANES], HIGH)
        cum[u] = new_cum
        cum_t = new_cum.T
        dt_t = new_dt.T
        same = same_rows(seg, mb, tokens)
        pieces = []
        for col in range(0, wide, LANES):
            pre = convolved(raw_f, same, prm, col, tokens)
            piece = (pre * sigmoid(pre)).astype(BF)
            co[u, :, col : col + LANES] = piece
            pieces.append(piece)
        values = jnp.concatenate(pieces[: inner // LANES], axis=1)
        in_b, in_c = pieces[-2], pieces[-1]
        entry, decay_end = gains(new_cum, seg, mb)
        toward = expand(decay_end * new_dt, matrix)
        con[...] = fine(mm_tn, values.astype(F32) * toward, in_b)
        mine = seg[mb, HALO:]
        same_before = (mine[-1:, :] == seg[mb, HALO - 1 : HALO]).astype(F32)
        car[u] = jnp.exp(cum_t[:heads, tokens - 1 :]) * same_before

        @when(first_q)
        def _():
            pass_state(u)

        inner_cb = jnp.where(
            causal_mask(seg, srow, mb, tokens, False), mm_nt(in_c, in_b), 0.0
        )
        lane = iota((tokens, LANES), 1)
        for pair in range(heads // 2):
            cols = slice(pair * LANES, (pair + 1) * LANES)
            acc = jnp.zeros((tokens, LANES), F32)
            for j in range(2):
                one = slice(2 * pair + j, 2 * pair + j + 1)
                decay = jnp.exp(jnp.minimum(new_cum[:, one] - cum_t[one, :], 0.0))
                mask = jnp.right_shift(lane, HEAD_SHIFT) == j
                value = jnp.where(mask, values[:, cols], jnp.zeros((), BF))
                acc = acc + mm((inner_cb * decay * dt_t[one, :]).astype(BF), value)
            yn[u, :, cols] = acc

    def gate_part(u):
        layer = u // count
        mb = lax.rem(u, count)
        entry, _ = gains(cum[u], seg, mb)
        in_c = co[u, :, inner + LANES :]
        readout = fine(lambda a, b: mm_nt(b, a), st[u], in_c)
        y = yn[u] + expand(entry, matrix) * readout
        yn[u] = y
        ssd = y + pr[layer, 8:9, :inner] * co[u, :, :inner].astype(F32)
        gate = z[u]
        gated = ssd * (gate * sigmoid(gate))
        gated_s[...] = gated
        ones = jnp.ones((8, inner), BF)
        ssend[u] = fine(lambda a, b: mm_nt(b, a), gated * gated, ones)

    def out_part(u):
        layer = u // count
        total = ssend[u]
        for j in range(n - 1):
            squares(u, j).wait_recv()
            total = total + srecv[u, j]
        scale_row = lax.rsqrt(total / full + EPS)
        scale = mm_tn(scale_row * 0.125, jnp.ones((8, LANES), F32), HIGH)
        gsc[u] = scale
        x = (gated_s[...] * wide_copy(scale, inner) * pr[layer, 9:10, :inner]).astype(BF)
        product = mm(x, wo[layer])

        @when(u < count)
        def _():
            part0[u] = product.astype(BF)
            for j in range(n - 1):
                scatter(u, j, 0).start()

        @when(u >= count)
        def _():
            part[u - count] = product.astype(BF)
            for j in range(n - 1):
                scatter(u, j, 1).start()

    def finish(u):
        @when(u < count)
        def _():
            total = part0[u, at_rows(h)].astype(F32)
            for j in range(n - 1):
                scatter(u, j, 0).wait_recv()
                total = total + rbuf0[u, j].astype(F32)
            h_new = hid[u, at_rows(h)] + total
            scale = lax.rsqrt(jnp.mean(h_new * h_new, axis=1, keepdims=True) + EPS)
            normed[u + count, slot_rows(h), :model] = (h_new * scale * pr[1, 0:1]).astype(BF)
            normed[u + count, slot_rows(h), model:] = two_lanes(scale)

        @when(u >= count)
        def _():
            total = part[u - count, at_rows(h)].astype(F32)
            for j in range(n - 1):
                scatter(u, j, 1).wait_recv()
                total = total + rbuf[u - count, j].astype(F32)
            normed[u + count, slot_rows(h), :model] = total.astype(BF)
            normed[u + count, slot_rows(h), model:] = jnp.zeros((rows, LANES), BF)

        for j in range(n - 1):
            gather(u, j, h).start()

        @when(both(u < count, edge_owner))
        def _():
            for head in range(n):
                edge(u, head).start()

    def arrived(u):
        for j in range(n - 1):
            gather(u, j, froms[j]).wait_recv()

    def step(u, _):
        @when(both(u >= count, u < units))
        def _():
            mb = u - count
            arrived(mb)

            @when(q > 0)
            def _():
                edge(mb, 0).wait_recv()

            scale = jnp.sum(normed[u, HALO:, model:].astype(F32), axis=1, keepdims=True)
            h_new = normed[u, HALO:, :model].astype(F32) / (scale * pr[1, 0:1])
            h1[mb] = h_new
            send_out(h1, mb, 0)
            add_stats(0, mb, h_new, h_new - hid[mb])

        @when(needs_weights(u))
        def _():
            weight(1, 1 - s).wait_recv()

        @when(u < units)
        def _():
            local_part(u)

            @when(q > 0)
            def _():
                pass_state(u)

            gate_part(u)
            for j in range(n - 1):
                squares(u, j).start()

        @when(u > 0)
        def _():
            finish(u - 1)

        @when(needs_weights(u))
        def _():
            weight(2, 1 - s).wait_recv()

        @when(u < units)
        def _():
            out_part(u)

        return 0

    lax.fori_loop(0, units + 1, step, 0)

    def last_out(mb, _):
        arrived(mb + count)
        branch = normed[mb + units, HALO:, :model].astype(F32)
        h_new = h1[mb] + branch
        lo1[mb] = h_new
        send_out(lo1, mb, 1)
        add_stats(1, mb, h_new, branch)
        return 0

    lax.fori_loop(0, count, last_out, 0)

    def drain(u, _):
        for j in range(n - 1):
            squares(u, j).wait_send()
            gather(u, j, h).wait_send()

        @when(u < count)
        def _():
            for j in range(n - 1):
                scatter(u, j, 0).wait_send()

        @when(u >= count)
        def _():
            for j in range(n - 1):
                scatter(u, j, 1).wait_send()

        @when(q < seqs - 1)
        def _():
            for k in range(2):
                chain(u, k).wait_send()

        @when(both(u < count, edge_owner))
        def _():
            for head in range(n):
                edge(u, head).wait_send()

        return 0

    lax.fori_loop(0, units, drain, 0)
    for i in range(3):
        weight(i, s).wait_send()

    @when(q < seqs - 1)
    def _():
        halo_copy.wait_send()

    def drain_out(mb, _):
        ship_local(h1, mb, 0).wait()
        ship(h1, mb).wait_send()
        remote(
            h1.at[mb], lo.at[(1 - s) * count + mb], l_s.at[mb], l_r.at[mb], other
        ).wait_recv()
        return 0

    lax.fori_loop(0, count, drain_out, 0)


def bwd_kernel(seqs, n, cot, hid, kept, pad, raw, z, dtp, dt, cum, co, st, car, yn, gsc,
               stats, seg, srow, wc, wo, pr,
               big, table, ig,
               gin, normed, raw_f, shift, gconv, gext, gz, gy_s, ng, ob, gdr, back, nxt, sbuf,
               part, hpart, rbuf, hbuf, acc, ag, gwb, small, srecv, ggn, dsend, drecv,
               c_s, c_r, s_s, s_r, g_s, g_r, h_s, h_r, m_s, m_r, l_c, l_s, l_r, in_s,
               d_s, d_r):
    s, q, h = place()
    count, tokens, model = gin.shape[0] // 2, gin.shape[1], gin.shape[2]
    inner = wo.shape[1]
    state = LANES
    wide = raw.shape[2]
    heads = inner >> HEAD_SHIFT
    rows = tokens // n
    ext = tokens + HALO
    steps = 2 * count
    full = inner * n
    half = inner // 2
    other = (1 - s, q, h)
    edge_owner = both(h == n - 1, q < seqs - 1)
    peers = [lax.rem(h + j, n) for j in range(1, n)]
    froms = [lax.rem(h + n - j, n) for j in range(1, n)]
    matrix = spread_matrix(inner)
    for p in peers:
        greet((s, q, p))
    greet(other)

    @when(q < seqs - 1)
    def _():
        greet((s, q + 1, h))

    @when(edge_owner)
    def _():
        for head in range(n - 1):
            greet((s, q + 1, head))

    await_greets(n + one_if(q > 0) * (1 + one_if(h < n - 1)))

    def at_rows(owner):
        return pl.ds(pl.multiple_of(owner * rows, rows), rows)

    def slot(w):
        return lax.rem(w, count)

    def chain(w, k):
        cut = pl.ds(k * half, half)
        return remote(
            sbuf.at[slot(w), cut], nxt.at[w, cut], c_s.at[w, k], c_r.at[w, k], (s, q - 1, h)
        )

    def scatter(w, j):
        return remote(
            part.at[slot(w), at_rows(peers[j])], rbuf.at[slot(w), j], s_s.at[w, j],
            s_r.at[w, j], (s, q, peers[j]),
        )

    def gather(w, j, owner):
        where = (slot(w), at_rows(owner))
        return remote(
            ag.at[where], ag.at[where], g_s.at[w, j], g_r.at[w, j], (s, q, peers[j])
        )

    def edge(w, head):
        return remote(
            hpart.at[w], hbuf.at[w, head], h_s.at[w], h_r.at[w, head], (s, q - 1, n - 1)
        )

    def little(layer, j):
        return remote(
            small.at[layer], srecv.at[layer, j], m_s.at[layer, j], m_r.at[layer, j],
            (s, q, peers[j]),
        )

    def ship_local(v):
        mb = lax.rem(v, count)
        return pltpu.make_async_copy(gin.at[v], ig.at[s * count + mb], l_c.at[mb])

    def ship(v):
        mb = lax.rem(v, count)
        return remote(gin.at[v], ig.at[s * count + mb], l_s.at[mb], l_r.at[mb], other)

    def norm_part(v):
        layer = 1 - v // count
        mb = lax.rem(v, count)
        u = layer * count + mb
        for j in range(n - 1):
            gather(v, j, froms[j]).wait_recv()
        gn = ag[mb, :, :model].astype(F32)
        scale = jnp.sum(normed[u, HALO:, model:].astype(F32), axis=1, keepdims=True)
        gain = pr[layer, 0:1]

        def rest(h_in, grad_out):
            x = gn * gain
            dots = jnp.sum(x * h_in, axis=1, keepdims=True)
            gin[v] = grad_out + x * scale - h_in * (scale * scale * scale * dots / model)
            table[layer, 0:1] += jnp.sum(gn * h_in * scale, axis=0, keepdims=True)

        @when(layer == 1)
        def _():
            rest(
                normed[u, HALO:, :model].astype(F32) / (scale * gain),
                gin[mb] * wide_copy(pad[mb], model),
            )

        @when(layer == 0)
        def _():
            rest(gin[v], gin[mb])

        @when(s == layer)
        def _():
            ship_local(v).start()

        @when(s != layer)
        def _():
            ship(v).start()

        grad_w = mm_tn(normed[u, HALO:, :model], ag[mb, :, model:])

        @when(mb == 0)
        def _():
            gwb[...] = grad_w

        @when(mb > 0)
        def _():
            gwb[...] += grad_w

        @when(mb == count - 1)
        def _():
            base = model + inner
            deep = 2 * state
            for k in range(model // deep):
                cut = slice(k * deep, (k + 1) * deep)
                big[layer, base : base + deep, cut] = gwb[cut].astype(TOTAL_T)

    def dots(w, j):
        return remote(
            dsend.at[w], drecv.at[w, j], d_s.at[w, j], d_r.at[w, j], (s, q, peers[j])
        )

    def gate_forward(u, layer):
        gate = z[u]
        sig = sigmoid(gate)
        silu = gate * sig
        ssd = yn[u] + pr[layer, 8:9, :inner] * co[u, :, :inner].astype(F32)
        return gate, sig, silu, ssd, ssd * silu

    def gate_first(w):
        layer = 1 - w // count
        mb = lax.rem(w, count)
        u = layer * count + mb

        @when(layer == 1)
        def _():
            ob[mb] = (gin[mb] * wide_copy(pad[mb], model)).astype(BF)

        @when(layer == 0)
        def _():
            ob[mb] = gin[mb].astype(BF)

        grad_gn = mm_nt(ob[mb], wo[layer])
        ggn[...] = grad_gn
        gated = gate_forward(u, layer)[-1]
        ones = jnp.ones((8, inner), BF)
        dsend[w] = fine(
            lambda a, b: mm_nt(b, a), grad_gn * gated * pr[layer, 9:10, :inner], ones
        )
        for j in range(n - 1):
            dots(w, j).start()

    def gate_part(w):
        layer = 1 - w // count
        mb = lax.rem(w, count)
        u = layer * count + mb
        total = dsend[w]
        for j in range(n - 1):
            dots(w, j).wait_recv()
            total = total + drecv[w, j]
        across = mm_tn(total * 0.125, jnp.ones((8, LANES), F32), HIGH)
        scale = gsc[u]
        scale_x = wide_copy(scale, inner)
        gate, sig, silu, ssd, gated = gate_forward(u, layer)
        grad_gn = ggn[...]
        values = co[u, :, :inner].astype(F32)
        gain = pr[layer, 9:10, :inner]
        scaled = gated * scale_x
        grad_gated = grad_gn * (gain * scale_x) - scaled * wide_copy(
            scale * scale * across / full, inner
        )
        gy = (grad_gated * silu).astype(BF)
        gy_s[...] = gy
        gz[mb] = (grad_gated * ssd * (sig * (1.0 + gate * (1.0 - sig)))).astype(BF)
        ng[mb] = (scaled * gain).astype(BF)
        gy_f = gy.astype(F32)
        table[layer, 8:9, :inner] += jnp.sum(grad_gn * scaled, axis=0, keepdims=True)
        table[layer, 9:10, :inner] += jnp.sum(gy_f * values, axis=0, keepdims=True)
        entry, _ = gains(cum[u], seg, mb)
        read = expand(entry, matrix) * gy_f
        back[...] = fine(mm_tn, read, co[u, :, inner + state :])
        per = inner // heads
        for k in range(2):
            @when(q < seqs - 1)
            def _():
                chain(w, k).wait_recv()

            @when(q == seqs - 1)
            def _():
                nxt[w, k * half : (k + 1) * half] = jnp.zeros((half, LANES), F32)

            @when(q > 0)
            def _():
                @when(w >= count)
                def _():
                    chain(w - count, k).wait_send()

                for i in range(k * heads // 2, (k + 1) * heads // 2):
                    cut = slice(i * per, (i + 1) * per)
                    sbuf[slot(w), cut] = car[u, i : i + 1] * nxt[w, cut] + back[cut]
                chain(w, k).start()

    def local_part(w):
        layer = 1 - w // count
        mb = lax.rem(w, count)
        u = layer * count + mb
        prm = pr[layer]
        cum_u, dt_u = cum[u], dt[u]
        cum_t = cum_u.T
        entry, decay_end = gains(cum_u, seg, mb)
        values = co[u, :, :inner]
        in_b = co[u, :, inner : inner + state]
        in_c = co[u, :, inner + state :]
        gy = gy_s[...]
        gy_f = gy.astype(F32)
        causal = causal_mask(seg, srow, mb, tokens, True)
        inner_bc = jnp.where(causal, mm_nt(in_b, in_c), 0.0)
        grad_inner = jnp.zeros((tokens, tokens), F32)
        lane = iota((tokens, LANES), 1)
        grad_dt = jnp.zeros((tokens, LANES), F32)
        locals_, rows_ = [], []
        for pair in range(heads // 2):
            cols = slice(pair * LANES, (pair + 1) * LANES)
            total = jnp.zeros((tokens, LANES), F32)
            for j in range(2):
                head = 2 * pair + j
                one = slice(head, head + 1)
                dt_col = dt_u[:, one]
                decay = jnp.exp(jnp.minimum(cum_t[one, :] - cum_u[:, one], 0.0))
                mask = jnp.right_shift(lane, HEAD_SHIFT) == j
                gy_one = jnp.where(mask, gy[:, cols], jnp.zeros((), BF))
                grad_mix = mm_nt(values[:, cols], gy_one)
                mixed = inner_bc * decay
                total = total + mm((mixed * dt_col).astype(BF), gy_one)
                grad_inner = grad_inner + grad_mix * (decay * dt_col)
                weighted = grad_mix * mixed
                sums = jnp.sum(weighted, axis=1, keepdims=True)
                grad_dt = jnp.where(lane == head, sums, grad_dt)
                rows_.append(jnp.sum(weighted * dt_col, axis=0, keepdims=True))
            locals_.append(total)
        grad_inner = jnp.where(causal, grad_inner, 0.0)
        toward = decay_end * dt_u
        toward_x = expand(toward, matrix)
        values_f = values.astype(F32)
        pulled = fine(lambda a, b: mm_nt(b, a), nxt[w], in_b)
        gconv[:, :inner] = (
            prm[8:9, :inner] * gy_f + jnp.concatenate(locals_, axis=1) + toward_x * pulled
        )
        read = expand(entry, matrix) * gy_f
        from_row = (iota((heads, LANES), 0) == iota((heads, LANES), 1)).astype(F32)
        grad_cum = (
            mm_tn(jnp.concatenate(rows_, axis=0), from_row, HIGH)
            - dt_u * grad_dt
            + head_sums(read * fine(lambda a, b: mm_nt(b, a), st[u], in_c), matrix)
        )
        pulled_sums = head_sums(values_f * pulled, matrix)
        grad_dt = grad_dt + pulled_sums * decay_end
        high, low = split(nxt[w] * st[u])
        carried = jnp.sum(
            lax.dot_general(high, matrix, (((0,), (1,)), ((), ())), preferred_element_type=F32)
            + lax.dot_general(low, matrix, (((0,), (1,)), ((), ())), preferred_element_type=F32),
            axis=0,
            keepdims=True,
        )
        ahead = (iota((tokens, tokens), 0) > iota((tokens, tokens), 1)).astype(F32)
        grad_rate = (
            mm_tn(lower(tokens), grad_cum, HIGH)
            + mm(ahead, pulled_sums * toward, HIGH)
            + carried * entry[-1:]
        )
        neg = prm[7:8, :LANES]
        grad_pre = (grad_dt + grad_rate * neg) * sigmoid(dtp[u])
        table[layer, 6:7, :LANES] += jnp.sum(grad_pre, axis=0, keepdims=True)
        table[layer, 7:8, :LANES] += jnp.sum(grad_rate * dt_u * neg, axis=0, keepdims=True)
        grad_raw_dt = grad_pre.astype(BF)
        gdr[mb] = grad_raw_dt
        gconv[:, inner : inner + state] = fine(mm, grad_inner, in_c) + finer(
            values_f * toward_x, nxt[w]
        )
        gconv[:, inner + state :] = fine(mm_tn, grad_inner, in_b) + finer(read, st[u])
        raw_f[...] = raw[u].astype(F32)
        same = same_rows(seg, mb, tokens)
        first = HALO - KC + 1
        shift[:HALO] = jnp.zeros((HALO, LANES), F32)
        shift[ext:] = jnp.zeros((HALO, LANES), F32)
        for col in range(0, wide, LANES):
            cols = slice(col, col + LANES)
            pre = convolved(raw_f, same, prm, col, tokens)
            sig = sigmoid(pre)
            grad = gconv[:, cols] * (sig * (1.0 + pre * (1.0 - sig)))
            target = table if col < inner else small
            off = col if col < inner else col - inner
            tc = slice(off, off + LANES)
            target[layer, 5:6, tc] += jnp.sum(grad, axis=0, keepdims=True)
            total = jnp.zeros((ext, LANES), F32)
            for k in range(KC):
                masked = grad * same[k]
                target[layer, 1 + k : 2 + k, tc] += jnp.sum(
                    masked * raw_f[first + k : first + k + tokens, cols], axis=0, keepdims=True
                )
                shift[HALO:ext] = masked * prm[1 + k : 2 + k, cols]
                total = total + shift[KC - 1 - k : KC - 1 - k + ext]
            gext[mb, :, cols] = total.astype(BF)
        grad_raw = gext[mb]
        main = mm_nt(gz[mb], wc[layer, :, :inner]) + mm_nt(
            grad_raw_dt, wc[layer, :, inner + wide :]
        )
        rest = mm_nt(grad_raw, wc[layer, :, inner : inner + wide])
        part[mb, :, :model] = (main + rest[HALO:]).astype(BF)
        hpart[w, :, :model] = rest[:HALO].astype(BF)
        part[mb, :, model:] = grad_raw[HALO:, inner:]
        hpart[w, :, model:] = grad_raw[:HALO, inner:]

    def finish(w):
        acc[...] = part[slot(w), at_rows(h)].astype(F32)
        for j in range(n - 1):
            scatter(w, j).wait_recv()
            acc[...] += rbuf[slot(w), j].astype(F32)

        @when(edge_owner)
        def _():
            for head in range(n):
                edge(w, head).wait_recv()
                acc[rows - HALO :] += hbuf[w, head].astype(F32)

        ag[slot(w), at_rows(h)] = acc[...].astype(BF)
        for j in range(n - 1):
            gather(w, j, h).start()

    def weights_part(layer):
        gate_w = jnp.zeros((inner, model), F32)
        z_w = jnp.zeros((model, inner), F32)
        x_w = jnp.zeros((model, inner), F32)
        dt_w = jnp.zeros((LANES, model), F32)
        for mb in range(count):
            x = normed[layer * count + mb, :, :model]
            gate_w = gate_w + mm_tn(ng[mb], ob[mb])
            z_w = z_w + mm_tn(x[HALO:], gz[mb])
            x_w = x_w + mm_tn(x, gext[mb, :, :inner])
            dt_w = dt_w + mm_tn(gdr[mb], x[HALO:])
        big[layer, :model, :inner] = z_w.astype(TOTAL_T)
        big[layer, :model, inner:] = x_w.astype(TOTAL_T)
        big[layer, model : model + inner] = gate_w.astype(TOTAL_T)
        table[layer, 16:24] = dt_w[:8]
        for j in range(n - 1):
            little(layer, j).start()

    loads = [
        pltpu.make_async_copy(cot.at[pl.ds(s * count, count)], gin.at[pl.ds(0, count)], in_s.at[0]),
        pltpu.make_async_copy(
            hid.at[pl.ds(s * count, count)], gin.at[pl.ds(count, count)], in_s.at[1]
        ),
        pltpu.make_async_copy(kept.at[pl.ds(0, steps)], normed, in_s.at[2]),
    ]
    for load in loads:
        load.start()
    table[...] = jnp.zeros_like(table)
    small[...] = jnp.zeros_like(small)
    table[:, 24:32, :LANES] = stats[...]
    for load in loads:
        load.wait()

    def step(w, _):
        @when(w >= count)
        def _():
            norm_part(w - count)

        @when(w < steps)
        def _():
            gate_first(w)

        @when(both(w > 0, w <= steps))
        def _():
            finish(w - 1)

        @when(w < steps)
        def _():
            gate_part(w)

        @when(both(w >= count, w < steps))
        def _():
            for j in range(n - 1):
                scatter(w - count, j).wait_send()
                gather(w - count, j, h).wait_send()

        @when(w < steps)
        def _():
            local_part(w)

            @when(q > 0)
            def _():
                edge(w, h).start()

            for j in range(n - 1):
                scatter(w, j).start()

            @when(lax.rem(w, count) == count - 1)
            def _():
                weights_part(1 - w // count)

        return 0

    lax.fori_loop(0, steps + count, step, 0)

    def drain(w, _):
        @when(w >= count)
        def _():
            for j in range(n - 1):
                scatter(w, j).wait_send()
                gather(w, j, h).wait_send()

            @when(q > 0)
            def _():
                for k in range(2):
                    chain(w, k).wait_send()

        for j in range(n - 1):
            dots(w, j).wait_send()

        @when(q > 0)
        def _():
            edge(w, h).wait_send()

        return 0

    lax.fori_loop(0, steps, drain, 0)
    for layer in range(2):
        total = small[layer]
        for j in range(n - 1):
            little(layer, j).wait_recv()
            total = total + srecv[layer, j]
        for j in range(n - 1):
            little(layer, j).wait_send()
        table[layer, 1:6, inner : inner + 2 * state] = total[1:6]

    def drain_out(mb, _):
        ship_local(mb).wait()
        ship(mb).wait_send()
        remote(
            gin.at[mb], ig.at[(1 - s) * count + mb], l_s.at[mb], l_r.at[mb], other
        ).wait_recv()
        return 0

    lax.fori_loop(0, count, drain_out, 0)


def total_kernel(seqs, g, small, out, small_o, pbuf, rbuf, tbuf, ps, rs_, ts,
                 sp, rp, s1, r1, s2, r2, sx, rx):
    s, q, h = place()
    rows = out.shape[0]
    half = rows // 2
    chunks = half // CHUNK
    other = (1 - s, q, h)
    greet(other)

    @pl.when(q > 0)
    def _():
        greet((s, q - 1, h))

    @pl.when(q < seqs - 1)
    def _():
        greet((s, q + 1, h))

    await_greets(1 + one_if(q > 0) + one_if(q < seqs - 1))

    def span(side, c):
        return pl.ds(pl.multiple_of(side * half + c * CHUNK, CHUNK), CHUNK)

    def cross(side, c):
        k = side * chunks + c
        at = span(side, c)
        return remote(g.at[1 - s, at], pbuf.at[at], sp.at[k], rp.at[k], other)

    def along(side, c):
        k = side * chunks + c
        at = span(side, c)
        return remote(
            tbuf.at[at], rbuf.at[at], s1.at[k], r1.at[k], (s, q + 1 - 2 * side, h)
        )

    def back(side, c):
        k = side * chunks + c
        at = span(side, c)
        return remote(out.at[at], out.at[at], s2.at[k], r2.at[k], (s, q - 1 + 2 * side, h))

    small_cross = remote(small.at[1 - s], ps, sx.at[0], rx.at[0], other)
    small_along = remote(ts, rs_, sx.at[1], rx.at[1], (s, q + 1, h))
    small_back = remote(small_o, small_o, sx.at[2], rx.at[2], (s, q - 1, h))
    small_cross.start()

    def start_cross(c, _):
        cross(0, c).start()
        cross(1, c).start()
        return 0

    lax.fori_loop(0, chunks, start_cross, 0)
    small_cross.wait_recv()
    ts[...] = small[s] + ps[...]

    @pl.when(q > 0)
    def _():
        small_along.wait_recv()
        ts[...] += rs_[...]

    @pl.when(q < seqs - 1)
    def _():
        small_along.start()

    @pl.when(q == seqs - 1)
    def _():
        small_o[...] = ts[...]

        @pl.when(q > 0)
        def _():
            small_back.start()

    ends = [(q > 0, q < seqs - 1), (q < seqs - 1, q > 0)]
    ahead = [q, seqs - 1 - q]

    def reduce_step(t, _):
        @pl.when(jnp.logical_and(t == chunks, q < seqs - 1))
        def _():
            small_back.wait_recv()

            @pl.when(q > 0)
            def _():
                small_back.start()

        for side in range(2):
            has_prev, has_next = ends[side]
            c = t - SKEW * ahead[side]

            @pl.when(jnp.logical_and(c >= 0, c < chunks))
            def _():
                at = span(side, c)
                cross(side, c).wait_recv()
                tbuf[at] = (g[s, at].astype(F32) + pbuf[at].astype(F32)).astype(TOTAL_T)

                @pl.when(has_prev)
                def _():
                    along(side, c).wait_recv()
                    tbuf[at] = (
                        g[s, at].astype(F32) + pbuf[at].astype(F32) + rbuf[at].astype(F32)
                    ).astype(TOTAL_T)

                @pl.when(has_next)
                def _():
                    along(side, c).start()

                @pl.when(jnp.logical_not(has_next))
                def _():
                    out[at] = tbuf[at]

                    @pl.when(has_prev)
                    def _():
                        back(side, c).start()

            e = t - SKEW * (2 * (seqs - 1) - ahead[side])

            @pl.when(jnp.logical_and(has_next, jnp.logical_and(e >= 0, e < chunks)))
            def _():
                back(side, e).wait_recv()

                @pl.when(has_prev)
                def _():
                    back(side, e).start()

        return 0

    lax.fori_loop(0, chunks + 2 * SKEW * (seqs - 1), reduce_step, 0)

    def drain(c, _):
        for side in range(2):
            has_prev, has_next = ends[side]
            cross(side, c).wait_send()

            @pl.when(has_next)
            def _():
                along(side, c).wait_send()

            @pl.when(has_prev)
            def _():
                back(side, c).wait_send()

        return 0

    lax.fori_loop(0, chunks, drain, 0)
    small_cross.wait_send()

    @pl.when(q < seqs - 1)
    def _():
        small_along.wait_send()

    @pl.when(q > 0)
    def _():
        small_back.wait_send()


def total_grads(g, small, ident):
    _, rows, width = g.shape
    chunks = rows // CHUNK
    tiny = small.shape[1:]
    return comm(
        functools.partial(total_kernel, lax.axis_size(SEQ)),
        (g, small),
        (((rows, width), TOTAL_T), (tiny, F32)),
        [pltpu.VMEM((rows, width), TOTAL_T)] * 3
        + [pltpu.VMEM(tiny, F32)] * 3
        + [DMA((chunks,))] * 6
        + [DMA((3,))] * 2,
        ident,
        "total_grads",
    )


def pad_lanes(a, width):
    return jnp.pad(a, ((0, 0), (0, width - a.shape[1])))


def final_kernel(zx, wo, bc, table, g_zx, g_wo, g_bc, rms, g_norm, g_dt, g_cx, g_cxb, g_cb, g_cbb,
                 g_dtb, g_al, g_sk, g_gate):
    inner = g_zx.shape[3]
    model = table.shape[1]
    heads = g_dtb.shape[1]
    step = pl.program_id(0)
    g_zx[0, :, 0, :] = zx[:, :inner].astype(F32)
    g_zx[0, :, 1, :] = zx[:, inner:].astype(F32)
    g_wo[0] = wo[...].astype(F32)

    @when(step == 0)
    def _():
        deep = g_bc.shape[2]
        for k in range(model // deep):
            cut = slice(k * deep, (k + 1) * deep)
            g_bc[0, cut] = bc[:, cut].astype(F32)
        live = table[26:27, :LANES] * model
        first = jnp.sqrt(table[24:25, :LANES] / live)
        second = jnp.sqrt(table[25:26, :LANES] / live)
        rms[...] = jnp.where(iota((1, LANES), 1) == 0, first, second)[:, :2]
        g_norm[...] = table[0:1]
        g_dt[0] = table[16 : 16 + heads]
        g_cx[0] = table[1:5, :inner]
        g_cxb[...] = table[5:6, :inner]
        g_cb[0] = table[1:5, inner : inner + deep]
        g_cbb[...] = table[5:6, inner : inner + deep]
        g_dtb[...] = table[6:7, :heads]
        g_al[...] = table[7:8, :heads]
        sums = mm(table[8:16, :inner], spread_matrix(inner).astype(F32).T, HIGH)
        g_sk[...] = sums[1:2, :heads]
        g_gate[...] = table[8:9, :inner]


def finalize(big, table, inner, heads, state):
    model = big.shape[1]
    steps = 4
    deep = 2 * state

    def whole(shape):
        return pl.BlockSpec(shape, lambda i: (0,) * len(shape))

    shapes = [
        (1, model, 2, inner), (1, inner, model), (1, model, deep), (1, 2), (1, model),
        (1, heads, model), (1, 4, inner), (1, inner), (1, 4, deep), (1, deep),
        (1, heads), (1, heads), (1, heads), (1, inner),
    ]
    specs = [
        pl.BlockSpec((1, model // steps, 2, inner), lambda i: (0, i, 0, 0)),
        pl.BlockSpec((1, inner // steps, model), lambda i: (0, i, 0)),
    ] + [whole(x) for x in shapes[2:]]
    base = model // (inner // steps)
    return pl.pallas_call(
        final_kernel,
        grid=(steps,),
        in_specs=[
            pl.BlockSpec((model // steps, model), lambda i: (i, 0)),
            pl.BlockSpec((inner // steps, model), lambda i: (base + i, 0)),
            pl.BlockSpec((deep, model), lambda i: ((model + inner) // deep, 0)),
            whole(table.shape),
        ],
        out_specs=specs,
        out_shape=[jax.ShapeDtypeStruct(x, F32) for x in shapes],
        compiler_params=pltpu.CompilerParams(vmem_limit_bytes=LIMIT),
        name="final",
    )(big, big, big, table)


def local(hidden_in, cotangent, segments, padding, norm_gain, w_zx, w_bc, w_dt, conv_x,
          conv_x_bias, conv_bc, conv_bc_bias, dt_bias, a_log, skip_d, gate_gain, w_out):
    s, q, h = place()
    seqs = lax.axis_size(SEQ)
    n = lax.axis_size(HEAD)
    sections = lax.axis_size(SEC)
    batches, tokens, model = hidden_in.shape
    count = batches // sections
    inner = w_out.shape[1]
    heads = w_dt.shape[2]
    per = inner // heads
    state = w_bc.shape[2] // 2
    wide = inner + 2 * state
    wc = jnp.concatenate(
        [w_zx[0, :, 0], w_zx[0, :, 1], w_bc[0], pad_lanes(w_dt[0], LANES)], axis=1
    )
    prm = jnp.concatenate(
        [
            norm_gain,
            pad_lanes(jnp.concatenate([conv_x[0], conv_bc[0]], axis=1), model),
            pad_lanes(jnp.concatenate([conv_x_bias, conv_bc_bias], axis=1), model),
            pad_lanes(dt_bias, model),
            pad_lanes(-jnp.exp(a_log), model),
            pad_lanes(jnp.repeat(skip_d, per, axis=1), model),
            pad_lanes(gate_gain, model),
            jnp.zeros((6, model), F32),
        ],
        axis=0,
    )

    def mine(a):
        return lax.dynamic_slice_in_dim(a, s * count, count, 0)

    seg = mine(segments).astype(F32)
    pad = jnp.broadcast_to(mine(padding).astype(F32)[:, :, None], (count, tokens, LANES))
    seg_col = jnp.broadcast_to(seg[:, :, None], (count, tokens, LANES))
    srow = jnp.broadcast_to(seg[:, None, :], (count, 8, tokens))
    edge = jnp.concatenate(
        [mine(hidden_in[:, tokens - HALO :]), seg_col[:, tokens - HALO :]], axis=2
    )
    units = 2 * count
    rows = tokens + HALO
    part_rows = tokens // n
    lane_shape = (units, tokens, LANES)
    inner_shape = (units, tokens, inner)
    state_shape = (units, inner, LANES)
    peer_sems = DMA((units, n - 1))
    out_shape = ((batches, tokens, model), F32)
    kept = comm(
        functools.partial(fwd_kernel, seqs, n),
        (hidden_in, edge, seg_col, srow, pad, wc, w_out[0], prm),
        (
            ((units + count, rows, model + LANES), BF),
            ((units, rows, wide), BF),
            (inner_shape, F32),
            (lane_shape, F32),
            (lane_shape, F32),
            (lane_shape, F32),
            ((units, tokens, wide), BF),
            (state_shape, F32),
            ((units, heads, LANES), F32),
            (inner_shape, F32),
            (lane_shape, F32),
            ((2, 8, LANES), F32),
            ((2,) + wc.shape, BF),
            ((2,) + w_out.shape[1:], BF),
            ((2,) + prm.shape, F32),
            ((count, rows, LANES), F32),
            out_shape,
        ),
        [
            pltpu.VMEM(edge.shape, F32),
            pltpu.VMEM((count, tokens, model), F32),
            pltpu.VMEM((count, tokens, model), F32),
            pltpu.VMEM((rows, wide), F32),
            pltpu.VMEM((inner, LANES), F32),
            pltpu.VMEM(state_shape, F32),
            pltpu.VMEM((tokens, inner), F32),
            pltpu.VMEM((count, tokens, model), BF),
            pltpu.VMEM((count, tokens, model), BF),
            pltpu.VMEM((count, n - 1, part_rows, model), BF),
            pltpu.VMEM((count, n - 1, part_rows, model), BF),
            pltpu.VMEM((units, 8, tokens), F32),
            pltpu.VMEM((units, n - 1, 8, tokens), F32),
            pltpu.VMEM((count, tokens, model), F32),
            DMA((units, 2)), DMA((units, 2)),
            peer_sems, peer_sems, peer_sems, peer_sems, peer_sems, peer_sems,
            DMA((count, n)), DMA((count,)),
            DMA((count,)), DMA((count,)), DMA((count,)), DMA((1,)),
            DMA((4,)), DMA((4,)),
        ],
        1, "fwd", 1, 1,
    )
    normed, raw, z, dtp, dt, cum, co, st, car, yn, gsc, stats = kept[:12]
    wc, wo, pr, seg_col, layer_out = kept[12:]
    big, table, input_grad = comm(
        functools.partial(bwd_kernel, seqs, n),
        (cotangent, hidden_in, normed, pad, raw, z, dtp, dt, cum, co, st, car, yn, gsc, stats,
         seg_col, srow, wc, wo, pr),
        (
            ((2, model + inner + 2 * state, model), TOTAL_T),
            ((2, 32, model), F32),
            out_shape,
        ),
        [
            pltpu.VMEM((units, tokens, model), F32),
            pltpu.VMEM((units, rows, model + LANES), BF),
            pltpu.VMEM((rows, wide), F32),
            pltpu.VMEM((rows + HALO, LANES), F32),
            pltpu.VMEM((tokens, wide), F32),
            pltpu.VMEM((count, rows, wide), BF),
            pltpu.VMEM((count, tokens, inner), BF),
            pltpu.VMEM((tokens, inner), BF),
            pltpu.VMEM((count, tokens, inner), BF),
            pltpu.VMEM((count, tokens, model), BF),
            pltpu.VMEM((count, tokens, LANES), BF),
            pltpu.VMEM((inner, LANES), F32),
            pltpu.VMEM(state_shape, F32),
            pltpu.VMEM((count, inner, LANES), F32),
            pltpu.VMEM((count, tokens, model + 2 * state), BF),
            pltpu.VMEM((units, HALO, model + 2 * state), BF),
            pltpu.VMEM((count, n - 1, part_rows, model + 2 * state), BF),
            pltpu.VMEM((units, n, HALO, model + 2 * state), BF),
            pltpu.VMEM((part_rows, model + 2 * state), F32),
            pltpu.VMEM((count, tokens, model + 2 * state), BF),
            pltpu.VMEM((model, 2 * state), F32),
            pltpu.VMEM((2, 8, 2 * state), F32),
            pltpu.VMEM((2, n - 1, 8, 2 * state), F32),
            pltpu.VMEM((tokens, inner), F32),
            pltpu.VMEM((units, 8, tokens), F32),
            pltpu.VMEM((units, n - 1, 8, tokens), F32),
            DMA((units, 2)), DMA((units, 2)),
            peer_sems, peer_sems, peer_sems, peer_sems,
            DMA((units,)), DMA((units, n)),
            DMA((2, n - 1)), DMA((2, n - 1)),
            DMA((count,)), DMA((count,)), DMA((count,)), DMA((3,)),
            peer_sems, peer_sems,
        ],
        2, "bwd", 1, 3,
    )
    big, table = total_grads(big, table, 3)
    (g_zx, g_wo, g_bc, rms, g_norm, g_dt, g_cx, g_cxb, g_cb, g_cbb, g_dtb, g_al, g_sk,
     g_gate) = finalize(big, table, inner, heads, state)
    return (layer_out[None], input_grad[None], rms, g_norm, g_zx, g_bc,
            jnp.transpose(g_dt, (0, 2, 1)), g_cx, g_cxb,
            g_cb, g_cbb, g_dtb, g_al, g_sk, g_gate, g_wo)


def solution(mesh):
    in_specs = (
        P(None, SEQ, None),
        P(None, SEQ, None),
        P(None, SEQ),
        P(None, SEQ),
        P(SEC, None),
        P(SEC, None, None, HEAD),
        P(SEC, None, None),
        P(SEC, None, HEAD),
        P(SEC, None, HEAD),
        P(SEC, HEAD),
        P(SEC, None, None),
        P(SEC, None),
        P(SEC, HEAD),
        P(SEC, HEAD),
        P(SEC, HEAD),
        P(SEC, HEAD),
        P(SEC, HEAD, None),
    )
    out_specs = (
        P(SEC, None, SEQ, None),
        P(SEC, None, SEQ, None),
        P(SEC, None),
        P(SEC, None),
        P(SEC, None, None, HEAD),
        P(SEC, None, None),
        P(SEC, None, HEAD),
        P(SEC, None, HEAD),
        P(SEC, HEAD),
        P(SEC, None, None),
        P(SEC, None),
        P(SEC, HEAD),
        P(SEC, HEAD),
        P(SEC, HEAD),
        P(SEC, HEAD),
        P(SEC, HEAD, None),
    )
    return jax.shard_map(local, mesh=mesh, in_specs=in_specs, out_specs=out_specs, check_vma=False)
```

```python
import functools

import jax
import jax.numpy as jnp
from jax import lax
from jax.experimental import pallas as pl
from jax.experimental.pallas import tpu as pltpu
from jax.sharding import PartitionSpec as P

SEC, SEQ, HEAD = "section", "seq", "head"
F32, BF = jnp.float32, jnp.bfloat16
MESH = pl.DeviceIdType.MESH
HIGH = lax.Precision.HIGHEST
EPS = 1e-05
KC = 4
HALO = 16
LANES = 128
HEAD_SHIFT = 6
LIMIT = 58 << 20
CHUNK = 32
SKEW = 2
LEAD = 2
TICKS = 20
TAIL_TICKS = 8
PIECES = 4
TOTAL_T = jnp.bfloat16


def mm(a, b, precision=None):
    return lax.dot_general(
        a, b, (((1,), (0,)), ((), ())), precision=precision, preferred_element_type=F32
    )


def mm_nt(a, b):
    return lax.dot_general(a, b, (((1,), (1,)), ((), ())), preferred_element_type=F32)


def mm_tn(a, b, precision=None):
    return lax.dot_general(
        a, b, (((0,), (0,)), ((), ())), precision=precision, preferred_element_type=F32
    )


def iota(shape, dim):
    return lax.broadcasted_iota(jnp.int32, shape, dim)


def spread_matrix(width):
    shape = (LANES, width)
    return (iota(shape, 0) == jnp.right_shift(iota(shape, 1), HEAD_SHIFT)).astype(BF)


def split(x):
    high = x.astype(BF)
    return high, (x - high.astype(F32)).astype(BF)


def expand(x, matrix):
    high, low = split(x)
    return mm(high, matrix) + mm(low, matrix)


def head_sums(x, matrix):
    high, low = split(x)
    return mm_nt(high, matrix) + mm_nt(low, matrix)


def fine(product, a, b):
    high, low = split(a)
    return product(high, b) + product(low, b)


def two_lanes(column):
    high = column.astype(BF).astype(F32)
    lane = iota((column.shape[0], LANES), 1)
    return jnp.where(lane == 0, high, jnp.where(lane == 1, column - high, 0.0)).astype(BF)


def sigmoid(v):
    return 1.0 / (1.0 + jnp.exp(-v))


def lower(size):
    return (iota((size, size), 0) >= iota((size, size), 1)).astype(F32)


def same_rows(seg_ref, mb, tokens):
    mine = seg_ref[mb, HALO:]
    first = HALO - KC + 1
    return [
        (seg_ref[mb, first + k : first + k + tokens] == mine).astype(F32) for k in range(KC)
    ]


def convolved(raw_f, same, prm, col, tokens):
    first = HALO - KC + 1
    cols = slice(col, col + LANES)
    pre = jnp.zeros((tokens, LANES), F32) + prm[5:6, cols]
    for k in range(KC):
        pre = pre + prm[1 + k : 2 + k, cols] * raw_f[first + k : first + k + tokens, cols] * same[k]
    return pre


def gains(cum, seg_ref, mb):
    mine = seg_ref[mb, HALO:]
    before = seg_ref[mb, HALO - 1 : HALO]
    last = mine[-1:]
    entry = jnp.exp(cum) * (mine == before).astype(F32)
    decay_end = jnp.exp(cum[-1:] - cum) * (mine == last).astype(F32)
    return entry, decay_end


def place():
    return lax.axis_index(SEC), lax.axis_index(SEQ), lax.axis_index(HEAD)


def remote(src, dst, send, recv, device):
    return pltpu.make_async_remote_copy(
        src_ref=src, dst_ref=dst, send_sem=send, recv_sem=recv, device_id=device,
        device_id_type=MESH,
    )


def greet(device):
    pl.semaphore_signal(
        pltpu.get_barrier_semaphore(), inc=1, device_id=device, device_id_type=MESH
    )


def await_greets(count):
    pl.semaphore_wait(pltpu.get_barrier_semaphore(), count)


def one_if(condition):
    return condition.astype(jnp.int32)


def comm(kernel, ins, outs, scratch, ident, name, in_hbm=0, from_hbm=0):
    sources = [pl.ANY] * from_hbm + [pltpu.VMEM] * (len(ins) - from_hbm)
    spaces = [pltpu.VMEM] * (len(outs) - in_hbm) + [pl.ANY] * in_hbm
    return pl.pallas_call(
        kernel,
        in_specs=[pl.BlockSpec(memory_space=space) for space in sources],
        out_specs=[pl.BlockSpec(memory_space=space) for space in spaces],
        out_shape=[jax.ShapeDtypeStruct(s, d) for s, d in outs],
        scratch_shapes=scratch,
        compiler_params=pltpu.CompilerParams(
            collective_id=ident, has_side_effects=True, vmem_limit_bytes=LIMIT
        ),
        name=name,
    )(*ins)


DMA = pltpu.SemaphoreType.DMA


def wide_copy(x, width):
    return jnp.concatenate([x] * (width // LANES), axis=1)


def causal_mask(seg_ref, srow_ref, mb, tokens, transposed):
    row = iota((tokens, tokens), 0)
    col = iota((tokens, tokens), 1)
    same = wide_copy(seg_ref[mb, HALO:], tokens) == srow_ref[mb, 0:1]
    return same & ((row <= col) if transposed else (row >= col))


def when(condition):
    return pl.when(condition)


def both(a, b):
    return jnp.logical_and(a, b)


def fwd_kernel(seqs, n, source, edge_in, seg_in, srow, pad, wc_in, wo_in, pr_in,
               normed, raw, z, dtp, dt, cum, co, st, car, yn, gsc, stats, wc, wo, pr, seg, lo,
               halo, hid, h1, raw_f, con, sbuf, gated_s, part0, part, rbuf0, rbuf, ssend, srecv, lo1,
               c_s, c_r, q_s, q_r, s_s, s_r, g_s, g_r, h_s, h_r, l_c, l_s, l_r, in_s, w_s, w_r):
    s, q, h = place()
    count, tokens, model = hid.shape
    inner = wo.shape[1]
    wide = raw.shape[2]
    heads = inner >> HEAD_SHIFT
    rows = tokens // n
    units = 2 * count
    full = inner * n
    piece = inner // PIECES
    other = (1 - s, q, h)
    first_q, last_q = q == 0, q == seqs - 1
    edge_owner = both(h == n - 1, q < seqs - 1)
    peers = [lax.rem(h + j, n) for j in range(1, n)]
    froms = [lax.rem(h + n - j, n) for j in range(1, n)]
    matrix = spread_matrix(inner)
    load = pltpu.make_async_copy(source.at[pl.ds(s * count, count)], hid, in_s.at[0])
    load.start()
    for p in peers:
        greet((s, q, p))
    greet(other)

    @when(q > 0)
    def _():
        greet((s, q - 1, n - 1))

    @when(both(q > 0, h < n - 1))
    def _():
        greet((s, q - 1, h))

    await_greets(n + one_if(q < seqs - 1) * (1 + (n - 1) * one_if(h == n - 1)))

    def at_rows(owner):
        return pl.ds(pl.multiple_of(owner * rows, rows), rows)

    def slot_rows(owner):
        return pl.ds(pl.multiple_of(HALO + owner * rows, HALO), rows)

    def chain(u, k):
        cut = pl.ds(k * piece, piece)
        return remote(
            sbuf.at[u, cut], st.at[u, cut], c_s.at[u, k], c_r.at[u, k], (s, q + 1, h)
        )

    def squares(u, j):
        return remote(
            ssend.at[u], srecv.at[u, j], q_s.at[u, j], q_r.at[u, j], (s, q, peers[j])
        )

    def scatter(u, j, layer):
        src, dst = (part, rbuf) if layer else (part0, rbuf0)
        mb = u - layer * count
        return remote(
            src.at[mb, at_rows(peers[j])], dst.at[mb, j], s_s.at[u, j], s_r.at[u, j],
            (s, q, peers[j]),
        )

    def gather(u, j, owner):
        where = (u + count, slot_rows(owner))
        return remote(
            normed.at[where], normed.at[where], g_s.at[u, j], g_r.at[u, j], (s, q, peers[j])
        )

    def edge(u, head):
        return remote(
            normed.at[u + count, pl.ds(tokens, HALO)], normed.at[u + count, pl.ds(0, HALO)],
            h_s.at[u, head], h_r.at[u], (s, q + 1, head),
        )

    def ship_local(src, mb, layer):
        return pltpu.make_async_copy(src.at[mb], lo.at[s * count + mb], l_c.at[mb])

    def ship(src, mb):
        return remote(src.at[mb], lo.at[s * count + mb], l_s.at[mb], l_r.at[mb], other)

    def send_out(src, mb, layer):
        @when(s == layer)
        def _():
            ship_local(src, mb, layer).start()

        @when(s != layer)
        def _():
            ship(src, mb).start()

    def add_stats(layer, mb, h_new, branch):
        live = pad[mb]
        stats[layer, 0:1] += jnp.sum(
            jnp.sum(h_new * h_new, axis=1, keepdims=True) * live, axis=0, keepdims=True
        )
        stats[layer, 1:2] += jnp.sum(
            jnp.sum(branch * branch, axis=1, keepdims=True) * live, axis=0, keepdims=True
        )
        stats[layer, 2:3] += jnp.sum(live, axis=0, keepdims=True)

    def pass_state(u):
        for k in range(PIECES):
            @when(q > 0)
            def _():
                chain(u, k).wait_recv()

            @when(first_q)
            def _():
                st[u, k * piece : (k + 1) * piece] = jnp.zeros((piece, LANES), BF)

            @when(q < seqs - 1)
            def _():
                per = inner // heads
                for i in range(k * heads // PIECES, (k + 1) * heads // PIECES):
                    cut = slice(i * per, (i + 1) * per)
                    sbuf[u, cut] = (
                        car[u, i : i + 1] * st[u, cut].astype(F32) + con[cut]
                    ).astype(BF)
                chain(u, k).start()

    def weight(i, layer):
        src, dst = ((pr_in, pr), (wc_in, wc), (wo_in, wo))[i]
        return remote(src, dst.at[layer], w_s.at[i], w_r.at[i], other)

    halo_copy = remote(edge_in, halo, w_s.at[3], w_r.at[3], (s, q + 1, h))
    weight(0, s).start()

    @when(q < seqs - 1)
    def _():
        halo_copy.start()

    weight(1, s).start()
    weight(2, s).start()
    pr[s] = pr_in[...]
    wc[s] = wc_in[...]
    wo[s] = wo_in[...]

    @when(q > 0)
    def _():
        halo_copy.wait_recv()

    @when(first_q)
    def _():
        halo[:, :, :model] = jnp.zeros((count, HALO, model), F32)
        halo[:, :, model:] = jnp.full((count, HALO, LANES), -1.0, F32)

    seg[:, :HALO] = halo[:, :, model:]
    seg[:, HALO:] = seg_in[...]
    weight(0, 1 - s).wait_recv()

    def needs_weights(u):
        return u == count * (1 - s)

    def in_norm(mb, _):
        hx = jnp.concatenate([halo[mb, :, :model], hid[mb]], axis=0)
        scale = lax.rsqrt(jnp.mean(hx * hx, axis=1, keepdims=True) + EPS)
        normed[mb, :, :model] = (hx * scale * pr[0, 0:1]).astype(BF)
        normed[mb, :, model:] = two_lanes(scale)

        @when(first_q)
        def _():
            normed[mb + count, :HALO] = jnp.zeros((HALO, model + LANES), BF)

        return 0

    load.wait()
    stats[...] = jnp.zeros_like(stats)
    lax.fori_loop(0, count, in_norm, 0)

    def local_part(u):
        layer = u // count
        mb = lax.rem(u, count)
        prm = pr[layer]
        x = normed[u, :, :model]
        new_raw = mm(x, wc[layer, :, inner : inner + wide]).astype(BF)
        raw[u] = new_raw
        raw_f[...] = new_raw.astype(F32)
        x = x[HALO:]
        z[u] = mm(x, wc[layer, :, :inner])
        new_dtp = mm(x, wc[layer, :, inner + wide :]) + prm[6:7, :LANES]
        dtp[u] = new_dtp
        new_dt = jax.nn.softplus(new_dtp)
        dt[u] = new_dt
        new_cum = mm(lower(tokens), new_dt * prm[7:8, :LANES], HIGH)
        cum[u] = new_cum
        cum_t = new_cum.T
        dt_t = new_dt.T
        same = same_rows(seg, mb, tokens)
        pieces = []
        for col in range(0, wide, LANES):
            pre = convolved(raw_f, same, prm, col, tokens)
            piece = (pre * sigmoid(pre)).astype(BF)
            co[u, :, col : col + LANES] = piece
            pieces.append(piece)
        values = jnp.concatenate(pieces[: inner // LANES], axis=1)
        in_b, in_c = pieces[-2], pieces[-1]
        entry, decay_end = gains(new_cum, seg, mb)
        toward = expand(decay_end * new_dt, matrix)
        con[...] = fine(mm_tn, values.astype(F32) * toward, in_b)
        mine = seg[mb, HALO:]
        same_before = (mine[-1:, :] == seg[mb, HALO - 1 : HALO]).astype(F32)
        car[u] = jnp.exp(cum_t[:heads, tokens - 1 :]) * same_before

        @when(first_q)
        def _():
            pass_state(u)

        inner_cb = jnp.where(
            causal_mask(seg, srow, mb, tokens, False), mm_nt(in_c, in_b), 0.0
        )
        lane = iota((tokens, LANES), 1)
        for pair in range(heads // 2):
            cols = slice(pair * LANES, (pair + 1) * LANES)
            acc = jnp.zeros((tokens, LANES), F32)
            for j in range(2):
                one = slice(2 * pair + j, 2 * pair + j + 1)
                decay = jnp.exp(jnp.minimum(new_cum[:, one] - cum_t[one, :], 0.0))
                mask = jnp.right_shift(lane, HEAD_SHIFT) == j
                value = jnp.where(mask, values[:, cols], jnp.zeros((), BF))
                acc = acc + mm((inner_cb * decay * dt_t[one, :]).astype(BF), value)
            yn[u, :, cols] = acc

    def gate_part(u):
        layer = u // count
        mb = lax.rem(u, count)
        entry, _ = gains(cum[u], seg, mb)
        in_c = co[u, :, inner + LANES :]
        readout = mm_nt(in_c, st[u])
        y = yn[u] + expand(entry, matrix) * readout
        yn[u] = y
        ssd = y + pr[layer, 8:9, :inner] * co[u, :, :inner].astype(F32)
        gate = z[u]
        gated = ssd * (gate * sigmoid(gate))
        gated_s[...] = gated
        ones = jnp.ones((8, inner), BF)
        ssend[u] = fine(lambda a, b: mm_nt(b, a), gated * gated, ones)

    def out_part(u):
        layer = u // count
        total = ssend[u]
        for j in range(n - 1):
            squares(u, j).wait_recv()
            total = total + srecv[u, j]
        scale_row = lax.rsqrt(total / full + EPS)
        scale = mm_tn(scale_row * 0.125, jnp.ones((8, LANES), F32), HIGH)
        gsc[u] = scale
        x = (gated_s[...] * wide_copy(scale, inner) * pr[layer, 9:10, :inner]).astype(BF)
        product = mm(x, wo[layer])

        @when(u < count)
        def _():
            part0[u] = product.astype(BF)
            for j in range(n - 1):
                scatter(u, j, 0).start()

        @when(u >= count)
        def _():
            part[u - count] = product.astype(BF)
            for j in range(n - 1):
                scatter(u, j, 1).start()

    def finish(u):
        @when(u < count)
        def _():
            total = part0[u, at_rows(h)].astype(F32)
            for j in range(n - 1):
                scatter(u, j, 0).wait_recv()
                total = total + rbuf0[u, j].astype(F32)
            h_new = hid[u, at_rows(h)] + total
            scale = lax.rsqrt(jnp.mean(h_new * h_new, axis=1, keepdims=True) + EPS)
            normed[u + count, slot_rows(h), :model] = (h_new * scale * pr[1, 0:1]).astype(BF)
            normed[u + count, slot_rows(h), model:] = two_lanes(scale)

        @when(u >= count)
        def _():
            total = part[u - count, at_rows(h)].astype(F32)
            for j in range(n - 1):
                scatter(u, j, 1).wait_recv()
                total = total + rbuf[u - count, j].astype(F32)
            normed[u + count, slot_rows(h), :model] = total.astype(BF)
            normed[u + count, slot_rows(h), model:] = jnp.zeros((rows, LANES), BF)

        for j in range(n - 1):
            gather(u, j, h).start()

        @when(both(u < count, edge_owner))
        def _():
            for head in range(n):
                edge(u, head).start()

    def arrived(u):
        for j in range(n - 1):
            gather(u, j, froms[j]).wait_recv()

    def step(u, _):
        @when(both(u >= count, u < units))
        def _():
            mb = u - count
            arrived(mb)

            @when(q > 0)
            def _():
                edge(mb, 0).wait_recv()

            scale = jnp.sum(normed[u, HALO:, model:].astype(F32), axis=1, keepdims=True)
            h_new = normed[u, HALO:, :model].astype(F32) / (scale * pr[1, 0:1])
            h1[mb] = h_new
            send_out(h1, mb, 0)
            add_stats(0, mb, h_new, h_new - hid[mb])

        @when(u == count)
        def _():
            finish(u - 1)

        @when(needs_weights(u))
        def _():
            weight(1, 1 - s).wait_recv()

        @when(u < units)
        def _():
            local_part(u)

            @when(q > 0)
            def _():
                pass_state(u)

            gate_part(u)
            for j in range(n - 1):
                squares(u, j).start()

        @when(both(u > 0, u != count))
        def _():
            finish(u - 1)

        @when(needs_weights(u))
        def _():
            weight(2, 1 - s).wait_recv()

        @when(u < units)
        def _():
            out_part(u)

        return 0

    lax.fori_loop(0, units + 1, step, 0)

    def last_out(mb, _):
        arrived(mb + count)
        branch = normed[mb + units, HALO:, :model].astype(F32)
        h_new = h1[mb] + branch
        lo1[mb] = h_new
        send_out(lo1, mb, 1)
        add_stats(1, mb, h_new, branch)
        return 0

    lax.fori_loop(0, count, last_out, 0)

    def drain(u, _):
        for j in range(n - 1):
            squares(u, j).wait_send()
            gather(u, j, h).wait_send()

        @when(u < count)
        def _():
            for j in range(n - 1):
                scatter(u, j, 0).wait_send()

        @when(u >= count)
        def _():
            for j in range(n - 1):
                scatter(u, j, 1).wait_send()

        @when(q < seqs - 1)
        def _():
            for k in range(PIECES):
                chain(u, k).wait_send()

        @when(both(u < count, edge_owner))
        def _():
            for head in range(n):
                edge(u, head).wait_send()

        return 0

    lax.fori_loop(0, units, drain, 0)
    for i in range(3):
        weight(i, s).wait_send()

    @when(q < seqs - 1)
    def _():
        halo_copy.wait_send()

    def drain_out(mb, _):
        ship_local(h1, mb, 0).wait()
        ship(h1, mb).wait_send()
        remote(
            h1.at[mb], lo.at[(1 - s) * count + mb], l_s.at[mb], l_r.at[mb], other
        ).wait_recv()
        return 0

    lax.fori_loop(0, count, drain_out, 0)


def bwd_kernel(seqs, n, cot, hid, kept, wc_in, wo_in, raw_in, z_in, dtp_in, dt_in, cum_in,
               co_in, st_in, yn_in, gsc_in, pad, car, stats, seg, srow, pr,
               out, small_o, ig,
               gin, normed, wc, wo, raw, z, dtp, dt, cum, co, st, yn, gsc,
               big, pbuf, table, ps, rs_, ts,
               raw_f, shift, gconv, gext, gz, gy_s, ng, ob, gdr, back, nxt, sbuf,
               part, hpart, rbuf, hbuf, acc, ag, gwb, small, srecv, ggn, dsend, drecv,
               c_s, c_r, s_s, s_r, g_s, g_r, h_s, h_r, m_s, m_r, l_c, l_s, l_r, in_s,
               d_s, d_r, f_s, w_s, x_s, x_r, a_s, a_r, b_s, b_r, t_s, t_r):
    s, q, h = place()
    count, tokens, model = gin.shape[0] // 2, gin.shape[1], gin.shape[2]
    inner = wo.shape[0]
    state = LANES
    wide = raw.shape[2]
    heads = inner >> HEAD_SHIFT
    rows = tokens // n
    ext = tokens + HALO
    steps = 2 * count
    full = inner * n
    piece = inner // PIECES
    other = (1 - s, q, h)
    edge_owner = both(h == n - 1, q < seqs - 1)
    peers = [lax.rem(h + j, n) for j in range(1, n)]
    froms = [lax.rem(h + n - j, n) for j in range(1, n)]
    matrix = spread_matrix(inner)
    sources = (raw_in, z_in, dtp_in, dt_in, cum_in, co_in, st_in, yn_in, gsc_in)
    targets = (raw, z, dtp, dt, cum, co, st, yn, gsc)

    def unit(w):
        return (1 - w // count) * count + lax.rem(w, count)

    def stream(w):
        k = lax.rem(w, count)
        return [
            pltpu.make_async_copy(a.at[unit(w)], b.at[k], f_s.at[i, k])
            for i, (a, b) in enumerate(zip(sources, targets))
        ]

    def wc_load(layer):
        return pltpu.make_async_copy(wc_in.at[layer], wc, w_s.at[0])

    def wo_load(layer):
        return pltpu.make_async_copy(wo_in.at[layer], wo, w_s.at[1])

    loads = [
        pltpu.make_async_copy(cot.at[pl.ds(s * count, count)], gin.at[pl.ds(0, count)], in_s.at[0]),
        pltpu.make_async_copy(
            hid.at[pl.ds(s * count, count)], gin.at[pl.ds(count, count)], in_s.at[1]
        ),
        pltpu.make_async_copy(kept.at[pl.ds(0, steps)], normed, in_s.at[2]),
    ]
    wo_load(1).start()
    for load in loads:
        load.start()
    for load in stream(0):
        load.start()
    wc_load(1).start()
    for p in peers:
        greet((s, q, p))
    greet(other)

    @when(q < seqs - 1)
    def _():
        greet((s, q + 1, h))

    @when(edge_owner)
    def _():
        for head in range(n - 1):
            greet((s, q + 1, head))

    @when(q > 0)
    def _():
        greet((s, q - 1, h))

    await_greets(
        n + one_if(q > 0) * (1 + one_if(h < n - 1)) + one_if(q < seqs - 1)
    )

    def at_rows(owner):
        return pl.ds(pl.multiple_of(owner * rows, rows), rows)

    def slot(w):
        return lax.rem(w, count)

    def chain(w, k):
        cut = pl.ds(k * piece, piece)
        return remote(
            sbuf.at[slot(w), cut], nxt.at[w, cut], c_s.at[w, k], c_r.at[w, k], (s, q - 1, h)
        )

    def scatter(w, j):
        return remote(
            part.at[slot(w), at_rows(peers[j])], rbuf.at[slot(w), j], s_s.at[w, j],
            s_r.at[w, j], (s, q, peers[j]),
        )

    def gather(w, j, owner):
        where = (slot(w), at_rows(owner))
        return remote(
            ag.at[where], ag.at[where], g_s.at[w, j], g_r.at[w, j], (s, q, peers[j])
        )

    def edge(w, head):
        return remote(
            hpart.at[w], hbuf.at[w, head], h_s.at[w], h_r.at[w, head], (s, q - 1, n - 1)
        )

    def little(layer, j):
        return remote(
            small.at[layer], srecv.at[layer, j], m_s.at[layer, j], m_r.at[layer, j],
            (s, q, peers[j]),
        )

    def ship_local(v):
        mb = lax.rem(v, count)
        return pltpu.make_async_copy(gin.at[v], ig.at[s * count + mb], l_c.at[mb])

    def ship(v):
        mb = lax.rem(v, count)
        return remote(gin.at[v], ig.at[s * count + mb], l_s.at[mb], l_r.at[mb], other)

    def norm_part(v):
        layer = 1 - v // count
        mb = lax.rem(v, count)
        u = layer * count + mb
        for j in range(n - 1):
            gather(v, j, froms[j]).wait_recv()
        gn = ag[mb, :, :model].astype(F32)
        scale = jnp.sum(normed[u, HALO:, model:].astype(F32), axis=1, keepdims=True)
        gain = pr[layer, 0:1]

        def rest(h_in, grad_out):
            x = gn * gain
            dots = jnp.sum(x * h_in, axis=1, keepdims=True)
            gin[v] = grad_out + x * scale - h_in * (scale * scale * scale * dots / model)
            table[layer, 0:1] += jnp.sum(gn * h_in * scale, axis=0, keepdims=True)

        @when(layer == 1)
        def _():
            rest(
                normed[u, HALO:, :model].astype(F32) / (scale * gain),
                gin[mb] * wide_copy(pad[mb], model),
            )

        @when(layer == 0)
        def _():
            rest(gin[v], gin[mb])

        @when(s == layer)
        def _():
            ship_local(v).start()

        @when(s != layer)
        def _():
            ship(v).start()

        grad_w = mm_tn(normed[u, HALO:, :model], ag[mb, :, model:])

        @when(mb == 0)
        def _():
            gwb[...] = grad_w

        @when(mb > 0)
        def _():
            gwb[...] += grad_w

        @when(mb == count - 1)
        def _():
            base = model + inner
            deep = 2 * state
            for k in range(model // deep):
                cut = slice(k * deep, (k + 1) * deep)
                big[layer, base : base + deep, cut] = gwb[cut].astype(TOTAL_T)

            @when(s != layer)
            def _():
                start_cross((model + inner) // CHUNK, 2 * chunks)

    def dots(w, j):
        return remote(
            dsend.at[w], drecv.at[w, j], d_s.at[w, j], d_r.at[w, j], (s, q, peers[j])
        )

    def gate_forward(mb, layer):
        gate = z[mb]
        sig = sigmoid(gate)
        silu = gate * sig
        ssd = yn[mb] + pr[layer, 8:9, :inner] * co[mb, :, :inner].astype(F32)
        return gate, sig, silu, ssd, ssd * silu

    def gate_first(w):
        layer = 1 - w // count
        mb = lax.rem(w, count)
        u = layer * count + mb

        @when(layer == 1)
        def _():
            ob[mb] = (gin[mb] * wide_copy(pad[mb], model)).astype(BF)

        @when(layer == 0)
        def _():
            ob[mb] = gin[mb].astype(BF)

        grad_gn = mm_nt(ob[mb], wo[...])
        ggn[...] = grad_gn
        gated = gate_forward(mb, layer)[-1]
        ones = jnp.ones((8, inner), BF)
        dsend[w] = fine(
            lambda a, b: mm_nt(b, a), grad_gn * gated * pr[layer, 9:10, :inner], ones
        )
        for j in range(n - 1):
            dots(w, j).start()

    def conv_slope(w):
        mb = lax.rem(w, count)
        raw_f[...] = raw[mb].astype(F32)
        same = same_rows(seg, mb, tokens)
        prm = pr[1 - w // count]
        for col in range(0, wide, LANES):
            pre = convolved(raw_f, same, prm, col, tokens)
            sig = sigmoid(pre)
            gconv[:, col : col + LANES] = sig * (1.0 + pre * (1.0 - sig))

    def gate_part(w):
        layer = 1 - w // count
        mb = lax.rem(w, count)
        u = layer * count + mb
        total = dsend[w]
        for j in range(n - 1):
            dots(w, j).wait_recv()
            total = total + drecv[w, j]
        across = mm_tn(total * 0.125, jnp.ones((8, LANES), F32), HIGH)
        scale = gsc[mb]
        scale_x = wide_copy(scale, inner)
        gate, sig, silu, ssd, gated = gate_forward(mb, layer)
        grad_gn = ggn[...]
        values = co[mb, :, :inner].astype(F32)
        gain = pr[layer, 9:10, :inner]
        scaled = gated * scale_x
        grad_gated = grad_gn * (gain * scale_x) - scaled * wide_copy(
            scale * scale * across / full, inner
        )
        gy = (grad_gated * silu).astype(BF)
        gy_s[...] = gy
        gz[mb] = (grad_gated * ssd * (sig * (1.0 + gate * (1.0 - sig)))).astype(BF)
        ng[mb] = (scaled * gain).astype(BF)
        gy_f = gy.astype(F32)
        table[layer, 8:9, :inner] += jnp.sum(grad_gn * scaled, axis=0, keepdims=True)
        table[layer, 9:10, :inner] += jnp.sum(gy_f * values, axis=0, keepdims=True)
        entry, _ = gains(cum[mb], seg, mb)
        read = expand(entry, matrix) * gy_f
        back[...] = fine(mm_tn, read, co[mb, :, inner + state :])

        @when(q == seqs - 1)
        def _():
            pass_state(w, u)

    def pass_state(w, u):
        per = inner // heads
        for k in range(PIECES):
            @when(q < seqs - 1)
            def _():
                chain(w, k).wait_recv()

            @when(q == seqs - 1)
            def _():
                nxt[w, k * piece : (k + 1) * piece] = jnp.zeros((piece, LANES), BF)

            @when(q > 0)
            def _():
                @when(w >= count)
                def _():
                    chain(w - count, k).wait_send()

                for i in range(k * heads // PIECES, (k + 1) * heads // PIECES):
                    cut = slice(i * per, (i + 1) * per)
                    sbuf[slot(w), cut] = (
                        car[u, i : i + 1] * nxt[w, cut].astype(F32) + back[cut]
                    ).astype(BF)
                chain(w, k).start()

    def local_part(w):
        layer = 1 - w // count
        mb = lax.rem(w, count)
        u = layer * count + mb
        prm = pr[layer]
        cum_u, dt_u = cum[mb], dt[mb]
        cum_t = cum_u.T
        entry, decay_end = gains(cum_u, seg, mb)
        values = co[mb, :, :inner]
        in_b = co[mb, :, inner : inner + state]
        in_c = co[mb, :, inner + state :]
        gy = gy_s[...]
        gy_f = gy.astype(F32)
        causal = causal_mask(seg, srow, mb, tokens, True)
        inner_bc = jnp.where(causal, mm_nt(in_b, in_c), 0.0)
        grad_inner = jnp.zeros((tokens, tokens), F32)
        lane = iota((tokens, LANES), 1)
        grad_dt = jnp.zeros((tokens, LANES), F32)
        locals_, rows_ = [], []
        for pair in range(heads // 2):
            cols = slice(pair * LANES, (pair + 1) * LANES)
            total = jnp.zeros((tokens, LANES), F32)
            for j in range(2):
                head = 2 * pair + j
                one = slice(head, head + 1)
                dt_col = dt_u[:, one]
                decay = jnp.exp(jnp.minimum(cum_t[one, :] - cum_u[:, one], 0.0))
                mask = jnp.right_shift(lane, HEAD_SHIFT) == j
                gy_one = jnp.where(mask, gy[:, cols], jnp.zeros((), BF))
                grad_mix = mm_nt(values[:, cols], gy_one)
                mixed = inner_bc * decay
                total = total + mm((mixed * dt_col).astype(BF), gy_one)
                grad_inner = grad_inner + grad_mix * (decay * dt_col)
                weighted = grad_mix * mixed
                sums = jnp.sum(weighted, axis=1, keepdims=True)
                grad_dt = jnp.where(lane == head, sums, grad_dt)
                rows_.append(jnp.sum(weighted * dt_col, axis=0, keepdims=True))
            locals_.append(total)
            tick(w, 6 + 2 * pair, 2)

        @when(w > 0)
        def _():
            finish(w - 1)

        tick(w, 14, 1)

        @when(q < seqs - 1)
        def _():
            pass_state(w, u)

        grad_inner = jnp.where(causal, grad_inner, 0.0)
        toward = decay_end * dt_u
        toward_x = expand(toward, matrix)
        values_f = values.astype(F32)
        pulled = mm_nt(in_b, nxt[w])
        gconv[:, :inner] *= (
            prm[8:9, :inner] * gy_f + jnp.concatenate(locals_, axis=1) + toward_x * pulled
        )
        read = expand(entry, matrix) * gy_f
        from_row = (iota((heads, LANES), 0) == iota((heads, LANES), 1)).astype(F32)
        grad_cum = (
            mm_tn(jnp.concatenate(rows_, axis=0), from_row, HIGH)
            - dt_u * grad_dt
            + head_sums(read * mm_nt(in_c, st[mb]), matrix)
        )
        pulled_sums = head_sums(values_f * pulled, matrix)
        grad_dt = grad_dt + pulled_sums * decay_end
        high, low = split(nxt[w].astype(F32) * st[mb].astype(F32))
        carried = jnp.sum(
            lax.dot_general(high, matrix, (((0,), (1,)), ((), ())), preferred_element_type=F32)
            + lax.dot_general(low, matrix, (((0,), (1,)), ((), ())), preferred_element_type=F32),
            axis=0,
            keepdims=True,
        )
        ahead = (iota((tokens, tokens), 0) > iota((tokens, tokens), 1)).astype(F32)
        grad_rate = (
            mm_tn(lower(tokens), grad_cum, HIGH)
            + mm(ahead, pulled_sums * toward, HIGH)
            + carried * entry[-1:]
        )
        neg = prm[7:8, :LANES]
        grad_pre = (grad_dt + grad_rate * neg) * sigmoid(dtp[mb])
        table[layer, 6:7, :LANES] += jnp.sum(grad_pre, axis=0, keepdims=True)
        table[layer, 7:8, :LANES] += jnp.sum(grad_rate * dt_u * neg, axis=0, keepdims=True)
        grad_raw_dt = grad_pre.astype(BF)
        gdr[mb] = grad_raw_dt
        gconv[:, inner : inner + state] *= fine(mm, grad_inner, in_c) + fine(
            mm, values_f * toward_x, nxt[w]
        )
        gconv[:, inner + state :] *= fine(mm_tn, grad_inner, in_b) + fine(mm, read, st[mb])
        same = same_rows(seg, mb, tokens)
        first = HALO - KC + 1
        shift[:HALO] = jnp.zeros((HALO, LANES), F32)
        shift[ext:] = jnp.zeros((HALO, LANES), F32)
        for col in range(0, wide, LANES):
            cols = slice(col, col + LANES)
            grad = gconv[:, cols]
            target = table if col < inner else small
            off = col if col < inner else col - inner
            tc = slice(off, off + LANES)
            target[layer, 5:6, tc] += jnp.sum(grad, axis=0, keepdims=True)
            total = jnp.zeros((ext, LANES), F32)
            for k in range(KC):
                masked = grad * same[k]
                target[layer, 1 + k : 2 + k, tc] += jnp.sum(
                    masked * raw_f[first + k : first + k + tokens, cols], axis=0, keepdims=True
                )
                shift[HALO:ext] = masked * prm[1 + k : 2 + k, cols]
                total = total + shift[KC - 1 - k : KC - 1 - k + ext]
            gext[mb, :, cols] = total.astype(BF)
            if col % (2 * LANES):
                tick(w, 15 + col // (2 * LANES), 1)
        grad_raw = gext[mb]
        main = mm_nt(gz[mb], wc[:, :inner]) + mm_nt(
            grad_raw_dt, wc[:, inner + wide :]
        )
        rest = mm_nt(grad_raw, wc[:, inner : inner + wide])
        part[mb, :, :model] = (main + rest[HALO:]).astype(BF)
        hpart[w, :, :model] = rest[:HALO].astype(BF)
        part[mb, :, model:] = grad_raw[HALO:, inner:]
        hpart[w, :, model:] = grad_raw[:HALO, inner:]

    def finish(w):
        acc[...] = part[slot(w), at_rows(h)].astype(F32)
        for j in range(n - 1):
            scatter(w, j).wait_recv()
            acc[...] += rbuf[slot(w), j].astype(F32)

        @when(edge_owner)
        def _():
            for head in range(n):
                edge(w, head).wait_recv()
                acc[rows - HALO :] += hbuf[w, head].astype(F32)

        ag[slot(w), at_rows(h)] = acc[...].astype(BF)
        for j in range(n - 1):
            gather(w, j, h).start()

    def weights_part(layer):
        gate_w = jnp.zeros((inner, model), F32)
        z_w = jnp.zeros((model, inner), F32)
        x_w = jnp.zeros((model, inner), F32)
        dt_w = jnp.zeros((LANES, model), F32)
        for mb in range(count):
            x = normed[layer * count + mb, :, :model]
            gate_w = gate_w + mm_tn(ng[mb], ob[mb])
            z_w = z_w + mm_tn(x[HALO:], gz[mb])
            x_w = x_w + mm_tn(x, gext[mb, :, :inner])
            dt_w = dt_w + mm_tn(gdr[mb], x[HALO:])
        big[layer, :model, :inner] = z_w.astype(TOTAL_T)
        big[layer, :model, inner:] = x_w.astype(TOTAL_T)
        big[layer, model : model + inner] = gate_w.astype(TOTAL_T)
        table[layer, 16:24] = dt_w[:8]
        for j in range(n - 1):
            little(layer, j).start()

        @when(s != layer)
        def _():
            start_cross(0, (model + inner) // CHUNK)

    chunks = big.shape[1] // (2 * CHUNK)
    right = SKEW + LEAD * s
    left = SKEW
    ends = [(q > 0, q < seqs - 1), (q < seqs - 1, q > 0)]
    ahead = [right * q, left * (seqs - 1 - q)]
    behind = [
        right * (seqs - 1) + left * (seqs - 1 - q), left * (seqs - 1) + right * q
    ]

    def cross_at(k):
        at = pl.ds(pl.multiple_of(k * CHUNK, CHUNK), CHUNK)
        return remote(big.at[1 - s, at], pbuf.at[at], x_s.at[k], x_r.at[k], other)

    def start_cross(low, high):
        def one(k, _):
            cross_at(k).start()
            return 0

        lax.fori_loop(low, high, one, 0)

    def span(side, c):
        return pl.ds(pl.multiple_of((side * chunks + c) * CHUNK, CHUNK), CHUNK)

    def along(side, c):
        k, at = side * chunks + c, span(side, c)
        return remote(
            big.at[s, at], out.at[at], a_s.at[k], a_r.at[k], (s, q + 1 - 2 * side, h)
        )

    def home(side, c):
        k, at = side * chunks + c, span(side, c)
        return remote(out.at[at], out.at[at], b_s.at[k], b_r.at[k], (s, q - 1 + 2 * side, h))

    def advance(t):
        for side in range(2):
            has_prev, has_next = ends[side]
            c = t - ahead[side]

            @when(both(c >= 0, c < chunks))
            def _():
                at = span(side, c)
                cross_at(side * chunks + c).wait_recv()
                sums = big[s, at].astype(F32) + pbuf[at].astype(F32)

                @when(has_prev)
                def _():
                    along(side, c).wait_recv()
                    big[s, at] = (sums + out[at].astype(F32)).astype(TOTAL_T)

                @when(jnp.logical_not(has_prev))
                def _():
                    big[s, at] = sums.astype(TOTAL_T)

                @when(has_next)
                def _():
                    along(side, c).start()

                @when(jnp.logical_not(has_next))
                def _():
                    out[at] = big[s, at]

                    @when(has_prev)
                    def _():
                        home(side, c).start()

            e = t - behind[side]

            @when(both(has_next, both(e >= 0, e < chunks)))
            def _():
                home(side, e).wait_recv()

                @when(has_prev)
                def _():
                    home(side, e).start()

    def advance_many(start, amount):
        def one(i, _):
            advance(start + i)
            return 0

        lax.fori_loop(0, amount, one, 0)

    def tick(w, offset, amount):
        @when(both(s == 1, w >= count))
        def _():
            advance_many((w - count) * TICKS + offset, amount)

    def tail_tick(w, offset, amount):
        advance_many((w - steps) * TAIL_TICKS + offset + s * count * TICKS, amount)

    table[...] = jnp.zeros_like(table)
    small[...] = jnp.zeros_like(small)
    table[:, 24:32, :LANES] = stats[...]
    for load in loads:
        load.wait()

    def step(w, _):
        @when(w < steps)
        def _():
            for load in stream(w):
                load.wait()

        @when(w + 1 < steps)
        def _():
            for load in stream(w + 1):
                load.start()

        @when(w >= count)
        def _():
            norm_part(w - count)

        @when(w >= steps)
        def _():
            tail_tick(w, 0, TAIL_TICKS // 2)

            @when(w == steps)
            def _():
                finish(w - 1)

            tail_tick(w, TAIL_TICKS // 2, TAIL_TICKS // 2)

        @when(w < steps)
        def _():
            tick(w, 0, 2)

            @when(both(lax.rem(w, count) == 0, w < steps))
            def _():
                wo_load(0).wait()

            gate_first(w)

            @when(w == count - 1)
            def _():
                wo_load(0).start()

            tick(w, 2, 2)
            conv_slope(w)
            tick(w, 4, 1)
            gate_part(w)
            tick(w, 5, 1)

            @when(w >= count)
            def _():
                for j in range(n - 1):
                    scatter(w - count, j).wait_send()
                    gather(w - count, j, h).wait_send()

            @when(lax.rem(w, count) == 0)
            def _():
                wc_load(0).wait()

            local_part(w)

            @when(w == count - 1)
            def _():
                wc_load(0).start()

            @when(q > 0)
            def _():
                edge(w, h).start()

            for j in range(n - 1):
                scatter(w, j).start()

            tick(w, 18, 2)

            @when(lax.rem(w, count) == count - 1)
            def _():
                weights_part(1 - w // count)

        return 0

    lax.fori_loop(0, steps + count, step, 0)

    def drain(w, _):
        @when(w >= count)
        def _():
            for j in range(n - 1):
                scatter(w, j).wait_send()
                gather(w, j, h).wait_send()

            @when(q > 0)
            def _():
                for k in range(PIECES):
                    chain(w, k).wait_send()

        for j in range(n - 1):
            dots(w, j).wait_send()

        @when(q > 0)
        def _():
            edge(w, h).wait_send()

        return 0

    lax.fori_loop(0, steps, drain, 0)
    for layer in range(2):
        total = small[layer]
        for j in range(n - 1):
            little(layer, j).wait_recv()
            total = total + srecv[layer, j]
        for j in range(n - 1):
            little(layer, j).wait_send()
        table[layer, 1:6, inner : inner + 2 * state] = total[1:6]
    small_cross = remote(table.at[1 - s], ps, t_s.at[0], t_r.at[0], other)
    small_along = remote(ts, rs_, t_s.at[1], t_r.at[1], (s, q + 1, h))
    small_home = remote(small_o, small_o, t_s.at[2], t_r.at[2], (s, q - 1, h))
    small_cross.start()
    done = count * TAIL_TICKS
    first_end = chunks + 2 * SKEW * (seqs - 1)
    second_end = chunks + (2 * SKEW + LEAD) * (seqs - 1) - count * TICKS
    last = max(first_end, second_end, done + 4)

    def finish_tick(t, _):
        @when(t == done + 2)
        def _():
            small_cross.wait_recv()
            ts[...] = table[s] + ps[...]

            @when(q > 0)
            def _():
                small_along.wait_recv()
                ts[...] += rs_[...]

            @when(q < seqs - 1)
            def _():
                small_along.start()

            @when(q == seqs - 1)
            def _():
                small_o[...] = ts[...]

                @when(q > 0)
                def _():
                    small_home.start()

        advance(t + s * count * TICKS)
        return 0

    lax.fori_loop(done, last, finish_tick, 0)

    @when(q < seqs - 1)
    def _():
        small_home.wait_recv()

        @when(q > 0)
        def _():
            small_home.start()

    def drain_sum(c, _):
        for side in range(2):
            has_prev, has_next = ends[side]
            cross_at(side * chunks + c).wait_send()

            @when(has_next)
            def _():
                along(side, c).wait_send()

            @when(has_prev)
            def _():
                home(side, c).wait_send()

        return 0

    lax.fori_loop(0, chunks, drain_sum, 0)
    small_cross.wait_send()

    @when(q < seqs - 1)
    def _():
        small_along.wait_send()

    @when(q > 0)
    def _():
        small_home.wait_send()

    def drain_out(mb, _):
        ship_local(mb).wait()
        ship(mb).wait_send()
        remote(
            gin.at[mb], ig.at[(1 - s) * count + mb], l_s.at[mb], l_r.at[mb], other
        ).wait_recv()
        return 0

    lax.fori_loop(0, count, drain_out, 0)


def pad_lanes(a, width):
    return jnp.pad(a, ((0, 0), (0, width - a.shape[1])))


def final_kernel(zx, wo, bc, table, g_zx, g_wo, g_bc, rms, g_norm, g_dt, g_cx, g_cxb, g_cb, g_cbb,
                 g_dtb, g_al, g_sk, g_gate):
    inner = g_zx.shape[3]
    model = table.shape[1]
    heads = g_dtb.shape[1]
    step = pl.program_id(0)
    g_zx[0, :, 0, :] = zx[:, :inner].astype(F32)
    g_zx[0, :, 1, :] = zx[:, inner:].astype(F32)
    g_wo[0] = wo[...].astype(F32)

    @when(step == 0)
    def _():
        deep = g_bc.shape[2]
        for k in range(model // deep):
            cut = slice(k * deep, (k + 1) * deep)
            g_bc[0, cut] = bc[:, cut].astype(F32)
        live = table[26:27, :LANES] * model
        first = jnp.sqrt(table[24:25, :LANES] / live)
        second = jnp.sqrt(table[25:26, :LANES] / live)
        rms[...] = jnp.where(iota((1, LANES), 1) == 0, first, second)[:, :2]
        g_norm[...] = table[0:1]
        g_dt[0] = table[16 : 16 + heads]
        g_cx[0] = table[1:5, :inner]
        g_cxb[...] = table[5:6, :inner]
        g_cb[0] = table[1:5, inner : inner + deep]
        g_cbb[...] = table[5:6, inner : inner + deep]
        g_dtb[...] = table[6:7, :heads]
        g_al[...] = table[7:8, :heads]
        sums = mm(table[8:16, :inner], spread_matrix(inner).astype(F32).T, HIGH)
        g_sk[...] = sums[1:2, :heads]
        g_gate[...] = table[8:9, :inner]


def finalize(big, table, inner, heads, state):
    model = big.shape[1]
    steps = 4
    deep = 2 * state

    def whole(shape):
        return pl.BlockSpec(shape, lambda i: (0,) * len(shape))

    shapes = [
        (1, model, 2, inner), (1, inner, model), (1, model, deep), (1, 2), (1, model),
        (1, heads, model), (1, 4, inner), (1, inner), (1, 4, deep), (1, deep),
        (1, heads), (1, heads), (1, heads), (1, inner),
    ]
    specs = [
        pl.BlockSpec((1, model // steps, 2, inner), lambda i: (0, i, 0, 0)),
        pl.BlockSpec((1, inner // steps, model), lambda i: (0, i, 0)),
    ] + [whole(x) for x in shapes[2:]]
    base = model // (inner // steps)
    return pl.pallas_call(
        final_kernel,
        grid=(steps,),
        in_specs=[
            pl.BlockSpec((model // steps, model), lambda i: (i, 0)),
            pl.BlockSpec((inner // steps, model), lambda i: (base + i, 0)),
            pl.BlockSpec((deep, model), lambda i: ((model + inner) // deep, 0)),
            whole(table.shape),
        ],
        out_specs=specs,
        out_shape=[jax.ShapeDtypeStruct(x, F32) for x in shapes],
        compiler_params=pltpu.CompilerParams(vmem_limit_bytes=LIMIT),
        name="final",
    )(big, big, big, table)


def local(hidden_in, cotangent, segments, padding, norm_gain, w_zx, w_bc, w_dt, conv_x,
          conv_x_bias, conv_bc, conv_bc_bias, dt_bias, a_log, skip_d, gate_gain, w_out):
    s, q, h = place()
    seqs = lax.axis_size(SEQ)
    n = lax.axis_size(HEAD)
    sections = lax.axis_size(SEC)
    batches, tokens, model = hidden_in.shape
    count = batches // sections
    inner = w_out.shape[1]
    heads = w_dt.shape[2]
    per = inner // heads
    state = w_bc.shape[2] // 2
    wide = inner + 2 * state
    wc = jnp.concatenate(
        [w_zx[0, :, 0], w_zx[0, :, 1], w_bc[0], pad_lanes(w_dt[0], LANES)], axis=1
    )
    prm = jnp.concatenate(
        [
            norm_gain,
            pad_lanes(jnp.concatenate([conv_x[0], conv_bc[0]], axis=1), model),
            pad_lanes(jnp.concatenate([conv_x_bias, conv_bc_bias], axis=1), model),
            pad_lanes(dt_bias, model),
            pad_lanes(-jnp.exp(a_log), model),
            pad_lanes(jnp.repeat(skip_d, per, axis=1), model),
            pad_lanes(gate_gain, model),
            jnp.zeros((6, model), F32),
        ],
        axis=0,
    )

    def mine(a):
        return lax.dynamic_slice_in_dim(a, s * count, count, 0)

    seg = mine(segments).astype(F32)
    pad = jnp.broadcast_to(mine(padding).astype(F32)[:, :, None], (count, tokens, LANES))
    seg_col = jnp.broadcast_to(seg[:, :, None], (count, tokens, LANES))
    srow = jnp.broadcast_to(seg[:, None, :], (count, 8, tokens))
    edge = jnp.concatenate(
        [mine(hidden_in[:, tokens - HALO :]), seg_col[:, tokens - HALO :]], axis=2
    )
    units = 2 * count
    rows = tokens + HALO
    part_rows = tokens // n
    lane_shape = (units, tokens, LANES)
    inner_shape = (units, tokens, inner)
    state_shape = (units, inner, LANES)
    peer_sems = DMA((units, n - 1))
    out_shape = ((batches, tokens, model), F32)
    kept = comm(
        functools.partial(fwd_kernel, seqs, n),
        (hidden_in, edge, seg_col, srow, pad, wc, w_out[0], prm),
        (
            ((units + count, rows, model + LANES), BF),
            ((units, rows, wide), BF),
            (inner_shape, F32),
            (lane_shape, F32),
            (lane_shape, F32),
            (lane_shape, F32),
            ((units, tokens, wide), BF),
            (state_shape, BF),
            ((units, heads, LANES), F32),
            (inner_shape, F32),
            (lane_shape, F32),
            ((2, 8, LANES), F32),
            ((2,) + wc.shape, BF),
            ((2,) + w_out.shape[1:], BF),
            ((2,) + prm.shape, F32),
            ((count, rows, LANES), F32),
            out_shape,
        ),
        [
            pltpu.VMEM(edge.shape, F32),
            pltpu.VMEM((count, tokens, model), F32),
            pltpu.VMEM((count, tokens, model), F32),
            pltpu.VMEM((rows, wide), F32),
            pltpu.VMEM((inner, LANES), F32),
            pltpu.VMEM(state_shape, BF),
            pltpu.VMEM((tokens, inner), F32),
            pltpu.VMEM((count, tokens, model), BF),
            pltpu.VMEM((count, tokens, model), BF),
            pltpu.VMEM((count, n - 1, part_rows, model), BF),
            pltpu.VMEM((count, n - 1, part_rows, model), BF),
            pltpu.VMEM((units, 8, tokens), F32),
            pltpu.VMEM((units, n - 1, 8, tokens), F32),
            pltpu.VMEM((count, tokens, model), F32),
            DMA((units, PIECES)), DMA((units, PIECES)),
            peer_sems, peer_sems, peer_sems, peer_sems, peer_sems, peer_sems,
            DMA((count, n)), DMA((count,)),
            DMA((count,)), DMA((count,)), DMA((count,)), DMA((1,)),
            DMA((4,)), DMA((4,)),
        ],
        1, "fwd", 1, 1,
    )
    normed, raw, z, dtp, dt, cum, co, st, car, yn, gsc, stats = kept[:12]
    wc, wo, pr, seg_col, layer_out = kept[12:]
    total_rows = model + inner + 2 * state
    chunk_sems = DMA((total_rows // CHUNK,))
    table_shape = (32, model)
    grad_shape = (tokens, model + 2 * state)
    big, table, input_grad = comm(
        functools.partial(bwd_kernel, seqs, n),
        (cotangent, hidden_in, normed, wc, wo, raw, z, dtp, dt, cum, co, st, yn, gsc,
         pad, car, stats, seg_col, srow, pr),
        (((total_rows, model), TOTAL_T), (table_shape, F32), out_shape),
        [
            pltpu.VMEM((units, tokens, model), F32),
            pltpu.VMEM((units, rows, model + LANES), BF),
            pltpu.VMEM(wc.shape[1:], BF),
            pltpu.VMEM(wo.shape[1:], BF),
            pltpu.VMEM((count, rows, wide), BF),
            pltpu.VMEM((count, tokens, inner), F32),
            pltpu.VMEM((count, tokens, LANES), F32),
            pltpu.VMEM((count, tokens, LANES), F32),
            pltpu.VMEM((count, tokens, LANES), F32),
            pltpu.VMEM((count, tokens, wide), BF),
            pltpu.VMEM((count, inner, LANES), BF),
            pltpu.VMEM((count, tokens, inner), F32),
            pltpu.VMEM((count, tokens, LANES), F32),
            pltpu.VMEM((2, total_rows, model), TOTAL_T),
            pltpu.VMEM((total_rows, model), TOTAL_T),
            pltpu.VMEM((2,) + table_shape, F32),
            pltpu.VMEM(table_shape, F32),
            pltpu.VMEM(table_shape, F32),
            pltpu.VMEM(table_shape, F32),
            pltpu.VMEM((rows, wide), F32),
            pltpu.VMEM((rows + HALO, LANES), F32),
            pltpu.VMEM((tokens, wide), F32),
            pltpu.VMEM((count, rows, wide), BF),
            pltpu.VMEM((count, tokens, inner), BF),
            pltpu.VMEM((tokens, inner), BF),
            pltpu.VMEM((count, tokens, inner), BF),
            pltpu.VMEM((count, tokens, model), BF),
            pltpu.VMEM((count, tokens, LANES), BF),
            pltpu.VMEM((inner, LANES), F32),
            pltpu.VMEM(state_shape, BF),
            pltpu.VMEM((count, inner, LANES), BF),
            pltpu.VMEM((count,) + grad_shape, BF),
            pltpu.VMEM((units, HALO, model + 2 * state), BF),
            pltpu.VMEM((count, n - 1, part_rows, model + 2 * state), BF),
            pltpu.VMEM((units, n, HALO, model + 2 * state), BF),
            pltpu.VMEM((part_rows, model + 2 * state), F32),
            pltpu.VMEM((count,) + grad_shape, BF),
            pltpu.VMEM((model, 2 * state), F32),
            pltpu.VMEM((2, 8, 2 * state), F32),
            pltpu.VMEM((2, n - 1, 8, 2 * state), F32),
            pltpu.VMEM((tokens, inner), F32),
            pltpu.VMEM((units, 8, tokens), F32),
            pltpu.VMEM((units, n - 1, 8, tokens), F32),
            DMA((units, PIECES)), DMA((units, PIECES)),
            peer_sems, peer_sems, peer_sems, peer_sems,
            DMA((units,)), DMA((units, n)),
            DMA((2, n - 1)), DMA((2, n - 1)),
            DMA((count,)), DMA((count,)), DMA((count,)), DMA((3,)),
            peer_sems, peer_sems,
            DMA((9, count)), DMA((2,)),
            chunk_sems, chunk_sems, chunk_sems, chunk_sems, chunk_sems, chunk_sems,
            DMA((3,)), DMA((3,)),
        ],
        2, "bwd", 1, 14,
    )
    (g_zx, g_wo, g_bc, rms, g_norm, g_dt, g_cx, g_cxb, g_cb, g_cbb, g_dtb, g_al, g_sk,
     g_gate) = finalize(big, table, inner, heads, state)
    return (layer_out[None], input_grad[None], rms, g_norm, g_zx, g_bc,
            jnp.transpose(g_dt, (0, 2, 1)), g_cx, g_cxb,
            g_cb, g_cbb, g_dtb, g_al, g_sk, g_gate, g_wo)


def solution(mesh):
    in_specs = (
        P(None, SEQ, None),
        P(None, SEQ, None),
        P(None, SEQ),
        P(None, SEQ),
        P(SEC, None),
        P(SEC, None, None, HEAD),
        P(SEC, None, None),
        P(SEC, None, HEAD),
        P(SEC, None, HEAD),
        P(SEC, HEAD),
        P(SEC, None, None),
        P(SEC, None),
        P(SEC, HEAD),
        P(SEC, HEAD),
        P(SEC, HEAD),
        P(SEC, HEAD),
        P(SEC, HEAD, None),
    )
    out_specs = (
        P(SEC, None, SEQ, None),
        P(SEC, None, SEQ, None),
        P(SEC, None),
        P(SEC, None),
        P(SEC, None, None, HEAD),
        P(SEC, None, None),
        P(SEC, None, HEAD),
        P(SEC, None, HEAD),
        P(SEC, HEAD),
        P(SEC, None, None),
        P(SEC, None),
        P(SEC, HEAD),
        P(SEC, HEAD),
        P(SEC, HEAD),
        P(SEC, HEAD),
        P(SEC, HEAD, None),
    )
    return jax.shard_map(local, mesh=mesh, in_specs=in_specs, out_specs=out_specs, check_vma=False)
```

```python
import functools

import jax
import jax.numpy as jnp
from jax import lax
from jax.experimental import pallas as pl
from jax.experimental.pallas import tpu as pltpu
from jax.sharding import PartitionSpec as P

SEC, SEQ, HEAD = "section", "seq", "head"
F32, BF = jnp.float32, jnp.bfloat16
MESH = pl.DeviceIdType.MESH
HIGH = lax.Precision.HIGHEST
EPS = 1e-05
KC = 4
HALO = 16
LANES = 128
HEAD_SHIFT = 6
LIMIT = 58 << 20
CHUNK = 64
SKEW = 3
LEAD = 2
TICKS = 10
TAIL_TICKS = 4
PIECES = 4
TOTAL_T = jnp.bfloat16


def mm(a, b, precision=None):
    return lax.dot_general(
        a, b, (((1,), (0,)), ((), ())), precision=precision, preferred_element_type=F32
    )


def mm_nt(a, b):
    return lax.dot_general(a, b, (((1,), (1,)), ((), ())), preferred_element_type=F32)


def mm_tn(a, b, precision=None):
    return lax.dot_general(
        a, b, (((0,), (0,)), ((), ())), precision=precision, preferred_element_type=F32
    )


def iota(shape, dim):
    return lax.broadcasted_iota(jnp.int32, shape, dim)


def spread_matrix(width):
    shape = (LANES, width)
    return (iota(shape, 0) == jnp.right_shift(iota(shape, 1), HEAD_SHIFT)).astype(BF)


def split(x):
    high = x.astype(BF)
    return high, (x - high.astype(F32)).astype(BF)


def expand(x, matrix):
    high, low = split(x)
    return mm(high, matrix) + mm(low, matrix)


def head_sums(x, matrix):
    high, low = split(x)
    return mm_nt(high, matrix) + mm_nt(low, matrix)


def fine(product, a, b):
    high, low = split(a)
    return product(high, b) + product(low, b)


def two_lanes(column):
    high = column.astype(BF).astype(F32)
    lane = iota((column.shape[0], LANES), 1)
    return jnp.where(lane == 0, high, jnp.where(lane == 1, column - high, 0.0)).astype(BF)


def sigmoid(v):
    return 1.0 / (1.0 + jnp.exp(-v))


def lower(size):
    return (iota((size, size), 0) >= iota((size, size), 1)).astype(F32)


def same_rows(seg_ref, mb, tokens):
    mine = seg_ref[mb, HALO:]
    first = HALO - KC + 1
    return [
        (seg_ref[mb, first + k : first + k + tokens] == mine).astype(F32) for k in range(KC)
    ]


def convolved(raw_f, same, prm, col, tokens):
    first = HALO - KC + 1
    cols = slice(col, col + LANES)
    pre = jnp.zeros((tokens, LANES), F32) + prm[5:6, cols]
    for k in range(KC):
        pre = pre + prm[1 + k : 2 + k, cols] * raw_f[first + k : first + k + tokens, cols] * same[k]
    return pre


def gains(cum, seg_ref, mb):
    mine = seg_ref[mb, HALO:]
    before = seg_ref[mb, HALO - 1 : HALO]
    last = mine[-1:]
    entry = jnp.exp(cum) * (mine == before).astype(F32)
    decay_end = jnp.exp(cum[-1:] - cum) * (mine == last).astype(F32)
    return entry, decay_end


def place():
    return lax.axis_index(SEC), lax.axis_index(SEQ), lax.axis_index(HEAD)


def remote(src, dst, send, recv, device):
    return pltpu.make_async_remote_copy(
        src_ref=src, dst_ref=dst, send_sem=send, recv_sem=recv, device_id=device,
        device_id_type=MESH,
    )


def greet(device):
    pl.semaphore_signal(
        pltpu.get_barrier_semaphore(), inc=1, device_id=device, device_id_type=MESH
    )


def await_greets(count):
    pl.semaphore_wait(pltpu.get_barrier_semaphore(), count)


def one_if(condition):
    return condition.astype(jnp.int32)


def comm(kernel, ins, outs, scratch, ident, name, in_hbm=0, from_hbm=0):
    sources = [pl.ANY] * from_hbm + [pltpu.VMEM] * (len(ins) - from_hbm)
    spaces = [pltpu.VMEM] * (len(outs) - in_hbm) + [pl.ANY] * in_hbm
    return pl.pallas_call(
        kernel,
        in_specs=[pl.BlockSpec(memory_space=space) for space in sources],
        out_specs=[pl.BlockSpec(memory_space=space) for space in spaces],
        out_shape=[jax.ShapeDtypeStruct(s, d) for s, d in outs],
        scratch_shapes=scratch,
        compiler_params=pltpu.CompilerParams(
            collective_id=ident, has_side_effects=True, vmem_limit_bytes=LIMIT
        ),
        name=name,
    )(*ins)


DMA = pltpu.SemaphoreType.DMA


def wide_copy(x, width):
    return jnp.concatenate([x] * (width // LANES), axis=1)


def causal_mask(seg_ref, srow_ref, mb, tokens, transposed):
    row = iota((tokens, tokens), 0)
    col = iota((tokens, tokens), 1)
    same = wide_copy(seg_ref[mb, HALO:], tokens) == srow_ref[mb, 0:1]
    return same & ((row <= col) if transposed else (row >= col))


def when(condition):
    return pl.when(condition)


def both(a, b):
    return jnp.logical_and(a, b)


def fwd_kernel(seqs, n, source, segments, padding, norm_gain, conv_x, conv_xb, conv_bc, conv_bcb,
               dt_bias, a_log, skip_d, gate_gain, wc_in, wo_in,
               car, pr, seg, srow, pad, normed_o, raw_o, z_o, dtp_o, dt_o, cum_o, co_o, st_o,
               yn_o, gsc_o, part_o, wc_o, wo_o,
               normed, raw, z, dtp, dt, cum, co, st, yn, gsc, part, wc, wo,
               halo, seg_halo, pr_in, hid, raw_f, con, sbuf, gated_s, part0, rbuf0, ssend, srecv,
               c_s, c_r, q_s, q_r, s_s, s_r, g_s, g_r, h_s, h_r, in_s, w_s, w_r, o_s, v_s):
    s, q, h = place()
    count, tokens, model = hid.shape
    inner = wo.shape[1]
    wide = raw.shape[2]
    heads = inner >> HEAD_SHIFT
    rows = tokens // n
    units = 2 * count
    full = inner * n
    piece = inner // PIECES
    other = (1 - s, q, h)
    first_q, last_q = q == 0, q == seqs - 1
    edge_owner = both(h == n - 1, q < seqs - 1)
    peers = [lax.rem(h + j, n) for j in range(1, n)]
    froms = [lax.rem(h + n - j, n) for j in range(1, n)]
    matrix = spread_matrix(inner)
    load = pltpu.make_async_copy(source.at[pl.ds(s * count, count)], hid, in_s.at[0])
    load.start()
    for p in peers:
        greet((s, q, p))
    greet(other)

    @when(q > 0)
    def _():
        greet((s, q - 1, n - 1))

    @when(both(q > 0, h < n - 1))
    def _():
        greet((s, q - 1, h))

    await_greets(n + one_if(q < seqs - 1) * (1 + (n - 1) * one_if(h == n - 1)))

    def at_rows(owner):
        return pl.ds(pl.multiple_of(owner * rows, rows), rows)

    def slot_rows(owner):
        return pl.ds(pl.multiple_of(HALO + owner * rows, HALO), rows)

    def chain(u, k):
        cut = pl.ds(k * piece, piece)
        return remote(
            sbuf.at[u, cut], st.at[u, cut], c_s.at[u, k], c_r.at[u, k], (s, q + 1, h)
        )

    def squares(u, j):
        return remote(
            ssend.at[u], srecv.at[u, j], q_s.at[u, j], q_r.at[u, j], (s, q, peers[j])
        )

    def scatter(u, j):
        return remote(
            part0.at[u, at_rows(peers[j])], rbuf0.at[u, j], s_s.at[u, j], s_r.at[u, j],
            (s, q, peers[j]),
        )

    def gather(u, j, owner):
        where = (u + count, slot_rows(owner))
        return remote(
            normed.at[where], normed.at[where], g_s.at[u, j], g_r.at[u, j], (s, q, peers[j])
        )

    def edge(u, head):
        return remote(
            normed.at[u + count, pl.ds(tokens, HALO)], normed.at[u + count, pl.ds(0, HALO)],
            h_s.at[u, head], h_r.at[u], (s, q + 1, head),
        )

    keeps = (
        (raw, raw_o), (z, z_o), (dtp, dtp_o), (dt, dt_o), (cum, cum_o), (co, co_o), (st, st_o),
        (yn, yn_o), (gsc, gsc_o),
    )

    def keep(u):
        return [
            pltpu.make_async_copy(a.at[u], b.at[u], o_s.at[i, u]) for i, (a, b) in enumerate(keeps)
        ]

    def keep_normed(u):
        return pltpu.make_async_copy(normed.at[u], normed_o.at[u], o_s.at[len(keeps), u])

    def keep_part(mb):
        return pltpu.make_async_copy(
            part.at[mb], part_o.at[mb], o_s.at[len(keeps) + 1, mb]
        )

    def keep_weight(i, layer):
        a, b = ((wc, wc_o), (wo, wo_o))[i]
        return pltpu.make_async_copy(a.at[layer], b.at[layer], v_s.at[i, layer])

    def pass_state(u):
        for k in range(PIECES):
            @when(q > 0)
            def _():
                chain(u, k).wait_recv()

            @when(first_q)
            def _():
                st[u, k * piece : (k + 1) * piece] = jnp.zeros((piece, LANES), BF)

            @when(q < seqs - 1)
            def _():
                per = inner // heads
                for i in range(k * heads // PIECES, (k + 1) * heads // PIECES):
                    cut = slice(i * per, (i + 1) * per)
                    sbuf[u, cut] = (
                        car[u, i : i + 1] * st[u, cut].astype(F32) + con[cut]
                    ).astype(BF)
                chain(u, k).start()

    def weight(i, layer):
        src, dst = ((pr_in, pr), (wc_in, wc), (wo_in, wo))[i]
        return remote(src, dst.at[layer], w_s.at[i], w_r.at[i], other)

    weight(1, s).start()
    weight(2, s).start()
    halo_copy = remote(
        hid.at[:, pl.ds(tokens - HALO, HALO)], halo, w_s.at[3], w_r.at[3], (s, q + 1, h)
    )
    seg_copy = remote(
        seg.at[:, pl.ds(tokens, HALO)], seg_halo, w_s.at[4], w_r.at[4], (s, q + 1, h)
    )
    deep = conv_bc.shape[2]
    pr_in[...] = jnp.zeros_like(pr_in)
    pr_in[0:1] = norm_gain[...]
    pr_in[1:5, :inner] = conv_x[0]
    pr_in[1:5, inner : inner + deep] = conv_bc[0]
    pr_in[5:6, :inner] = conv_xb[...]
    pr_in[5:6, inner : inner + deep] = conv_bcb[...]
    pr_in[6:7, :heads] = dt_bias[...]
    pr_in[7:8, :heads] = -jnp.exp(a_log[...])
    pr_in[9:10, :inner] = gate_gain[...]
    skips = jnp.broadcast_to(
        jnp.concatenate([skip_d[...], jnp.zeros((1, LANES - heads), F32)], axis=1), (8, LANES)
    )
    pr_in[8:9, :inner] = mm(skips, matrix.astype(F32), HIGH)[:1]
    weight(0, s).start()
    batches = segments.shape[0]
    for mb in range(count):
        for given, rows_o in ((segments, srow), (padding, None)):
            row = jnp.zeros((1, tokens), F32)
            for b in range(batches):
                row = jnp.where(b == s * count + mb, given[b : b + 1].astype(F32), row)
            row = jnp.broadcast_to(row, (8, tokens))
            column = mm_tn(row * 0.125, jnp.ones((8, LANES), F32), HIGH)
            if rows_o is None:
                pad[mb] = column
            else:
                rows_o[mb] = row
                seg[mb, HALO:] = column
    load.wait()

    @when(q < seqs - 1)
    def _():
        halo_copy.start()
        seg_copy.start()

    pr[s] = pr_in[...]
    wc[s] = wc_in[...]
    wo[s] = wo_in[...]
    keep_weight(0, s).start()
    keep_weight(1, s).start()

    @when(q > 0)
    def _():
        halo_copy.wait_recv()
        seg_copy.wait_recv()
        seg[:, :HALO] = seg_halo[...]

    @when(first_q)
    def _():
        halo[...] = jnp.zeros_like(halo)
        seg[:, :HALO] = jnp.full((count, HALO, LANES), -1.0, F32)

    weight(0, 1 - s).wait_recv()

    def needs_weights(u):
        return u == count * (1 - s)

    def in_norm(mb, _):
        hx = jnp.concatenate([halo[mb], hid[mb]], axis=0)
        scale = lax.rsqrt(jnp.mean(hx * hx, axis=1, keepdims=True) + EPS)
        normed[mb, :, :model] = (hx * scale * pr[0, 0:1]).astype(BF)
        normed[mb, :, model:] = two_lanes(scale)
        keep_normed(mb).start()

        @when(first_q)
        def _():
            normed[mb + count, :HALO] = jnp.zeros((HALO, model + LANES), BF)

        return 0

    lax.fori_loop(0, count, in_norm, 0)

    def local_part(u):
        layer = u // count
        mb = lax.rem(u, count)
        prm = pr[layer]
        x = normed[u, :, :model]
        new_raw = mm(x, wc[layer, :, inner : inner + wide]).astype(BF)
        raw[u] = new_raw
        raw_f[...] = new_raw.astype(F32)
        x = x[HALO:]
        z[u] = mm(x, wc[layer, :, :inner])
        new_dtp = mm(x, wc[layer, :, inner + wide :]) + prm[6:7, :LANES]
        dtp[u] = new_dtp
        new_dt = jax.nn.softplus(new_dtp)
        dt[u] = new_dt
        new_cum = mm(lower(tokens), new_dt * prm[7:8, :LANES], HIGH)
        cum[u] = new_cum
        cum_t = new_cum.T
        dt_t = new_dt.T
        same = same_rows(seg, mb, tokens)
        pieces = []
        for col in range(0, wide, LANES):
            pre = convolved(raw_f, same, prm, col, tokens)
            piece = (pre * sigmoid(pre)).astype(BF)
            co[u, :, col : col + LANES] = piece
            pieces.append(piece)
        values = jnp.concatenate(pieces[: inner // LANES], axis=1)
        in_b, in_c = pieces[-2], pieces[-1]
        entry, decay_end = gains(new_cum, seg, mb)
        toward = expand(decay_end * new_dt, matrix)
        con[...] = fine(mm_tn, values.astype(F32) * toward, in_b)
        mine = seg[mb, HALO:]
        same_before = (mine[-1:, :] == seg[mb, HALO - 1 : HALO]).astype(F32)
        car[u] = jnp.exp(cum_t[:heads, tokens - 1 :]) * same_before

        @when(first_q)
        def _():
            pass_state(u)

        inner_cb = jnp.where(
            causal_mask(seg, srow, mb, tokens, False), mm_nt(in_c, in_b), 0.0
        )
        lane = iota((tokens, LANES), 1)
        for pair in range(heads // 2):
            cols = slice(pair * LANES, (pair + 1) * LANES)
            acc = jnp.zeros((tokens, LANES), F32)
            for j in range(2):
                one = slice(2 * pair + j, 2 * pair + j + 1)
                decay = jnp.exp(jnp.minimum(new_cum[:, one] - cum_t[one, :], 0.0))
                mask = jnp.right_shift(lane, HEAD_SHIFT) == j
                value = jnp.where(mask, values[:, cols], jnp.zeros((), BF))
                acc = acc + mm((inner_cb * decay * dt_t[one, :]).astype(BF), value)
            yn[u, :, cols] = acc

    def gate_part(u):
        layer = u // count
        mb = lax.rem(u, count)
        entry, _ = gains(cum[u], seg, mb)
        in_c = co[u, :, inner + LANES :]
        readout = mm_nt(in_c, st[u])
        y = yn[u] + expand(entry, matrix) * readout
        yn[u] = y
        ssd = y + pr[layer, 8:9, :inner] * co[u, :, :inner].astype(F32)
        gate = z[u]
        gated = ssd * (gate * sigmoid(gate))
        gated_s[...] = gated
        ones = jnp.ones((8, inner), BF)
        ssend[u] = fine(lambda a, b: mm_nt(b, a), gated * gated, ones)

    def out_part(u):
        layer = u // count
        total = ssend[u]
        for j in range(n - 1):
            squares(u, j).wait_recv()
            total = total + srecv[u, j]
        scale_row = lax.rsqrt(total / full + EPS)
        scale = mm_tn(scale_row * 0.125, jnp.ones((8, LANES), F32), HIGH)
        gsc[u] = scale
        x = (gated_s[...] * wide_copy(scale, inner) * pr[layer, 9:10, :inner]).astype(BF)
        product = mm(x, wo[layer])

        @when(u < count)
        def _():
            part0[u] = product.astype(BF)
            for j in range(n - 1):
                scatter(u, j).start()

        @when(u >= count)
        def _():
            part[u - count] = product.astype(BF)
            keep_part(u - count).start()

    def finish(u):
        total = part0[u, at_rows(h)].astype(F32)
        for j in range(n - 1):
            scatter(u, j).wait_recv()
            total = total + rbuf0[u, j].astype(F32)
        h_new = hid[u, at_rows(h)] + total
        scale = lax.rsqrt(jnp.mean(h_new * h_new, axis=1, keepdims=True) + EPS)
        normed[u + count, slot_rows(h), :model] = (h_new * scale * pr[1, 0:1]).astype(BF)
        normed[u + count, slot_rows(h), model:] = two_lanes(scale)
        for j in range(n - 1):
            gather(u, j, h).start()

        @when(edge_owner)
        def _():
            for head in range(n):
                edge(u, head).start()

    def arrived(u):
        for j in range(n - 1):
            gather(u, j, froms[j]).wait_recv()

    def step(u, _):
        @when(both(u >= count, u < units))
        def _():
            mb = u - count
            arrived(mb)

            @when(q > 0)
            def _():
                edge(mb, 0).wait_recv()

            keep_normed(u).start()

        @when(u == count)
        def _():
            finish(u - 1)

        @when(needs_weights(u))
        def _():
            weight(1, 1 - s).wait_recv()
            keep_weight(0, 1 - s).start()

        @when(u < units)
        def _():
            local_part(u)

            @when(q > 0)
            def _():
                pass_state(u)

            gate_part(u)
            for j in range(n - 1):
                squares(u, j).start()

        @when(both(u > 0, u < count))
        def _():
            finish(u - 1)

        @when(needs_weights(u))
        def _():
            weight(2, 1 - s).wait_recv()
            keep_weight(1, 1 - s).start()

        @when(u < units)
        def _():
            out_part(u)
            for copy in keep(u):
                copy.start()

        return 0

    lax.fori_loop(0, units, step, 0)

    def drain(u, _):
        for j in range(n - 1):
            squares(u, j).wait_send()

        @when(q < seqs - 1)
        def _():
            for k in range(PIECES):
                chain(u, k).wait_send()

        @when(u < count)
        def _():
            for j in range(n - 1):
                scatter(u, j).wait_send()
                gather(u, j, h).wait_send()
            keep_part(u).wait()

        @when(both(u < count, edge_owner))
        def _():
            for head in range(n):
                edge(u, head).wait_send()

        for copy in keep(u):
            copy.wait()
        keep_normed(u).wait()
        return 0

    lax.fori_loop(0, units, drain, 0)
    for i in range(3):
        weight(i, s).wait_send()
    for i in range(2):
        for layer in range(2):
            keep_weight(i, layer).wait()

    @when(q < seqs - 1)
    def _():
        halo_copy.wait_send()
        seg_copy.wait_send()


def bwd_kernel(seqs, n, cot, hid, kept, wc_in, wo_in, raw_in, z_in, dtp_in, dt_in, cum_in,
               co_in, st_in, yn_in, gsc_in, part_in, pad, car, seg, srow, pr,
               out, small_o, ig, lo,
               gin, lo_s, normed, wc, wo, raw, z, dtp, dt, cum, co, st, yn, gsc,
               big, pbuf, table, ps, rs_, ts,
               raw_f, shift, gconv, gext, gz, gy_s, ng, gdr, back, nxt, sbuf,
               part, hpart, rbuf, hbuf, acc, ag, gwb, small, srecv, ggn, dsend, drecv,
               c_s, c_r, s_s, s_r, g_s, g_r, h_s, h_r, m_s, m_r, l_c, l_s, l_r, in_s,
               d_s, d_r, f_s, w_s, x_s, x_r, a_s, a_r, b_s, b_r, t_s, t_r,
               k_c, k_s, k_r, e_s, e_r, p_s):
    s, q, h = place()
    count, tokens, model = gin.shape[0] // 2, gin.shape[1], gin.shape[2]
    inner = wo.shape[0]
    state = LANES
    wide = raw.shape[2]
    heads = inner >> HEAD_SHIFT
    rows = tokens // n
    ext = tokens + HALO
    steps = 2 * count
    full = inner * n
    piece = inner // PIECES
    other = (1 - s, q, h)
    edge_owner = both(h == n - 1, q < seqs - 1)
    peers = [lax.rem(h + j, n) for j in range(1, n)]
    froms = [lax.rem(h + n - j, n) for j in range(1, n)]
    matrix = spread_matrix(inner)
    sources = (raw_in, z_in, dtp_in, dt_in, cum_in, co_in, st_in, yn_in, gsc_in)
    targets = (raw, z, dtp, dt, cum, co, st, yn, gsc)

    def unit(w):
        return (1 - w // count) * count + lax.rem(w, count)

    def stream(w):
        k = lax.rem(w, count)
        return [
            pltpu.make_async_copy(a.at[unit(w)], b.at[k], f_s.at[i, k])
            for i, (a, b) in enumerate(zip(sources, targets))
        ]

    def wc_load(layer):
        return pltpu.make_async_copy(wc_in.at[layer], wc, w_s.at[0])

    def wo_load(layer):
        return pltpu.make_async_copy(wo_in.at[layer], wo, w_s.at[1])

    loads = [
        pltpu.make_async_copy(cot.at[pl.ds(s * count, count)], gin.at[pl.ds(0, count)], in_s.at[0]),
        pltpu.make_async_copy(
            hid.at[pl.ds(s * count, count)], gin.at[pl.ds(count, count)], in_s.at[1]
        ),
        pltpu.make_async_copy(kept.at[pl.ds(0, steps)], normed, in_s.at[2]),
    ]
    wo_load(1).start()
    for load in loads:
        load.start()
    for load in stream(0):
        load.start()
    wc_load(1).start()
    for p in peers:
        greet((s, q, p))
    greet(other)

    @when(q < seqs - 1)
    def _():
        greet((s, q + 1, h))

    @when(edge_owner)
    def _():
        for head in range(n - 1):
            greet((s, q + 1, head))

    @when(q > 0)
    def _():
        greet((s, q - 1, h))

    await_greets(
        n + one_if(q > 0) * (1 + one_if(h < n - 1)) + one_if(q < seqs - 1)
    )

    def at_rows(owner):
        return pl.ds(pl.multiple_of(owner * rows, rows), rows)

    def slot(w):
        return lax.rem(w, count)

    def chain(w, k):
        cut = pl.ds(k * piece, piece)
        return remote(
            sbuf.at[slot(w), cut], nxt.at[w, cut], c_s.at[w, k], c_r.at[w, k], (s, q - 1, h)
        )

    def scatter(w, j):
        return remote(
            part.at[slot(w), at_rows(peers[j])], rbuf.at[slot(w), j], s_s.at[w, j],
            s_r.at[w, j], (s, q, peers[j]),
        )

    def gather(w, j, owner):
        where = (slot(w), at_rows(owner))
        return remote(
            ag.at[where], ag.at[where], g_s.at[w, j], g_r.at[w, j], (s, q, peers[j])
        )

    def edge(w, head):
        return remote(
            hpart.at[w], hbuf.at[w, head], h_s.at[w], h_r.at[w, head], (s, q - 1, n - 1)
        )

    def little(layer, j):
        return remote(
            small.at[layer], srecv.at[layer, j], m_s.at[layer, j], m_r.at[layer, j],
            (s, q, peers[j]),
        )

    def ship_local(v):
        mb = lax.rem(v, count)
        return pltpu.make_async_copy(gin.at[v], ig.at[s * count + mb], l_c.at[mb])

    def ship(v):
        mb = lax.rem(v, count)
        return remote(gin.at[v], ig.at[s * count + mb], l_s.at[mb], l_r.at[mb], other)

    def out_local(mb):
        return pltpu.make_async_copy(lo_s.at[mb], lo.at[s * count + mb], k_c.at[mb])

    def out_ship(mb):
        return remote(lo_s.at[mb], lo.at[s * count + mb], k_s.at[mb], k_r.at[mb], other)

    def send_layer(layer, mb, h_new, branch):
        lo_s[mb] = h_new
        live = pad[mb]
        for i, x in enumerate((h_new, branch)):
            table[layer, 24 + i : 25 + i, :LANES] += jnp.sum(
                jnp.sum(x * x, axis=1, keepdims=True) * live, axis=0, keepdims=True
            )
        table[layer, 26:27, :LANES] += jnp.sum(live, axis=0, keepdims=True)

        @when(s == layer)
        def _():
            out_local(mb).start()

        @when(s != layer)
        def _():
            out_ship(mb).start()

    def norm_part(v):
        layer = 1 - v // count
        mb = lax.rem(v, count)
        u = layer * count + mb
        for j in range(n - 1):
            gather(v, j, froms[j]).wait_recv()
        gn = ag[mb, :, :model].astype(F32)
        scale = jnp.sum(normed[u, HALO:, model:].astype(F32), axis=1, keepdims=True)
        gain = pr[layer, 0:1]

        def rest(h_in, grad_out):
            x = gn * gain
            dots = jnp.sum(x * h_in, axis=1, keepdims=True)
            gin[v] = grad_out + x * scale - h_in * (scale * scale * scale * dots / model)
            table[layer, 0:1] += jnp.sum(gn * h_in * scale, axis=0, keepdims=True)

        @when(layer == 1)
        def _():
            h_in = normed[u, HALO:, :model].astype(F32) / (scale * gain)
            rest(h_in, gin[mb] * wide_copy(pad[mb], model))
            send_layer(0, mb, h_in, h_in - gin[mb + count])

        @when(layer == 0)
        def _():
            rest(gin[v], gin[mb])

        @when(s == layer)
        def _():
            ship_local(v).start()

        @when(s != layer)
        def _():
            ship(v).start()

        grad_w = mm_tn(normed[u, HALO:, :model], ag[mb, :, model:])

        @when(mb == 0)
        def _():
            gwb[...] = grad_w

        @when(mb > 0)
        def _():
            gwb[...] += grad_w

        @when(mb == count - 1)
        def _():
            base = model + inner
            deep = 2 * state
            for k in range(model // deep):
                cut = slice(k * deep, (k + 1) * deep)
                big[layer, base : base + deep, cut] = gwb[cut].astype(TOTAL_T)

            @when(s == 0)
            def _():
                start_cross(layer, (model + inner) // CHUNK - chunks, chunks)

    def dots(w, j):
        return remote(
            dsend.at[w], drecv.at[w, j], d_s.at[w, j], d_r.at[w, j], (s, q, peers[j])
        )

    def gate_forward(mb, layer):
        gate = z[mb]
        sig = sigmoid(gate)
        silu = gate * sig
        ssd = yn[mb] + pr[layer, 8:9, :inner] * co[mb, :, :inner].astype(F32)
        return gate, sig, silu, ssd, ssd * silu

    def out_b(layer, mb):
        live = jnp.where(layer == 1, pad[mb], jnp.ones((tokens, LANES), F32))
        return (gin[mb] * wide_copy(live, model)).astype(BF)

    def gate_first(w):
        layer = 1 - w // count
        mb = lax.rem(w, count)
        u = layer * count + mb

        grad_gn = mm_nt(out_b(layer, mb), wo[...])
        ggn[...] = grad_gn
        gated = gate_forward(mb, layer)[-1]
        ones = jnp.ones((8, inner), BF)
        dsend[w] = fine(
            lambda a, b: mm_nt(b, a), grad_gn * gated * pr[layer, 9:10, :inner], ones
        )
        for j in range(n - 1):
            dots(w, j).start()

    def conv_slope(w):
        mb = lax.rem(w, count)
        raw_f[...] = raw[mb].astype(F32)
        same = same_rows(seg, mb, tokens)
        prm = pr[1 - w // count]
        for col in range(0, wide, LANES):
            pre = convolved(raw_f, same, prm, col, tokens)
            sig = sigmoid(pre)
            gconv[:, col : col + LANES] = sig * (1.0 + pre * (1.0 - sig))

    def gate_part(w):
        layer = 1 - w // count
        mb = lax.rem(w, count)
        u = layer * count + mb
        total = dsend[w]
        for j in range(n - 1):
            dots(w, j).wait_recv()
            total = total + drecv[w, j]
        across = mm_tn(total * 0.125, jnp.ones((8, LANES), F32), HIGH)
        scale = gsc[mb]
        scale_x = wide_copy(scale, inner)
        gate, sig, silu, ssd, gated = gate_forward(mb, layer)
        grad_gn = ggn[...]
        values = co[mb, :, :inner].astype(F32)
        gain = pr[layer, 9:10, :inner]
        scaled = gated * scale_x
        grad_gated = grad_gn * (gain * scale_x) - scaled * wide_copy(
            scale * scale * across / full, inner
        )
        gy = (grad_gated * silu).astype(BF)
        gy_s[...] = gy
        gz[mb] = (grad_gated * ssd * (sig * (1.0 + gate * (1.0 - sig)))).astype(BF)
        ng[mb] = (scaled * gain).astype(BF)
        gy_f = gy.astype(F32)
        table[layer, 8:9, :inner] += jnp.sum(grad_gn * scaled, axis=0, keepdims=True)
        table[layer, 9:10, :inner] += jnp.sum(gy_f * values, axis=0, keepdims=True)
        entry, _ = gains(cum[mb], seg, mb)
        read = expand(entry, matrix) * gy_f
        back[...] = fine(mm_tn, read, co[mb, :, inner + state :])

        @when(q == seqs - 1)
        def _():
            pass_state(w, u)

    def pass_state(w, u):
        per = inner // heads
        for k in range(PIECES):
            @when(q < seqs - 1)
            def _():
                chain(w, k).wait_recv()

            @when(q == seqs - 1)
            def _():
                nxt[w, k * piece : (k + 1) * piece] = jnp.zeros((piece, LANES), BF)

            @when(q > 0)
            def _():
                @when(w >= count)
                def _():
                    chain(w - count, k).wait_send()

                for i in range(k * heads // PIECES, (k + 1) * heads // PIECES):
                    cut = slice(i * per, (i + 1) * per)
                    sbuf[slot(w), cut] = (
                        car[u, i : i + 1] * nxt[w, cut].astype(F32) + back[cut]
                    ).astype(BF)
                chain(w, k).start()

    def local_part(w):
        layer = 1 - w // count
        mb = lax.rem(w, count)
        u = layer * count + mb
        prm = pr[layer]
        cum_u, dt_u = cum[mb], dt[mb]
        cum_t = cum_u.T
        entry, decay_end = gains(cum_u, seg, mb)
        values = co[mb, :, :inner]
        in_b = co[mb, :, inner : inner + state]
        in_c = co[mb, :, inner + state :]
        gy = gy_s[...]
        gy_f = gy.astype(F32)
        causal = causal_mask(seg, srow, mb, tokens, True)
        inner_bc = jnp.where(causal, mm_nt(in_b, in_c), 0.0)
        grad_inner = jnp.zeros((tokens, tokens), F32)
        lane = iota((tokens, LANES), 1)
        grad_dt = jnp.zeros((tokens, LANES), F32)
        locals_, rows_ = [], []
        for pair in range(heads // 2):
            cols = slice(pair * LANES, (pair + 1) * LANES)
            total = jnp.zeros((tokens, LANES), F32)
            for j in range(2):
                head = 2 * pair + j
                one = slice(head, head + 1)
                dt_col = dt_u[:, one]
                decay = jnp.exp(jnp.minimum(cum_t[one, :] - cum_u[:, one], 0.0))
                mask = jnp.right_shift(lane, HEAD_SHIFT) == j
                gy_one = jnp.where(mask, gy[:, cols], jnp.zeros((), BF))
                grad_mix = mm_nt(values[:, cols], gy_one)
                mixed = inner_bc * decay
                total = total + mm((mixed * dt_col).astype(BF), gy_one)
                grad_inner = grad_inner + grad_mix * (decay * dt_col)
                weighted = grad_mix * mixed
                sums = jnp.sum(weighted, axis=1, keepdims=True)
                grad_dt = jnp.where(lane == head, sums, grad_dt)
                rows_.append(jnp.sum(weighted * dt_col, axis=0, keepdims=True))
            locals_.append(total)
            tick(w, 3 + pair, 1)

        @when(w > 0)
        def _():
            finish(w - 1)

        tick(w, 7, 1)

        @when(q < seqs - 1)
        def _():
            pass_state(w, u)

        grad_inner = jnp.where(causal, grad_inner, 0.0)
        toward = decay_end * dt_u
        toward_x = expand(toward, matrix)
        values_f = values.astype(F32)
        pulled = mm_nt(in_b, nxt[w])
        gconv[:, :inner] *= (
            prm[8:9, :inner] * gy_f + jnp.concatenate(locals_, axis=1) + toward_x * pulled
        )
        read = expand(entry, matrix) * gy_f
        from_row = (iota((heads, LANES), 0) == iota((heads, LANES), 1)).astype(F32)
        grad_cum = (
            mm_tn(jnp.concatenate(rows_, axis=0), from_row, HIGH)
            - dt_u * grad_dt
            + head_sums(read * mm_nt(in_c, st[mb]), matrix)
        )
        pulled_sums = head_sums(values_f * pulled, matrix)
        grad_dt = grad_dt + pulled_sums * decay_end
        high, low = split(nxt[w].astype(F32) * st[mb].astype(F32))
        carried = jnp.sum(
            lax.dot_general(high, matrix, (((0,), (1,)), ((), ())), preferred_element_type=F32)
            + lax.dot_general(low, matrix, (((0,), (1,)), ((), ())), preferred_element_type=F32),
            axis=0,
            keepdims=True,
        )
        ahead = (iota((tokens, tokens), 0) > iota((tokens, tokens), 1)).astype(F32)
        grad_rate = (
            mm_tn(lower(tokens), grad_cum, HIGH)
            + mm(ahead, pulled_sums * toward, HIGH)
            + carried * entry[-1:]
        )
        neg = prm[7:8, :LANES]
        grad_pre = (grad_dt + grad_rate * neg) * sigmoid(dtp[mb])
        table[layer, 6:7, :LANES] += jnp.sum(grad_pre, axis=0, keepdims=True)
        table[layer, 7:8, :LANES] += jnp.sum(grad_rate * dt_u * neg, axis=0, keepdims=True)
        grad_raw_dt = grad_pre.astype(BF)
        gdr[mb] = grad_raw_dt
        gconv[:, inner : inner + state] *= fine(mm, grad_inner, in_c) + fine(
            mm, values_f * toward_x, nxt[w]
        )
        gconv[:, inner + state :] *= fine(mm_tn, grad_inner, in_b) + fine(mm, read, st[mb])
        same = same_rows(seg, mb, tokens)
        first = HALO - KC + 1
        shift[:HALO] = jnp.zeros((HALO, LANES), F32)
        shift[ext:] = jnp.zeros((HALO, LANES), F32)
        for col in range(0, wide, LANES):
            cols = slice(col, col + LANES)
            grad = gconv[:, cols]
            target = table if col < inner else small
            off = col if col < inner else col - inner
            tc = slice(off, off + LANES)
            target[layer, 5:6, tc] += jnp.sum(grad, axis=0, keepdims=True)
            total = jnp.zeros((ext, LANES), F32)
            for k in range(KC):
                masked = grad * same[k]
                target[layer, 1 + k : 2 + k, tc] += jnp.sum(
                    masked * raw_f[first + k : first + k + tokens, cols], axis=0, keepdims=True
                )
                shift[HALO:ext] = masked * prm[1 + k : 2 + k, cols]
                total = total + shift[KC - 1 - k : KC - 1 - k + ext]
            gext[mb, :, cols] = total.astype(BF)
            if col == wide // 2:
                tick(w, 8, 1)
        grad_raw = gext[mb]
        main = mm_nt(gz[mb], wc[:, :inner]) + mm_nt(
            grad_raw_dt, wc[:, inner + wide :]
        )
        rest = mm_nt(grad_raw, wc[:, inner : inner + wide])
        part[mb, :, :model] = (main + rest[HALO:]).astype(BF)
        hpart[w, :, :model] = rest[:HALO].astype(BF)
        part[mb, :, model:] = grad_raw[HALO:, inner:]
        hpart[w, :, model:] = grad_raw[:HALO, inner:]

    def finish(w):
        acc[...] = part[slot(w), at_rows(h)].astype(F32)
        for j in range(n - 1):
            scatter(w, j).wait_recv()
            acc[...] += rbuf[slot(w), j].astype(F32)

        @when(both(edge_owner, w < steps))
        def _():
            for head in range(n):
                edge(w, head).wait_recv()
                acc[rows - HALO :] += hbuf[w, head].astype(F32)

        ag[slot(w), at_rows(h)] = acc[...].astype(BF)
        for j in range(n - 1):
            gather(w, j, h).start()

    def weights_part(layer):
        gate_w = jnp.zeros((inner, model), F32)
        z_w = jnp.zeros((model, inner), F32)
        x_w = jnp.zeros((model, inner), F32)
        dt_w = jnp.zeros((LANES, model), F32)
        for mb in range(count):
            x = normed[layer * count + mb, :, :model]
            gate_w = gate_w + mm_tn(ng[mb], out_b(layer, mb))
            z_w = z_w + mm_tn(x[HALO:], gz[mb])
            x_w = x_w + mm_tn(x, gext[mb, :, :inner])
            dt_w = dt_w + mm_tn(gdr[mb], x[HALO:])
        big[layer, :model, :inner] = z_w.astype(TOTAL_T)
        big[layer, :model, inner:] = x_w.astype(TOTAL_T)
        big[layer, model : model + inner] = gate_w.astype(TOTAL_T)
        table[layer, 16:24] = dt_w[:8]
        for j in range(n - 1):
            little(layer, j).start()

        @when(s == 0)
        def _():
            start_cross(layer, 0, (model + inner) // CHUNK - chunks)

        @when(s == 1)
        def _():
            start_cross(layer, 0, chunks)

    chunks = big.shape[1] // (2 * CHUNK)
    spot = s * (seqs - 1) + (1 - 2 * s) * q
    way = 1 - 2 * s
    has_prev, has_next = spot > 0, spot < seqs - 1
    delays = [(SKEW, SKEW), (SKEW + LEAD * (1 - s), SKEW + LEAD * s)]

    def span(base, c):
        return pl.ds(pl.multiple_of(base + c * CHUNK, CHUNK), CHUNK)

    def cross_at(layer, c):
        k = layer * chunks + c
        return remote(
            big.at[layer, span((1 - s) * chunks * CHUNK, c)],
            pbuf.at[layer, span(0, c)], x_s.at[k], x_r.at[k], other,
        )

    def start_cross(layer, low, high):
        def one(c, _):
            cross_at(layer, c).start()
            return 0

        lax.fori_loop(low, high, one, 0)

    def work(layer, c):
        mine = one_if(s == layer)
        return span((mine * s + 2 * (1 - mine)) * chunks * CHUNK, c)

    def along(layer, c):
        k = layer * chunks + c
        return remote(
            big.at[layer, span(s * chunks * CHUNK, c)], out.at[work(layer, c)],
            a_s.at[k], a_r.at[k], (s, q + way, h),
        )

    def home(layer, c):
        k, at = layer * chunks + c, work(layer, c)
        return remote(out.at[at], out.at[at], b_s.at[k], b_r.at[k], (s, q - way, h))

    def deliver(layer, c):
        return remote(
            out.at[work(layer, c)], out.at[span(s * chunks * CHUNK, c)], e_s.at[c], e_r.at[c],
            other,
        )

    def settled(layer, c):
        @when(has_prev)
        def _():
            home(layer, c).start()

        @when(s != layer)
        def _():
            deliver(layer, c).start()

    def advance(layer, t):
        outward, inward = delays[layer]
        c = t - outward * spot

        @when(both(c >= 0, c < chunks))
        def _():
            at = span(s * chunks * CHUNK, c)
            cross_at(layer, c).wait_recv()
            sums = big[layer, at].astype(F32) + pbuf[layer, span(0, c)].astype(F32)

            @when(has_prev)
            def _():
                along(layer, c).wait_recv()
                big[layer, at] = (sums + out[work(layer, c)].astype(F32)).astype(TOTAL_T)

            @when(jnp.logical_not(has_prev))
            def _():
                big[layer, at] = sums.astype(TOTAL_T)

            @when(has_next)
            def _():
                along(layer, c).start()

            @when(jnp.logical_not(has_next))
            def _():
                out[work(layer, c)] = big[layer, at]
                settled(layer, c)

        e = t - outward * (seqs - 1) - inward * (seqs - 1 - spot)

        @when(both(has_next, both(e >= 0, e < chunks)))
        def _():
            home(layer, e).wait_recv()
            settled(layer, e)

    def tick(w, offset, amount):
        @when(w >= count)
        def _():
            def one(i, _):
                advance(1, (w - count) * TICKS + offset + i)
                return 0

            lax.fori_loop(0, amount, one, 0)

    def late_tick(t, _):
        advance(0, t)
        advance(1, t + count * TICKS)
        return 0

    def tail_tick(w, offset, amount):
        first = (w - steps) * TAIL_TICKS + offset
        lax.fori_loop(first, first + amount, late_tick, 0)

    table[...] = jnp.zeros_like(table)
    small[...] = jnp.zeros_like(small)
    for load in loads:
        load.wait()

    def step(w, _):
        @when(w < steps)
        def _():
            for load in stream(w):
                load.wait()

        @when(w + 1 < steps)
        def _():
            for load in stream(w + 1):
                load.start()

        @when(w >= count)
        def _():
            norm_part(w - count)

        @when(w >= steps)
        def _():
            tail_tick(w, 0, TAIL_TICKS // 2)

            @when(w == steps)
            def _():
                finish(w - 1)

            tail_tick(w, TAIL_TICKS // 2, TAIL_TICKS - TAIL_TICKS // 2)

        @when(w < steps)
        def _():
            tick(w, 0, 1)

            @when(both(lax.rem(w, count) == 0, w < steps))
            def _():
                wo_load(0).wait()

            gate_first(w)

            @when(w == count - 1)
            def _():
                wo_load(0).start()

            tick(w, 1, 1)
            conv_slope(w)
            tick(w, 2, 1)
            gate_part(w)

            @when(w >= count)
            def _():
                for j in range(n - 1):
                    scatter(w - count, j).wait_send()
                    gather(w - count, j, h).wait_send()

            @when(lax.rem(w, count) == 0)
            def _():
                wc_load(0).wait()

            local_part(w)

            @when(w == count - 1)
            def _():
                wc_load(0).start()

            @when(q > 0)
            def _():
                edge(w, h).start()

            for j in range(n - 1):
                scatter(w, j).start()

            tick(w, 9, 1)

            @when(lax.rem(w, count) == count - 1)
            def _():
                weights_part(1 - w // count)

        return 0

    lax.fori_loop(0, steps + count, step, 0)

    def settle_sends(mb, _):
        for j in range(n - 1):
            scatter(mb + count, j).wait_send()
            gather(mb + count, j, h).wait_send()
        load_part(mb).start()
        return 0

    def load_part(mb):
        return pltpu.make_async_copy(
            part_in.at[mb], part.at[mb, :, pl.ds(0, model)], p_s.at[mb]
        )

    lax.fori_loop(0, count, settle_sends, 0)
    for mb in range(count):
        load_part(mb).wait()
        for j in range(n - 1):
            scatter(steps + mb, j).start()
    tail_tick(steps + count, 0, TAIL_TICKS)

    def finish_branch(mb, _):
        finish(steps + mb)
        return 0

    lax.fori_loop(0, count, finish_branch, 0)
    tail_tick(steps + count + 1, 0, TAIL_TICKS)

    def last_layer(mb, _):
        @when(s == 0)
        def _():
            out_local(mb).wait()

        @when(s == 1)
        def _():
            out_ship(mb).wait_send()

        for j in range(n - 1):
            gather(steps + mb, j, froms[j]).wait_recv()
        u = count + mb
        scale = jnp.sum(normed[u, HALO:, model:].astype(F32), axis=1, keepdims=True)
        h_in = normed[u, HALO:, :model].astype(F32) / (scale * pr[1, 0:1])
        branch = ag[mb, :, :model].astype(F32)
        send_layer(1, mb, h_in + branch, branch)
        return 0

    lax.fori_loop(0, count, last_layer, 0)

    def drain(w, _):
        @when(both(w >= count, q > 0))
        def _():
            for k in range(PIECES):
                chain(w, k).wait_send()

        @when(w < count)
        def _():
            for j in range(n - 1):
                scatter(steps + w, j).wait_send()
                gather(steps + w, j, h).wait_send()

        for j in range(n - 1):
            dots(w, j).wait_send()

        @when(q > 0)
        def _():
            edge(w, h).wait_send()

        return 0

    lax.fori_loop(0, steps, drain, 0)
    for layer in range(2):
        total = small[layer]
        for j in range(n - 1):
            little(layer, j).wait_recv()
            total = total + srecv[layer, j]
        for j in range(n - 1):
            little(layer, j).wait_send()
        table[layer, 1:6, inner : inner + 2 * state] = total[1:6]
    small_cross = remote(table.at[1 - s], ps, t_s.at[0], t_r.at[0], other)
    small_along = remote(ts, rs_, t_s.at[1], t_r.at[1], (s, q + 1, h))
    small_home = remote(small_o, small_o, t_s.at[2], t_r.at[2], (s, q - 1, h))
    small_cross.start()
    done = (count + 2) * TAIL_TICKS
    first_end = chunks + 2 * SKEW * (seqs - 1)
    second_end = chunks + (2 * SKEW + LEAD) * (seqs - 1) - count * TICKS
    last = max(first_end, second_end, done + 2 * SKEW * (seqs - 1) + 1)
    back_at = done + SKEW * (2 * (seqs - 1) - q)

    def last_tick(t, _):
        @when(t == done + SKEW * q)
        def _():
            small_cross.wait_recv()
            ts[...] = table[s] + ps[...]

            @when(q > 0)
            def _():
                small_along.wait_recv()
                ts[...] += rs_[...]

            @when(q < seqs - 1)
            def _():
                small_along.start()

            @when(q == seqs - 1)
            def _():
                small_o[...] = ts[...]

                @when(q > 0)
                def _():
                    small_home.start()

        @when(both(t == back_at, q < seqs - 1))
        def _():
            small_home.wait_recv()

            @when(q > 0)
            def _():
                small_home.start()

        return late_tick(t, _)

    lax.fori_loop(done, last, last_tick, 0)

    def drain_sum(c, _):
        for layer in range(2):
            cross_at(layer, c).wait_send()

            @when(has_next)
            def _():
                along(layer, c).wait_send()

            @when(has_prev)
            def _():
                home(layer, c).wait_send()

            @when(s != layer)
            def _():
                deliver(layer, c).wait_send()

        remote(
            out.at[work(0, c)], out.at[span((1 - s) * chunks * CHUNK, c)], e_s.at[c], e_r.at[c],
            other,
        ).wait_recv()
        return 0

    lax.fori_loop(0, chunks, drain_sum, 0)
    small_cross.wait_send()

    @when(q < seqs - 1)
    def _():
        small_along.wait_send()

    @when(q > 0)
    def _():
        small_home.wait_send()

    def drain_out(mb, _):
        ship_local(mb).wait()
        ship(mb).wait_send()
        remote(
            gin.at[mb], ig.at[(1 - s) * count + mb], l_s.at[mb], l_r.at[mb], other
        ).wait_recv()

        @when(s == 1)
        def _():
            out_local(mb).wait()

        @when(s == 0)
        def _():
            out_ship(mb).wait_send()

        remote(
            lo_s.at[mb], lo.at[(1 - s) * count + mb], k_s.at[mb], k_r.at[mb], other
        ).wait_recv()
        return 0

    lax.fori_loop(0, count, drain_out, 0)


def pad_lanes(a, width):
    return jnp.pad(a, ((0, 0), (0, width - a.shape[1])))


def final_kernel(zx, wo, bc, table, lo, ig, g_zx, g_wo, g_bc, lo_o, ig_o, rms, g_norm, g_dt, g_cx, g_cxb, g_cb, g_cbb,
                 g_dtb, g_al, g_sk, g_gate):
    inner = g_zx.shape[3]
    model = table.shape[1]
    heads = g_dtb.shape[1]
    step = pl.program_id(0)
    g_zx[0, :, 0, :] = zx[:, :inner].astype(F32)
    g_zx[0, :, 1, :] = zx[:, inner:].astype(F32)
    g_wo[0] = wo[...].astype(F32)
    lo_o[0] = lo[...]
    ig_o[0] = ig[...]

    @when(step == 0)
    def _():
        deep = g_bc.shape[2]
        for k in range(model // deep):
            cut = slice(k * deep, (k + 1) * deep)
            g_bc[0, cut] = bc[:, cut].astype(F32)
        live = table[26:27, :LANES] * model
        first = jnp.sqrt(table[24:25, :LANES] / live)
        second = jnp.sqrt(table[25:26, :LANES] / live)
        rms[...] = jnp.where(iota((1, LANES), 1) == 0, first, second)[:, :2]
        g_norm[...] = table[0:1]
        g_dt[0] = table[16 : 16 + heads]
        g_cx[0] = table[1:5, :inner]
        g_cxb[...] = table[5:6, :inner]
        g_cb[0] = table[1:5, inner : inner + deep]
        g_cbb[...] = table[5:6, inner : inner + deep]
        g_dtb[...] = table[6:7, :heads]
        g_al[...] = table[7:8, :heads]
        sums = mm(table[8:16, :inner], spread_matrix(inner).astype(F32).T, HIGH)
        g_sk[...] = sums[1:2, :heads]
        g_gate[...] = table[8:9, :inner]


def finalize(big, table, lo, ig, inner, heads, state):
    model = big.shape[1]
    steps = lo.shape[0]
    each = (1,) + lo.shape[1:]
    deep = 2 * state

    def whole(shape):
        return pl.BlockSpec(shape, lambda i: (0,) * len(shape))

    shapes = [
        (1, model, 2, inner), (1, inner, model), (1, model, deep), (1,) + lo.shape,
        (1,) + ig.shape, (1, 2), (1, model),
        (1, heads, model), (1, 4, inner), (1, inner), (1, 4, deep), (1, deep),
        (1, heads), (1, heads), (1, heads), (1, inner),
    ]
    specs = [
        pl.BlockSpec((1, model // steps, 2, inner), lambda i: (0, i, 0, 0)),
        pl.BlockSpec((1, inner // steps, model), lambda i: (0, i, 0)),
        whole(shapes[2]),
        pl.BlockSpec((1,) + each, lambda i: (0, i, 0, 0)),
        pl.BlockSpec((1,) + each, lambda i: (0, i, 0, 0)),
    ] + [whole(x) for x in shapes[5:]]
    base = model // (inner // steps)
    return pl.pallas_call(
        final_kernel,
        grid=(steps,),
        in_specs=[
            pl.BlockSpec((model // steps, model), lambda i: (i, 0)),
            pl.BlockSpec((inner // steps, model), lambda i: (base + i, 0)),
            pl.BlockSpec((deep, model), lambda i: ((model + inner) // deep, 0)),
            whole(table.shape),
            pl.BlockSpec(each, lambda i: (i, 0, 0)),
            pl.BlockSpec(each, lambda i: (i, 0, 0)),
        ],
        out_specs=specs,
        out_shape=[jax.ShapeDtypeStruct(x, F32) for x in shapes],
        compiler_params=pltpu.CompilerParams(vmem_limit_bytes=LIMIT),
        name="final",
    )(big, big, big, table, lo, ig)


def local(hidden_in, cotangent, segments, padding, norm_gain, w_zx, w_bc, w_dt, conv_x,
          conv_x_bias, conv_bc, conv_bc_bias, dt_bias, a_log, skip_d, gate_gain, w_out):
    s, q, h = place()
    seqs = lax.axis_size(SEQ)
    n = lax.axis_size(HEAD)
    sections = lax.axis_size(SEC)
    batches, tokens, model = hidden_in.shape
    count = batches // sections
    inner = w_out.shape[1]
    heads = w_dt.shape[2]
    state = w_bc.shape[2] // 2
    wide = inner + 2 * state
    wc = jnp.concatenate(
        [w_zx[0, :, 0], w_zx[0, :, 1], w_bc[0], pad_lanes(w_dt[0], LANES)], axis=1
    )
    units = 2 * count
    rows = tokens + HALO
    part_rows = tokens // n
    lane_shape = (units, tokens, LANES)
    inner_shape = (units, tokens, inner)
    state_shape = (units, inner, LANES)
    peer_sems = DMA((units, n - 1))
    out_shape = ((batches, tokens, model), F32)
    kept_shapes = [
        ((units, rows, model + LANES), BF),
        ((units, rows, wide), BF),
        (inner_shape, F32),
        (lane_shape, F32),
        (lane_shape, F32),
        (lane_shape, F32),
        ((units, tokens, wide), BF),
        (state_shape, BF),
        (inner_shape, F32),
        (lane_shape, F32),
        ((count, tokens, model), BF),
        ((2,) + wc.shape, BF),
        ((2,) + w_out.shape[1:], BF),
    ]
    car, pr, seg_col, srow, pad, *kept = comm(
        functools.partial(fwd_kernel, seqs, n),
        (hidden_in, segments, padding, norm_gain, conv_x, conv_x_bias, conv_bc, conv_bc_bias,
         dt_bias, a_log, skip_d, gate_gain, wc, w_out[0]),
        [
            ((units, heads, LANES), F32),
            ((2, 16, model), F32),
            ((count, rows, LANES), F32),
            ((count, 8, tokens), F32),
            ((count, tokens, LANES), F32),
        ]
        + kept_shapes,
        [pltpu.VMEM(*x) for x in kept_shapes]
        + [
            pltpu.VMEM((count, HALO, model), F32),
            pltpu.VMEM((count, HALO, LANES), F32),
            pltpu.VMEM((16, model), F32),
            pltpu.VMEM((count, tokens, model), F32),
            pltpu.VMEM((rows, wide), F32),
            pltpu.VMEM((inner, LANES), F32),
            pltpu.VMEM(state_shape, BF),
            pltpu.VMEM((tokens, inner), F32),
            pltpu.VMEM((count, tokens, model), BF),
            pltpu.VMEM((count, n - 1, part_rows, model), BF),
            pltpu.VMEM((units, 8, tokens), F32),
            pltpu.VMEM((units, n - 1, 8, tokens), F32),
            DMA((units, PIECES)), DMA((units, PIECES)),
            peer_sems, peer_sems, peer_sems, peer_sems, peer_sems, peer_sems,
            DMA((count, n)), DMA((count,)), DMA((1,)),
            DMA((5,)), DMA((5,)), DMA((11, units)), DMA((2, 2)),
        ],
        1, "fwd", len(kept_shapes), 1,
    )
    normed, raw, z, dtp, dt, cum, co, st, yn, gsc, part, wc, wo = kept
    total_rows = model + inner + 2 * state
    chunk_sems = DMA((total_rows // CHUNK,))
    more_sems = DMA((units + count, n - 1))
    table_shape = (32, model)
    grad_shape = (tokens, model + 2 * state)
    big, table, input_grad, layer_out = comm(
        functools.partial(bwd_kernel, seqs, n),
        (cotangent, hidden_in, normed, wc, wo, raw, z, dtp, dt, cum, co, st, yn, gsc,
         part, pad, car, seg_col, srow, pr),
        (((total_rows * 3 // 2, model), TOTAL_T), (table_shape, F32), out_shape, out_shape),
        [
            pltpu.VMEM((units, tokens, model), F32),
            pltpu.VMEM((count, tokens, model), F32),
            pltpu.VMEM((units, rows, model + LANES), BF),
            pltpu.VMEM(wc.shape[1:], BF),
            pltpu.VMEM(wo.shape[1:], BF),
            pltpu.VMEM((count, rows, wide), BF),
            pltpu.VMEM((count, tokens, inner), F32),
            pltpu.VMEM((count, tokens, LANES), F32),
            pltpu.VMEM((count, tokens, LANES), F32),
            pltpu.VMEM((count, tokens, LANES), F32),
            pltpu.VMEM((count, tokens, wide), BF),
            pltpu.VMEM((count, inner, LANES), BF),
            pltpu.VMEM((count, tokens, inner), F32),
            pltpu.VMEM((count, tokens, LANES), F32),
            pltpu.VMEM((2, total_rows, model), TOTAL_T),
            pltpu.VMEM((2, total_rows // 2, model), TOTAL_T),
            pltpu.VMEM((2,) + table_shape, F32),
            pltpu.VMEM(table_shape, F32),
            pltpu.VMEM(table_shape, F32),
            pltpu.VMEM(table_shape, F32),
            pltpu.VMEM((rows, wide), F32),
            pltpu.VMEM((rows + HALO, LANES), F32),
            pltpu.VMEM((tokens, wide), F32),
            pltpu.VMEM((count, rows, wide), BF),
            pltpu.VMEM((count, tokens, inner), BF),
            pltpu.VMEM((tokens, inner), BF),
            pltpu.VMEM((count, tokens, inner), BF),
            pltpu.VMEM((count, tokens, LANES), BF),
            pltpu.VMEM((inner, LANES), F32),
            pltpu.VMEM(state_shape, BF),
            pltpu.VMEM((count, inner, LANES), BF),
            pltpu.VMEM((count,) + grad_shape, BF),
            pltpu.VMEM((units, HALO, model + 2 * state), BF),
            pltpu.VMEM((count, n - 1, part_rows, model + 2 * state), BF),
            pltpu.VMEM((units, n, HALO, model + 2 * state), BF),
            pltpu.VMEM((part_rows, model + 2 * state), F32),
            pltpu.VMEM((count,) + grad_shape, BF),
            pltpu.VMEM((model, 2 * state), F32),
            pltpu.VMEM((2, 8, 2 * state), F32),
            pltpu.VMEM((2, n - 1, 8, 2 * state), F32),
            pltpu.VMEM((tokens, inner), F32),
            pltpu.VMEM((units, 8, tokens), F32),
            pltpu.VMEM((units, n - 1, 8, tokens), F32),
            DMA((units, PIECES)), DMA((units, PIECES)),
            more_sems, more_sems, more_sems, more_sems,
            DMA((units,)), DMA((units, n)),
            DMA((2, n - 1)), DMA((2, n - 1)),
            DMA((count,)), DMA((count,)), DMA((count,)), DMA((3,)),
            peer_sems, peer_sems,
            DMA((9, count)), DMA((2,)),
            chunk_sems, chunk_sems, chunk_sems, chunk_sems, chunk_sems, chunk_sems,
            DMA((3,)), DMA((3,)), DMA((count,)), DMA((count,)), DMA((count,)),
            DMA((total_rows // CHUNK // 2,)), DMA((total_rows // CHUNK // 2,)), DMA((count,)),
        ],
        2, "bwd", 2, 15,
    )
    (g_zx, g_wo, g_bc, layer_out, input_grad, rms, g_norm, g_dt, g_cx, g_cxb, g_cb, g_cbb, g_dtb, g_al, g_sk,
     g_gate) = finalize(
        big, table, layer_out, input_grad, inner, heads, state
    )
    return (layer_out, input_grad, rms, g_norm, g_zx, g_bc,
            jnp.transpose(g_dt, (0, 2, 1)), g_cx, g_cxb,
            g_cb, g_cbb, g_dtb, g_al, g_sk, g_gate, g_wo)


def solution(mesh):
    in_specs = (
        P(None, SEQ, None),
        P(None, SEQ, None),
        P(None, SEQ),
        P(None, SEQ),
        P(SEC, None),
        P(SEC, None, None, HEAD),
        P(SEC, None, None),
        P(SEC, None, HEAD),
        P(SEC, None, HEAD),
        P(SEC, HEAD),
        P(SEC, None, None),
        P(SEC, None),
        P(SEC, HEAD),
        P(SEC, HEAD),
        P(SEC, HEAD),
        P(SEC, HEAD),
        P(SEC, HEAD, None),
    )
    out_specs = (
        P(SEC, None, SEQ, None),
        P(SEC, None, SEQ, None),
        P(SEC, None),
        P(SEC, None),
        P(SEC, None, None, HEAD),
        P(SEC, None, None),
        P(SEC, None, HEAD),
        P(SEC, None, HEAD),
        P(SEC, HEAD),
        P(SEC, None, None),
        P(SEC, None),
        P(SEC, HEAD),
        P(SEC, HEAD),
        P(SEC, HEAD),
        P(SEC, HEAD),
        P(SEC, HEAD, None),
    )
    return jax.shard_map(local, mesh=mesh, in_specs=in_specs, out_specs=out_specs, check_vma=False)
```

```python
import functools

import jax
import jax.numpy as jnp
from jax import lax
from jax.experimental import pallas as pl
from jax.experimental.pallas import tpu as pltpu
from jax.sharding import PartitionSpec as P

SEC, SEQ, HEAD = "section", "seq", "head"
F32, BF = jnp.float32, jnp.bfloat16
MESH = pl.DeviceIdType.MESH
HIGH = lax.Precision.HIGHEST
EPS = 1e-05
KC = 4
HALO = 16
LANES = 128
HEAD_SHIFT = 6
LIMIT = 58 << 20
CHUNK = 64
SKEW = 3
LEAD = 2
TICKS = 10
TAIL_TICKS = 4
PIECES = 4
TOTAL_T = jnp.bfloat16


def mm(a, b, precision=None):
    return lax.dot_general(
        a, b, (((1,), (0,)), ((), ())), precision=precision, preferred_element_type=F32
    )


def mm_nt(a, b):
    return lax.dot_general(a, b, (((1,), (1,)), ((), ())), preferred_element_type=F32)


def mm_tn(a, b, precision=None):
    return lax.dot_general(
        a, b, (((0,), (0,)), ((), ())), precision=precision, preferred_element_type=F32
    )


def iota(shape, dim):
    return lax.broadcasted_iota(jnp.int32, shape, dim)


def spread_matrix(width):
    shape = (LANES, width)
    return (iota(shape, 0) == jnp.right_shift(iota(shape, 1), HEAD_SHIFT)).astype(BF)


def split(x):
    high = x.astype(BF)
    return high, (x - high.astype(F32)).astype(BF)


def expand(x, matrix):
    high, low = split(x)
    return mm(high, matrix) + mm(low, matrix)


def head_sums(x, matrix):
    high, low = split(x)
    return mm_nt(high, matrix) + mm_nt(low, matrix)


def fine(product, a, b):
    high, low = split(a)
    return product(high, b) + product(low, b)


def two_lanes(column):
    high = column.astype(BF).astype(F32)
    lane = iota((column.shape[0], LANES), 1)
    return jnp.where(lane == 0, high, jnp.where(lane == 1, column - high, 0.0)).astype(BF)


def sigmoid(v):
    return 1.0 / (1.0 + jnp.exp(-v))


def lower(size):
    return (iota((size, size), 0) >= iota((size, size), 1)).astype(F32)


def same_rows(seg_ref, mb, tokens):
    mine = seg_ref[mb, HALO:]
    first = HALO - KC + 1
    return [
        (seg_ref[mb, first + k : first + k + tokens] == mine).astype(F32) for k in range(KC)
    ]


def convolved(raw_f, same, prm, col, tokens):
    first = HALO - KC + 1
    cols = slice(col, col + LANES)
    pre = jnp.zeros((tokens, LANES), F32) + prm[5:6, cols]
    for k in range(KC):
        pre = pre + prm[1 + k : 2 + k, cols] * raw_f[first + k : first + k + tokens, cols] * same[k]
    return pre


def gains(cum, seg_ref, mb):
    mine = seg_ref[mb, HALO:]
    before = seg_ref[mb, HALO - 1 : HALO]
    last = mine[-1:]
    entry = jnp.exp(cum) * (mine == before).astype(F32)
    decay_end = jnp.exp(cum[-1:] - cum) * (mine == last).astype(F32)
    return entry, decay_end


def place():
    return lax.axis_index(SEC), lax.axis_index(SEQ), lax.axis_index(HEAD)


def remote(src, dst, send, recv, device):
    return pltpu.make_async_remote_copy(
        src_ref=src, dst_ref=dst, send_sem=send, recv_sem=recv, device_id=device,
        device_id_type=MESH,
    )


def greet(device):
    pl.semaphore_signal(
        pltpu.get_barrier_semaphore(), inc=1, device_id=device, device_id_type=MESH
    )


def await_greets(count):
    pl.semaphore_wait(pltpu.get_barrier_semaphore(), count)


def one_if(condition):
    return condition.astype(jnp.int32)


def comm(kernel, ins, outs, scratch, ident, name, in_hbm=0, from_hbm=0):
    sources = [pl.ANY] * from_hbm + [pltpu.VMEM] * (len(ins) - from_hbm)
    spaces = [pltpu.VMEM] * (len(outs) - in_hbm) + [pl.ANY] * in_hbm
    return pl.pallas_call(
        kernel,
        in_specs=[pl.BlockSpec(memory_space=space) for space in sources],
        out_specs=[pl.BlockSpec(memory_space=space) for space in spaces],
        out_shape=[jax.ShapeDtypeStruct(s, d) for s, d in outs],
        scratch_shapes=scratch,
        compiler_params=pltpu.CompilerParams(
            collective_id=ident, has_side_effects=True, vmem_limit_bytes=LIMIT
        ),
        name=name,
    )(*ins)


DMA = pltpu.SemaphoreType.DMA


def wide_copy(x, width):
    return jnp.concatenate([x] * (width // LANES), axis=1)


def causal_mask(seg_ref, srow_ref, mb, tokens, transposed):
    row = iota((tokens, tokens), 0)
    col = iota((tokens, tokens), 1)
    same = wide_copy(seg_ref[mb, HALO:], tokens) == srow_ref[mb, 0:1]
    return same & ((row <= col) if transposed else (row >= col))


def when(condition):
    return pl.when(condition)


def both(a, b):
    return jnp.logical_and(a, b)


def fwd_kernel(seqs, n, source, segments, padding, norm_gain, conv_x, conv_xb, conv_bc, conv_bcb,
               dt_bias, a_log, skip_d, gate_gain, wc_in, wo_in,
               car, pr, seg, srow, pad, normed_o, raw_o, z_o, dtp_o, dt_o, cum_o, co_o, st_o,
               yn_o, gsc_o, part_o, wc_o, wo_o,
               normed, raw, z, dtp, dt, cum, co, st, yn, gsc, part, wc, wo,
               halo, seg_halo, pr_in, hid, raw_f, con, sbuf, gated_s, part0, rbuf0, ssend, srecv,
               c_s, c_r, q_s, q_r, s_s, s_r, g_s, g_r, h_s, h_r, in_s, w_s, w_r, o_s, v_s):
    s, q, h = place()
    count, tokens, model = hid.shape
    inner = wo.shape[1]
    wide = raw.shape[2]
    heads = inner >> HEAD_SHIFT
    rows = tokens // n
    units = 2 * count
    full = inner * n
    piece = inner // PIECES
    other = (1 - s, q, h)
    first_q, last_q = q == 0, q == seqs - 1
    edge_owner = both(h == n - 1, q < seqs - 1)
    peers = [lax.rem(h + j, n) for j in range(1, n)]
    froms = [lax.rem(h + n - j, n) for j in range(1, n)]
    matrix = spread_matrix(inner)
    load = pltpu.make_async_copy(source.at[pl.ds(s * count, count)], hid, in_s.at[0])
    load.start()
    for p in peers:
        greet((s, q, p))
    greet(other)

    @when(q > 0)
    def _():
        greet((s, q - 1, n - 1))

    @when(both(q > 0, h < n - 1))
    def _():
        greet((s, q - 1, h))

    await_greets(n + one_if(q < seqs - 1) * (1 + (n - 1) * one_if(h == n - 1)))

    def at_rows(owner):
        return pl.ds(pl.multiple_of(owner * rows, rows), rows)

    def slot_rows(owner):
        return pl.ds(pl.multiple_of(HALO + owner * rows, HALO), rows)

    def chain(u, k):
        cut = pl.ds(k * piece, piece)
        return remote(
            sbuf.at[u, cut], st.at[u, cut], c_s.at[u, k], c_r.at[u, k], (s, q + 1, h)
        )

    def squares(u, j):
        return remote(
            ssend.at[u], srecv.at[u, j], q_s.at[u, j], q_r.at[u, j], (s, q, peers[j])
        )

    def scatter(u, j):
        return remote(
            part0.at[u, at_rows(peers[j])], rbuf0.at[u, j], s_s.at[u, j], s_r.at[u, j],
            (s, q, peers[j]),
        )

    def gather(u, j, owner):
        where = (u + count, slot_rows(owner))
        return remote(
            normed.at[where], normed.at[where], g_s.at[u, j], g_r.at[u, j], (s, q, peers[j])
        )

    def edge(u, head):
        return remote(
            normed.at[u + count, pl.ds(tokens, HALO)], normed.at[u + count, pl.ds(0, HALO)],
            h_s.at[u, head], h_r.at[u], (s, q + 1, head),
        )

    keeps = (
        (raw, raw_o), (z, z_o), (dtp, dtp_o), (dt, dt_o), (cum, cum_o), (co, co_o), (st, st_o),
        (yn, yn_o), (gsc, gsc_o),
    )

    def keep(u):
        return [
            pltpu.make_async_copy(a.at[u], b.at[u], o_s.at[i, u]) for i, (a, b) in enumerate(keeps)
        ]

    def keep_normed(u):
        return pltpu.make_async_copy(normed.at[u], normed_o.at[u], o_s.at[len(keeps), u])

    def keep_part(mb):
        return pltpu.make_async_copy(
            part.at[mb], part_o.at[mb], o_s.at[len(keeps) + 1, mb]
        )

    def keep_weight(i, layer):
        a, b = ((wc, wc_o), (wo, wo_o))[i]
        return pltpu.make_async_copy(a.at[layer], b.at[layer], v_s.at[i, layer])

    def pass_state(u):
        for k in range(PIECES):
            @when(q > 0)
            def _():
                chain(u, k).wait_recv()

            @when(first_q)
            def _():
                st[u, k * piece : (k + 1) * piece] = jnp.zeros((piece, LANES), BF)

            @when(q < seqs - 1)
            def _():
                per = inner // heads
                for i in range(k * heads // PIECES, (k + 1) * heads // PIECES):
                    cut = slice(i * per, (i + 1) * per)
                    sbuf[u, cut] = (
                        car[u, i : i + 1] * st[u, cut].astype(F32) + con[cut]
                    ).astype(BF)
                chain(u, k).start()

    def weight(i, layer):
        src, dst = ((pr_in, pr), (wc_in, wc), (wo_in, wo))[i]
        return remote(src, dst.at[layer], w_s.at[i], w_r.at[i], other)

    weight(1, s).start()
    weight(2, s).start()
    halo_copy = remote(
        hid.at[:, pl.ds(tokens - HALO, HALO)], halo, w_s.at[3], w_r.at[3], (s, q + 1, h)
    )
    seg_copy = remote(
        seg.at[:, pl.ds(tokens, HALO)], seg_halo, w_s.at[4], w_r.at[4], (s, q + 1, h)
    )
    deep = conv_bc.shape[2]
    pr_in[...] = jnp.zeros_like(pr_in)
    pr_in[0:1] = norm_gain[...]
    pr_in[1:5, :inner] = conv_x[0]
    pr_in[1:5, inner : inner + deep] = conv_bc[0]
    pr_in[5:6, :inner] = conv_xb[...]
    pr_in[5:6, inner : inner + deep] = conv_bcb[...]
    pr_in[6:7, :heads] = dt_bias[...]
    pr_in[7:8, :heads] = -jnp.exp(a_log[...])
    pr_in[9:10, :inner] = gate_gain[...]
    skips = jnp.broadcast_to(
        jnp.concatenate([skip_d[...], jnp.zeros((1, LANES - heads), F32)], axis=1), (8, LANES)
    )
    pr_in[8:9, :inner] = mm(skips, matrix.astype(F32), HIGH)[:1]
    weight(0, s).start()
    batches = segments.shape[0]
    for mb in range(count):
        for given, rows_o in ((segments, srow), (padding, None)):
            row = jnp.zeros((1, tokens), F32)
            for b in range(batches):
                row = jnp.where(b == s * count + mb, given[b : b + 1].astype(F32), row)
            row = jnp.broadcast_to(row, (8, tokens))
            column = mm_tn(row * 0.125, jnp.ones((8, LANES), F32), HIGH)
            if rows_o is None:
                pad[mb] = column
            else:
                rows_o[mb] = row
                seg[mb, HALO:] = column
    load.wait()

    @when(q < seqs - 1)
    def _():
        halo_copy.start()
        seg_copy.start()

    pr[s] = pr_in[...]
    wc[s] = wc_in[...]
    wo[s] = wo_in[...]
    keep_weight(0, s).start()
    keep_weight(1, s).start()

    @when(q > 0)
    def _():
        halo_copy.wait_recv()
        seg_copy.wait_recv()
        seg[:, :HALO] = seg_halo[...]

    @when(first_q)
    def _():
        halo[...] = jnp.zeros_like(halo)
        seg[:, :HALO] = jnp.full((count, HALO, LANES), -1.0, F32)

    weight(0, 1 - s).wait_recv()

    def needs_weights(u):
        return u == count * (1 - s)

    def in_norm(mb, _):
        hx = jnp.concatenate([halo[mb], hid[mb]], axis=0)
        scale = lax.rsqrt(jnp.mean(hx * hx, axis=1, keepdims=True) + EPS)
        normed[mb, :, :model] = (hx * scale * pr[0, 0:1]).astype(BF)
        normed[mb, :, model:] = two_lanes(scale)
        keep_normed(mb).start()

        @when(first_q)
        def _():
            normed[mb + count, :HALO] = jnp.zeros((HALO, model + LANES), BF)

        return 0

    lax.fori_loop(0, count, in_norm, 0)

    def local_part(u):
        layer = u // count
        mb = lax.rem(u, count)
        prm = pr[layer]
        x = normed[u, :, :model]
        new_raw = mm(x, wc[layer, :, inner : inner + wide]).astype(BF)
        raw[u] = new_raw
        raw_f[...] = new_raw.astype(F32)
        x = x[HALO:]
        z[u] = mm(x, wc[layer, :, :inner])
        new_dtp = mm(x, wc[layer, :, inner + wide :]) + prm[6:7, :LANES]
        dtp[u] = new_dtp
        new_dt = jax.nn.softplus(new_dtp)
        dt[u] = new_dt
        new_cum = mm(lower(tokens), new_dt * prm[7:8, :LANES], HIGH)
        cum[u] = new_cum
        cum_t = new_cum.T
        dt_t = new_dt.T
        same = same_rows(seg, mb, tokens)
        pieces = []
        for col in range(0, wide, LANES):
            pre = convolved(raw_f, same, prm, col, tokens)
            piece = (pre * sigmoid(pre)).astype(BF)
            co[u, :, col : col + LANES] = piece
            pieces.append(piece)
        values = jnp.concatenate(pieces[: inner // LANES], axis=1)
        in_b, in_c = pieces[-2], pieces[-1]
        entry, decay_end = gains(new_cum, seg, mb)
        toward = expand(decay_end * new_dt, matrix)
        con[...] = fine(mm_tn, values.astype(F32) * toward, in_b)
        mine = seg[mb, HALO:]
        same_before = (mine[-1:, :] == seg[mb, HALO - 1 : HALO]).astype(F32)
        car[u] = jnp.exp(cum_t[:heads, tokens - 1 :]) * same_before

        @when(first_q)
        def _():
            pass_state(u)

        inner_cb = jnp.where(
            causal_mask(seg, srow, mb, tokens, False), mm_nt(in_c, in_b), 0.0
        )
        mid = tokens // 2
        blocks = [(slice(0, mid), slice(0, mid)), (slice(mid, tokens), slice(0, tokens))]
        for pair in range(heads // 2):
            cols = slice(pair * LANES, (pair + 1) * LANES)
            accs = [jnp.zeros((mid, LANES), F32) for _ in blocks]
            for j in range(2):
                one = slice(2 * pair + j, 2 * pair + j + 1)
                for i, (to, of) in enumerate(blocks):
                    decay = jnp.exp(jnp.minimum(new_cum[to, one] - cum_t[one, of], 0.0))
                    mask = jnp.right_shift(iota((of.stop, LANES), 1), HEAD_SHIFT) == j
                    value = jnp.where(mask, values[of, cols], jnp.zeros((), BF))
                    mixed = (inner_cb[to, of] * decay * dt_t[one, of]).astype(BF)
                    accs[i] = accs[i] + mm(mixed, value)
            for i, (to, of) in enumerate(blocks):
                yn[u, to, cols] = accs[i]

    def gate_part(u):
        layer = u // count
        mb = lax.rem(u, count)
        entry, _ = gains(cum[u], seg, mb)
        in_c = co[u, :, inner + LANES :]
        readout = mm_nt(in_c, st[u])
        y = yn[u] + expand(entry, matrix) * readout
        yn[u] = y
        ssd = y + pr[layer, 8:9, :inner] * co[u, :, :inner].astype(F32)
        gate = z[u]
        gated = ssd * (gate * sigmoid(gate))
        gated_s[...] = gated
        ones = jnp.ones((8, inner), BF)
        ssend[u] = fine(lambda a, b: mm_nt(b, a), gated * gated, ones)

    def out_part(u):
        layer = u // count
        total = ssend[u]
        for j in range(n - 1):
            squares(u, j).wait_recv()
            total = total + srecv[u, j]
        scale_row = lax.rsqrt(total / full + EPS)
        scale = mm_tn(scale_row * 0.125, jnp.ones((8, LANES), F32), HIGH)
        gsc[u] = scale
        x = (gated_s[...] * wide_copy(scale, inner) * pr[layer, 9:10, :inner]).astype(BF)
        product = mm(x, wo[layer])

        @when(u < count)
        def _():
            part0[u] = product.astype(BF)
            for j in range(n - 1):
                scatter(u, j).start()

        @when(u >= count)
        def _():
            part[u - count] = product.astype(BF)
            keep_part(u - count).start()

    def finish(u):
        total = part0[u, at_rows(h)].astype(F32)
        for j in range(n - 1):
            scatter(u, j).wait_recv()
            total = total + rbuf0[u, j].astype(F32)
        h_new = hid[u, at_rows(h)] + total
        scale = lax.rsqrt(jnp.mean(h_new * h_new, axis=1, keepdims=True) + EPS)
        normed[u + count, slot_rows(h), :model] = (h_new * scale * pr[1, 0:1]).astype(BF)
        normed[u + count, slot_rows(h), model:] = two_lanes(scale)
        for j in range(n - 1):
            gather(u, j, h).start()

        @when(edge_owner)
        def _():
            for head in range(n):
                edge(u, head).start()

    def arrived(u):
        for j in range(n - 1):
            gather(u, j, froms[j]).wait_recv()

    def step(u, _):
        @when(both(u >= count, u < units))
        def _():
            mb = u - count
            arrived(mb)

            @when(q > 0)
            def _():
                edge(mb, 0).wait_recv()

            keep_normed(u).start()

        @when(u == count)
        def _():
            finish(u - 1)

        @when(needs_weights(u))
        def _():
            weight(1, 1 - s).wait_recv()
            keep_weight(0, 1 - s).start()

        @when(u < units)
        def _():
            local_part(u)

            @when(q > 0)
            def _():
                pass_state(u)

            gate_part(u)
            for j in range(n - 1):
                squares(u, j).start()

        @when(both(u > 0, u < count))
        def _():
            finish(u - 1)

        @when(needs_weights(u))
        def _():
            weight(2, 1 - s).wait_recv()
            keep_weight(1, 1 - s).start()

        @when(u < units)
        def _():
            out_part(u)
            for copy in keep(u):
                copy.start()

        return 0

    lax.fori_loop(0, units, step, 0)

    def drain(u, _):
        for j in range(n - 1):
            squares(u, j).wait_send()

        @when(q < seqs - 1)
        def _():
            for k in range(PIECES):
                chain(u, k).wait_send()

        @when(u < count)
        def _():
            for j in range(n - 1):
                scatter(u, j).wait_send()
                gather(u, j, h).wait_send()
            keep_part(u).wait()

        @when(both(u < count, edge_owner))
        def _():
            for head in range(n):
                edge(u, head).wait_send()

        for copy in keep(u):
            copy.wait()
        keep_normed(u).wait()
        return 0

    lax.fori_loop(0, units, drain, 0)
    for i in range(3):
        weight(i, s).wait_send()
    for i in range(2):
        for layer in range(2):
            keep_weight(i, layer).wait()

    @when(q < seqs - 1)
    def _():
        halo_copy.wait_send()
        seg_copy.wait_send()


def bwd_kernel(seqs, n, cot, hid, kept, wc_in, wo_in, raw_in, z_in, dtp_in, dt_in, cum_in,
               co_in, st_in, yn_in, gsc_in, part_in, pad, car, seg, srow, pr,
               out, small_o, ig, lo,
               gin, lo_s, normed, wc, wo, raw, z, dtp, dt, cum, co, st, yn, gsc,
               big, pbuf, table, ps, rs_, ts,
               raw_f, shift, gconv, gext, gz, gy_s, ng, gdr, back, nxt, sbuf,
               part, hpart, rbuf, hbuf, acc, ag, gwb, small, srecv, ggn, dsend, drecv,
               c_s, c_r, s_s, s_r, g_s, g_r, h_s, h_r, m_s, m_r, l_c, l_s, l_r, in_s,
               d_s, d_r, f_s, w_s, x_s, x_r, a_s, a_r, b_s, b_r, t_s, t_r,
               k_c, k_s, k_r, e_s, e_r, p_s):
    s, q, h = place()
    count, tokens, model = gin.shape[0] // 2, gin.shape[1], gin.shape[2]
    inner = wo.shape[0]
    state = LANES
    wide = raw.shape[2]
    heads = inner >> HEAD_SHIFT
    rows = tokens // n
    ext = tokens + HALO
    steps = 2 * count
    full = inner * n
    piece = inner // PIECES
    other = (1 - s, q, h)
    edge_owner = both(h == n - 1, q < seqs - 1)
    peers = [lax.rem(h + j, n) for j in range(1, n)]
    froms = [lax.rem(h + n - j, n) for j in range(1, n)]
    matrix = spread_matrix(inner)
    sources = (raw_in, z_in, dtp_in, dt_in, cum_in, co_in, st_in, yn_in, gsc_in)
    targets = (raw, z, dtp, dt, cum, co, st, yn, gsc)

    def unit(w):
        return (1 - w // count) * count + lax.rem(w, count)

    def stream(w):
        k = lax.rem(w, count)
        return [
            pltpu.make_async_copy(a.at[unit(w)], b.at[k], f_s.at[i, k])
            for i, (a, b) in enumerate(zip(sources, targets))
        ]

    def wc_load(layer):
        return pltpu.make_async_copy(wc_in.at[layer], wc, w_s.at[0])

    def wo_load(layer):
        return pltpu.make_async_copy(wo_in.at[layer], wo, w_s.at[1])

    loads = [
        pltpu.make_async_copy(cot.at[pl.ds(s * count, count)], gin.at[pl.ds(0, count)], in_s.at[0]),
        pltpu.make_async_copy(
            hid.at[pl.ds(s * count, count)], gin.at[pl.ds(count, count)], in_s.at[1]
        ),
        pltpu.make_async_copy(kept.at[pl.ds(0, steps)], normed, in_s.at[2]),
    ]
    loads[0].start()
    wo_load(1).start()
    for load in stream(0):
        load.start()
    wc_load(1).start()
    for load in loads[1:]:
        load.start()
    for p in peers:
        greet((s, q, p))
    greet(other)

    @when(q < seqs - 1)
    def _():
        greet((s, q + 1, h))

    @when(edge_owner)
    def _():
        for head in range(n - 1):
            greet((s, q + 1, head))

    @when(q > 0)
    def _():
        greet((s, q - 1, h))

    await_greets(
        n + one_if(q > 0) * (1 + one_if(h < n - 1)) + one_if(q < seqs - 1)
    )

    def at_rows(owner):
        return pl.ds(pl.multiple_of(owner * rows, rows), rows)

    def slot(w):
        return lax.rem(w, count)

    def chain(w, k):
        cut = pl.ds(k * piece, piece)
        return remote(
            sbuf.at[slot(w), cut], nxt.at[w, cut], c_s.at[w, k], c_r.at[w, k], (s, q - 1, h)
        )

    def scatter(w, j):
        return remote(
            part.at[slot(w), at_rows(peers[j])], rbuf.at[slot(w), j], s_s.at[w, j],
            s_r.at[w, j], (s, q, peers[j]),
        )

    def gather(w, j, owner):
        where = (slot(w), at_rows(owner))
        return remote(
            ag.at[where], ag.at[where], g_s.at[w, j], g_r.at[w, j], (s, q, peers[j])
        )

    def branch_scatter(mb, j):
        lanes = pl.ds(0, model)
        return remote(
            part.at[mb, at_rows(peers[j]), lanes], rbuf.at[mb, j, :, lanes],
            s_s.at[steps + mb, j], s_r.at[steps + mb, j], (s, q, peers[j]),
        )

    def branch_gather(mb, j, owner):
        where = (mb, at_rows(owner), pl.ds(0, model))
        return remote(
            ag.at[where], ag.at[where], g_s.at[steps + mb, j], g_r.at[steps + mb, j],
            (s, q, peers[j]),
        )

    def edge(w, head):
        return remote(
            hpart.at[w], hbuf.at[w, head], h_s.at[w], h_r.at[w, head], (s, q - 1, n - 1)
        )

    def little(layer, j):
        return remote(
            small.at[layer], srecv.at[layer, j], m_s.at[layer, j], m_r.at[layer, j],
            (s, q, peers[j]),
        )

    def ship_local(v):
        mb = lax.rem(v, count)
        return pltpu.make_async_copy(gin.at[v], ig.at[s * count + mb], l_c.at[mb])

    def ship(v):
        mb = lax.rem(v, count)
        return remote(gin.at[v], ig.at[s * count + mb], l_s.at[mb], l_r.at[mb], other)

    def out_local(mb):
        return pltpu.make_async_copy(lo_s.at[mb], lo.at[s * count + mb], k_c.at[mb])

    def out_ship(mb):
        return remote(lo_s.at[mb], lo.at[s * count + mb], k_s.at[mb], k_r.at[mb], other)

    def send_layer(layer, mb, h_new, branch):
        lo_s[mb] = h_new
        live = pad[mb]
        for i, x in enumerate((h_new, branch)):
            table[layer, 24 + i : 25 + i, :LANES] += jnp.sum(
                jnp.sum(x * x, axis=1, keepdims=True) * live, axis=0, keepdims=True
            )
        table[layer, 26:27, :LANES] += jnp.sum(live, axis=0, keepdims=True)

        @when(s == layer)
        def _():
            out_local(mb).start()

        @when(s != layer)
        def _():
            out_ship(mb).start()

    def norm_part(v):
        layer = 1 - v // count
        mb = lax.rem(v, count)
        u = layer * count + mb
        for j in range(n - 1):
            gather(v, j, froms[j]).wait_recv()
        gn = ag[mb, :, :model].astype(F32)
        scale = jnp.sum(normed[u, HALO:, model:].astype(F32), axis=1, keepdims=True)
        gain = pr[layer, 0:1]

        def rest(h_in, grad_out):
            x = gn * gain
            dots = jnp.sum(x * h_in, axis=1, keepdims=True)
            gin[v] = grad_out + x * scale - h_in * (scale * scale * scale * dots / model)
            table[layer, 0:1] += jnp.sum(gn * h_in * scale, axis=0, keepdims=True)

        @when(layer == 1)
        def _():
            h_in = normed[u, HALO:, :model].astype(F32) / (scale * gain)
            rest(h_in, gin[mb] * wide_copy(pad[mb], model))
            send_layer(0, mb, h_in, h_in - gin[mb + count])

        @when(layer == 0)
        def _():
            rest(gin[v], gin[mb])

        @when(s == layer)
        def _():
            ship_local(v).start()

        @when(s != layer)
        def _():
            ship(v).start()

        grad_w = mm_tn(normed[u, HALO:, :model], ag[mb, :, model:])

        @when(mb == 0)
        def _():
            gwb[...] = grad_w

        @when(mb > 0)
        def _():
            gwb[...] += grad_w

        @when(mb == count - 1)
        def _():
            base = model + inner
            deep = 2 * state
            for k in range(model // deep):
                cut = slice(k * deep, (k + 1) * deep)
                big[layer, base : base + deep, cut] = gwb[cut].astype(TOTAL_T)

            @when(s == 0)
            def _():
                start_cross(layer, (model + inner) // CHUNK - chunks, chunks)

    def dots(w, j):
        return remote(
            dsend.at[w], drecv.at[w, j], d_s.at[w, j], d_r.at[w, j], (s, q, peers[j])
        )

    def gate_forward(mb, layer):
        gate = z[mb]
        sig = sigmoid(gate)
        silu = gate * sig
        ssd = yn[mb] + pr[layer, 8:9, :inner] * co[mb, :, :inner].astype(F32)
        return gate, sig, silu, ssd, ssd * silu

    def out_b(layer, mb):
        live = jnp.where(layer == 1, pad[mb], jnp.ones((tokens, LANES), F32))
        return (gin[mb] * wide_copy(live, model)).astype(BF)

    def gate_first(w):
        layer = 1 - w // count
        mb = lax.rem(w, count)
        u = layer * count + mb

        grad_gn = mm_nt(out_b(layer, mb), wo[...])
        ggn[...] = grad_gn
        gated = gate_forward(mb, layer)[-1]
        ones = jnp.ones((8, inner), BF)
        dsend[w] = fine(
            lambda a, b: mm_nt(b, a), grad_gn * gated * pr[layer, 9:10, :inner], ones
        )
        for j in range(n - 1):
            dots(w, j).start()

    def conv_slope(w):
        mb = lax.rem(w, count)
        raw_f[...] = raw[mb].astype(F32)
        same = same_rows(seg, mb, tokens)
        prm = pr[1 - w // count]
        for col in range(0, wide, LANES):
            pre = convolved(raw_f, same, prm, col, tokens)
            sig = sigmoid(pre)
            gconv[:, col : col + LANES] = sig * (1.0 + pre * (1.0 - sig))

    def gate_part(w):
        layer = 1 - w // count
        mb = lax.rem(w, count)
        u = layer * count + mb
        total = dsend[w]
        for j in range(n - 1):
            dots(w, j).wait_recv()
            total = total + drecv[w, j]
        across = mm_tn(total * 0.125, jnp.ones((8, LANES), F32), HIGH)
        scale = gsc[mb]
        scale_x = wide_copy(scale, inner)
        gate, sig, silu, ssd, gated = gate_forward(mb, layer)
        grad_gn = ggn[...]
        values = co[mb, :, :inner].astype(F32)
        gain = pr[layer, 9:10, :inner]
        scaled = gated * scale_x
        grad_gated = grad_gn * (gain * scale_x) - scaled * wide_copy(
            scale * scale * across / full, inner
        )
        gy = (grad_gated * silu).astype(BF)
        gy_s[...] = gy
        gz[mb] = (grad_gated * ssd * (sig * (1.0 + gate * (1.0 - sig)))).astype(BF)
        ng[mb] = (scaled * gain).astype(BF)
        gy_f = gy.astype(F32)
        table[layer, 8:9, :inner] += jnp.sum(grad_gn * scaled, axis=0, keepdims=True)
        table[layer, 9:10, :inner] += jnp.sum(gy_f * values, axis=0, keepdims=True)
        entry, _ = gains(cum[mb], seg, mb)
        read = expand(entry, matrix) * gy_f
        back[...] = fine(mm_tn, read, co[mb, :, inner + state :])

        @when(q == seqs - 1)
        def _():
            pass_state(w, u)

    def pass_state(w, u):
        per = inner // heads
        for k in range(PIECES):
            @when(q < seqs - 1)
            def _():
                chain(w, k).wait_recv()

            @when(q == seqs - 1)
            def _():
                nxt[w, k * piece : (k + 1) * piece] = jnp.zeros((piece, LANES), BF)

            @when(q > 0)
            def _():
                @when(w >= count)
                def _():
                    chain(w - count, k).wait_send()

                for i in range(k * heads // PIECES, (k + 1) * heads // PIECES):
                    cut = slice(i * per, (i + 1) * per)
                    sbuf[slot(w), cut] = (
                        car[u, i : i + 1] * nxt[w, cut].astype(F32) + back[cut]
                    ).astype(BF)
                chain(w, k).start()

    def local_part(w):
        layer = 1 - w // count
        mb = lax.rem(w, count)
        u = layer * count + mb
        prm = pr[layer]
        cum_u, dt_u = cum[mb], dt[mb]
        cum_t = cum_u.T
        entry, decay_end = gains(cum_u, seg, mb)
        values = co[mb, :, :inner]
        in_b = co[mb, :, inner : inner + state]
        in_c = co[mb, :, inner + state :]
        gy = gy_s[...]
        gy_f = gy.astype(F32)
        causal = causal_mask(seg, srow, mb, tokens, True)
        inner_bc = jnp.where(causal, mm_nt(in_b, in_c), 0.0)
        lane = iota((tokens, LANES), 1)
        mid = tokens // 2
        blocks = [(slice(0, mid), slice(0, tokens)), (slice(mid, tokens), slice(mid, tokens))]
        grad_inners = [jnp.zeros((mid, to.stop - to.start), F32) for _, to in blocks]
        grad_dts = [jnp.zeros((mid, LANES), F32) for _ in blocks]
        locals_, rows_ = [], []
        for pair in range(heads // 2):
            cols = slice(pair * LANES, (pair + 1) * LANES)
            totals = [jnp.zeros((mid, LANES), F32) for _ in blocks]
            for j in range(2):
                head = 2 * pair + j
                one = slice(head, head + 1)
                mask = jnp.right_shift(lane, HEAD_SHIFT) == j
                gy_one = jnp.where(mask, gy[:, cols], jnp.zeros((), BF))
                downs = []
                for i, (of, to) in enumerate(blocks):
                    dt_col = dt_u[of, one]
                    decay = jnp.exp(jnp.minimum(cum_t[one, to] - cum_u[of, one], 0.0))
                    grad_mix = mm_nt(values[of, cols], gy_one[to])
                    mixed = inner_bc[of, to] * decay
                    totals[i] = totals[i] + mm((mixed * dt_col).astype(BF), gy_one[to])
                    grad_inners[i] = grad_inners[i] + grad_mix * (decay * dt_col)
                    weighted = grad_mix * mixed
                    sums = jnp.sum(weighted, axis=1, keepdims=True)
                    grad_dts[i] = jnp.where(lane[:mid] == head, sums, grad_dts[i])
                    downs.append(jnp.sum(weighted * dt_col, axis=0, keepdims=True))
                rows_.append(
                    jnp.concatenate([downs[0][:, :mid], downs[0][:, mid:] + downs[1]], axis=1)
                )
            locals_.append(jnp.concatenate(totals, axis=0))
            tick(w, 3 + pair, 1)

        @when(w > 0)
        def _():
            finish(w - 1)

        tick(w, 7, 1)

        @when(q < seqs - 1)
        def _():
            pass_state(w, u)

        grad_inners = [
            jnp.where(causal[of, to], x, 0.0) for x, (of, to) in zip(grad_inners, blocks)
        ]
        grad_dt = jnp.concatenate(grad_dts, axis=0)
        toward = decay_end * dt_u
        toward_x = expand(toward, matrix)
        values_f = values.astype(F32)
        pulled = mm_nt(in_b, nxt[w])
        gconv[:, :inner] *= (
            prm[8:9, :inner] * gy_f + jnp.concatenate(locals_, axis=1) + toward_x * pulled
        )
        read = expand(entry, matrix) * gy_f
        from_row = (iota((heads, LANES), 0) == iota((heads, LANES), 1)).astype(F32)
        grad_cum = (
            mm_tn(jnp.concatenate(rows_, axis=0), from_row, HIGH)
            - dt_u * grad_dt
            + head_sums(read * mm_nt(in_c, st[mb]), matrix)
        )
        pulled_sums = head_sums(values_f * pulled, matrix)
        grad_dt = grad_dt + pulled_sums * decay_end
        high, low = split(nxt[w].astype(F32) * st[mb].astype(F32))
        carried = jnp.sum(
            lax.dot_general(high, matrix, (((0,), (1,)), ((), ())), preferred_element_type=F32)
            + lax.dot_general(low, matrix, (((0,), (1,)), ((), ())), preferred_element_type=F32),
            axis=0,
            keepdims=True,
        )
        ahead = (iota((tokens, tokens), 0) > iota((tokens, tokens), 1)).astype(F32)
        grad_rate = (
            mm_tn(lower(tokens), grad_cum, HIGH)
            + mm(ahead, pulled_sums * toward, HIGH)
            + carried * entry[-1:]
        )
        neg = prm[7:8, :LANES]
        grad_pre = (grad_dt + grad_rate * neg) * sigmoid(dtp[mb])
        table[layer, 6:7, :LANES] += jnp.sum(grad_pre, axis=0, keepdims=True)
        table[layer, 7:8, :LANES] += jnp.sum(grad_rate * dt_u * neg, axis=0, keepdims=True)
        grad_raw_dt = grad_pre.astype(BF)
        gdr[mb] = grad_raw_dt
        gconv[:, inner : inner + state] *= jnp.concatenate(
            [fine(mm, x, in_c[to]) for x, (of, to) in zip(grad_inners, blocks)], axis=0
        ) + fine(mm, values_f * toward_x, nxt[w])
        first_c = fine(mm_tn, grad_inners[0], in_b[:mid])
        second_c = first_c[mid:] + fine(mm_tn, grad_inners[1], in_b[mid:])
        gconv[:, inner + state :] *= jnp.concatenate([first_c[:mid], second_c], axis=0) + fine(
            mm, read, st[mb]
        )
        same = same_rows(seg, mb, tokens)
        first = HALO - KC + 1
        shift[:HALO] = jnp.zeros((HALO, LANES), F32)
        shift[ext:] = jnp.zeros((HALO, LANES), F32)
        for col in range(0, wide, LANES):
            cols = slice(col, col + LANES)
            grad = gconv[:, cols]
            target = table if col < inner else small
            off = col if col < inner else col - inner
            tc = slice(off, off + LANES)
            target[layer, 5:6, tc] += jnp.sum(grad, axis=0, keepdims=True)
            total = jnp.zeros((ext, LANES), F32)
            for k in range(KC):
                masked = grad * same[k]
                target[layer, 1 + k : 2 + k, tc] += jnp.sum(
                    masked * raw_f[first + k : first + k + tokens, cols], axis=0, keepdims=True
                )
                shift[HALO:ext] = masked * prm[1 + k : 2 + k, cols]
                total = total + shift[KC - 1 - k : KC - 1 - k + ext]
            gext[mb, :, cols] = total.astype(BF)
            if col == wide // 2:
                tick(w, 8, 1)
        grad_raw = gext[mb]
        main = mm_nt(gz[mb], wc[:, :inner]) + mm_nt(
            grad_raw_dt, wc[:, inner + wide :]
        )
        rest = mm_nt(grad_raw, wc[:, inner : inner + wide])
        part[mb, :, :model] = (main + rest[HALO:]).astype(BF)
        hpart[w, :, :model] = rest[:HALO].astype(BF)
        part[mb, :, model:] = grad_raw[HALO:, inner:]
        hpart[w, :, model:] = grad_raw[:HALO, inner:]

    def finish(w):
        acc[...] = part[slot(w), at_rows(h)].astype(F32)
        for j in range(n - 1):
            scatter(w, j).wait_recv()
            acc[...] += rbuf[slot(w), j].astype(F32)

        @when(both(edge_owner, w < steps))
        def _():
            for head in range(n):
                edge(w, head).wait_recv()
                acc[rows - HALO :] += hbuf[w, head].astype(F32)

        ag[slot(w), at_rows(h)] = acc[...].astype(BF)
        for j in range(n - 1):
            gather(w, j, h).start()

    def weights_part(layer):
        gate_w = jnp.zeros((inner, model), F32)
        z_w = jnp.zeros((model, inner), F32)
        x_w = jnp.zeros((model, inner), F32)
        dt_w = jnp.zeros((LANES, model), F32)
        for mb in range(count):
            x = normed[layer * count + mb, :, :model]
            gate_w = gate_w + mm_tn(ng[mb], out_b(layer, mb))
            z_w = z_w + mm_tn(x[HALO:], gz[mb])
            x_w = x_w + mm_tn(x, gext[mb, :, :inner])
            dt_w = dt_w + mm_tn(gdr[mb], x[HALO:])
        big[layer, :model, :inner] = z_w.astype(TOTAL_T)
        big[layer, :model, inner:] = x_w.astype(TOTAL_T)
        big[layer, model : model + inner] = gate_w.astype(TOTAL_T)
        table[layer, 16:24] = dt_w[:8]
        for j in range(n - 1):
            little(layer, j).start()

        @when(s == 0)
        def _():
            start_cross(layer, 0, (model + inner) // CHUNK - chunks)

        @when(s == 1)
        def _():
            start_cross(layer, 0, chunks)

    chunks = big.shape[1] // (2 * CHUNK)
    spot = s * (seqs - 1) + (1 - 2 * s) * q
    way = 1 - 2 * s
    has_prev, has_next = spot > 0, spot < seqs - 1
    delays = [(SKEW, SKEW), (SKEW + LEAD * (1 - s), SKEW + LEAD * s)]

    def span(base, c):
        return pl.ds(pl.multiple_of(base + c * CHUNK, CHUNK), CHUNK)

    def cross_at(layer, c):
        k = layer * chunks + c
        return remote(
            big.at[layer, span((1 - s) * chunks * CHUNK, c)],
            pbuf.at[layer, span(0, c)], x_s.at[k], x_r.at[k], other,
        )

    def start_cross(layer, low, high):
        def one(c, _):
            cross_at(layer, c).start()
            return 0

        lax.fori_loop(low, high, one, 0)

    def work(layer, c):
        mine = one_if(s == layer)
        return span((mine * s + 2 * (1 - mine)) * chunks * CHUNK, c)

    def along(layer, c):
        k = layer * chunks + c
        return remote(
            big.at[layer, span(s * chunks * CHUNK, c)], out.at[work(layer, c)],
            a_s.at[k], a_r.at[k], (s, q + way, h),
        )

    def home(layer, c):
        k, at = layer * chunks + c, work(layer, c)
        return remote(out.at[at], out.at[at], b_s.at[k], b_r.at[k], (s, q - way, h))

    def deliver(layer, c):
        return remote(
            out.at[work(layer, c)], out.at[span(s * chunks * CHUNK, c)], e_s.at[c], e_r.at[c],
            other,
        )

    def settled(layer, c):
        @when(has_prev)
        def _():
            home(layer, c).start()

        @when(s != layer)
        def _():
            deliver(layer, c).start()

    def advance(layer, t):
        outward, inward = delays[layer]
        c = t - outward * spot

        @when(both(c >= 0, c < chunks))
        def _():
            at = span(s * chunks * CHUNK, c)
            cross_at(layer, c).wait_recv()
            sums = big[layer, at].astype(F32) + pbuf[layer, span(0, c)].astype(F32)

            @when(has_prev)
            def _():
                along(layer, c).wait_recv()
                big[layer, at] = (sums + out[work(layer, c)].astype(F32)).astype(TOTAL_T)

            @when(jnp.logical_not(has_prev))
            def _():
                big[layer, at] = sums.astype(TOTAL_T)

            @when(has_next)
            def _():
                along(layer, c).start()

            @when(jnp.logical_not(has_next))
            def _():
                out[work(layer, c)] = big[layer, at]
                settled(layer, c)

        e = t - outward * (seqs - 1) - inward * (seqs - 1 - spot)

        @when(both(has_next, both(e >= 0, e < chunks)))
        def _():
            home(layer, e).wait_recv()
            settled(layer, e)

    def tick(w, offset, amount):
        @when(w >= count)
        def _():
            def one(i, _):
                advance(1, (w - count) * TICKS + offset + i)
                return 0

            lax.fori_loop(0, amount, one, 0)

    def late_tick(t, _):
        advance(0, t)
        advance(1, t + count * TICKS)
        return 0

    def tail_tick(w, offset, amount):
        first = (w - steps) * TAIL_TICKS + offset
        lax.fori_loop(first, first + amount, late_tick, 0)

    table[...] = jnp.zeros_like(table)
    small[...] = jnp.zeros_like(small)
    loads[0].wait()

    def step(w, _):
        @when(w < steps)
        def _():
            for load in stream(w):
                load.wait()

        @when(w + 1 < steps)
        def _():
            for load in stream(w + 1):
                load.start()

        @when(w == 1)
        def _():
            for load in loads[1:]:
                load.wait()

        @when(w >= count)
        def _():
            norm_part(w - count)

        @when(w >= steps)
        def _():
            tail_tick(w, 0, TAIL_TICKS // 2)

            @when(w == steps)
            def _():
                finish(w - 1)

            tail_tick(w, TAIL_TICKS // 2, TAIL_TICKS - TAIL_TICKS // 2)

        @when(w < steps)
        def _():
            tick(w, 0, 1)

            @when(both(lax.rem(w, count) == 0, w < steps))
            def _():
                wo_load(0).wait()

            gate_first(w)

            @when(w == count - 1)
            def _():
                wo_load(0).start()

            tick(w, 1, 1)
            conv_slope(w)
            tick(w, 2, 1)
            gate_part(w)

            @when(w >= count)
            def _():
                for j in range(n - 1):
                    scatter(w - count, j).wait_send()
                    gather(w - count, j, h).wait_send()

            @when(lax.rem(w, count) == 0)
            def _():
                wc_load(0).wait()

            local_part(w)

            @when(w == count - 1)
            def _():
                wc_load(0).start()

            @when(q > 0)
            def _():
                edge(w, h).start()

            for j in range(n - 1):
                scatter(w, j).start()

            tick(w, 9, 1)

            @when(lax.rem(w, count) == count - 1)
            def _():
                weights_part(1 - w // count)

        return 0

    lax.fori_loop(0, steps + count, step, 0)

    def settle_sends(mb, _):
        for j in range(n - 1):
            scatter(mb + count, j).wait_send()
            gather(mb + count, j, h).wait_send()
        load_part(mb).start()
        return 0

    def load_part(mb):
        return pltpu.make_async_copy(
            part_in.at[mb], part.at[mb, :, pl.ds(0, model)], p_s.at[mb]
        )

    lax.fori_loop(0, count, settle_sends, 0)
    for mb in range(count):
        load_part(mb).wait()
        for j in range(n - 1):
            branch_scatter(mb, j).start()
    tail_tick(steps + count, 0, TAIL_TICKS)

    def finish_branch(mb, _):
        total = part[mb, at_rows(h), :model].astype(F32)
        for j in range(n - 1):
            branch_scatter(mb, j).wait_recv()
            total = total + rbuf[mb, j, :, :model].astype(F32)
        ag[mb, at_rows(h), :model] = total.astype(BF)
        for j in range(n - 1):
            branch_gather(mb, j, h).start()
        return 0

    lax.fori_loop(0, count, finish_branch, 0)
    tail_tick(steps + count + 1, 0, TAIL_TICKS)

    def last_layer(mb, _):
        @when(s == 0)
        def _():
            out_local(mb).wait()

        @when(s == 1)
        def _():
            out_ship(mb).wait_send()

        for j in range(n - 1):
            branch_gather(mb, j, froms[j]).wait_recv()
        u = count + mb
        scale = jnp.sum(normed[u, HALO:, model:].astype(F32), axis=1, keepdims=True)
        h_in = normed[u, HALO:, :model].astype(F32) / (scale * pr[1, 0:1])
        branch = ag[mb, :, :model].astype(F32)
        send_layer(1, mb, h_in + branch, branch)
        return 0

    lax.fori_loop(0, count, last_layer, 0)

    def drain(w, _):
        @when(both(w >= count, q > 0))
        def _():
            for k in range(PIECES):
                chain(w, k).wait_send()

        @when(w < count)
        def _():
            for j in range(n - 1):
                branch_scatter(w, j).wait_send()
                branch_gather(w, j, h).wait_send()

        for j in range(n - 1):
            dots(w, j).wait_send()

        @when(q > 0)
        def _():
            edge(w, h).wait_send()

        return 0

    lax.fori_loop(0, steps, drain, 0)
    for layer in range(2):
        total = small[layer]
        for j in range(n - 1):
            little(layer, j).wait_recv()
            total = total + srecv[layer, j]
        for j in range(n - 1):
            little(layer, j).wait_send()
        table[layer, 1:6, inner : inner + 2 * state] = total[1:6]
    small_cross = remote(table.at[1 - s], ps, t_s.at[0], t_r.at[0], other)
    small_along = remote(ts, rs_, t_s.at[1], t_r.at[1], (s, q + 1, h))
    small_home = remote(small_o, small_o, t_s.at[2], t_r.at[2], (s, q - 1, h))
    small_cross.start()
    done = (count + 2) * TAIL_TICKS
    first_end = chunks + 2 * SKEW * (seqs - 1)
    second_end = chunks + (2 * SKEW + LEAD) * (seqs - 1) - count * TICKS
    last = max(first_end, second_end, done + 2 * SKEW * (seqs - 1) + 1)
    back_at = done + SKEW * (2 * (seqs - 1) - q)

    def last_tick(t, _):
        @when(t == done + SKEW * q)
        def _():
            small_cross.wait_recv()
            ts[...] = table[s] + ps[...]

            @when(q > 0)
            def _():
                small_along.wait_recv()
                ts[...] += rs_[...]

            @when(q < seqs - 1)
            def _():
                small_along.start()

            @when(q == seqs - 1)
            def _():
                small_o[...] = ts[...]

                @when(q > 0)
                def _():
                    small_home.start()

        @when(both(t == back_at, q < seqs - 1))
        def _():
            small_home.wait_recv()

            @when(q > 0)
            def _():
                small_home.start()

        return late_tick(t, _)

    lax.fori_loop(done, last, last_tick, 0)

    def drain_sum(c, _):
        for layer in range(2):
            cross_at(layer, c).wait_send()

            @when(has_next)
            def _():
                along(layer, c).wait_send()

            @when(has_prev)
            def _():
                home(layer, c).wait_send()

            @when(s != layer)
            def _():
                deliver(layer, c).wait_send()

        remote(
            out.at[work(0, c)], out.at[span((1 - s) * chunks * CHUNK, c)], e_s.at[c], e_r.at[c],
            other,
        ).wait_recv()
        return 0

    lax.fori_loop(0, chunks, drain_sum, 0)
    small_cross.wait_send()

    @when(q < seqs - 1)
    def _():
        small_along.wait_send()

    @when(q > 0)
    def _():
        small_home.wait_send()

    def drain_out(mb, _):
        ship_local(mb).wait()
        ship(mb).wait_send()
        remote(
            gin.at[mb], ig.at[(1 - s) * count + mb], l_s.at[mb], l_r.at[mb], other
        ).wait_recv()

        @when(s == 1)
        def _():
            out_local(mb).wait()

        @when(s == 0)
        def _():
            out_ship(mb).wait_send()

        remote(
            lo_s.at[mb], lo.at[(1 - s) * count + mb], k_s.at[mb], k_r.at[mb], other
        ).wait_recv()
        return 0

    lax.fori_loop(0, count, drain_out, 0)


def pad_lanes(a, width):
    return jnp.pad(a, ((0, 0), (0, width - a.shape[1])))


def final_kernel(zx, wo, bc, table, lo, ig, g_zx, g_wo, g_bc, lo_o, ig_o, rms, g_norm, g_dt, g_cx, g_cxb, g_cb, g_cbb,
                 g_dtb, g_al, g_sk, g_gate):
    inner = g_zx.shape[3]
    model = table.shape[1]
    heads = g_dtb.shape[1]
    step = pl.program_id(0)
    g_zx[0, :, 0, :] = zx[:, :inner].astype(F32)
    g_zx[0, :, 1, :] = zx[:, inner:].astype(F32)
    g_wo[0] = wo[...].astype(F32)
    lo_o[0] = lo[...]
    ig_o[0] = ig[...]

    @when(step == 0)
    def _():
        deep = g_bc.shape[2]
        for k in range(model // deep):
            cut = slice(k * deep, (k + 1) * deep)
            g_bc[0, cut] = bc[:, cut].astype(F32)
        live = table[26:27, :LANES] * model
        first = jnp.sqrt(table[24:25, :LANES] / live)
        second = jnp.sqrt(table[25:26, :LANES] / live)
        rms[...] = jnp.where(iota((1, LANES), 1) == 0, first, second)[:, :2]
        g_norm[...] = table[0:1]
        g_dt[0] = table[16 : 16 + heads]
        g_cx[0] = table[1:5, :inner]
        g_cxb[...] = table[5:6, :inner]
        g_cb[0] = table[1:5, inner : inner + deep]
        g_cbb[...] = table[5:6, inner : inner + deep]
        g_dtb[...] = table[6:7, :heads]
        g_al[...] = table[7:8, :heads]
        sums = mm(table[8:16, :inner], spread_matrix(inner).astype(F32).T, HIGH)
        g_sk[...] = sums[1:2, :heads]
        g_gate[...] = table[8:9, :inner]


def finalize(big, table, lo, ig, inner, heads, state):
    model = big.shape[1]
    steps = lo.shape[0]
    each = (1,) + lo.shape[1:]
    deep = 2 * state

    def whole(shape):
        return pl.BlockSpec(shape, lambda i: (0,) * len(shape))

    shapes = [
        (1, model, 2, inner), (1, inner, model), (1, model, deep), (1,) + lo.shape,
        (1,) + ig.shape, (1, 2), (1, model),
        (1, heads, model), (1, 4, inner), (1, inner), (1, 4, deep), (1, deep),
        (1, heads), (1, heads), (1, heads), (1, inner),
    ]
    specs = [
        pl.BlockSpec((1, model // steps, 2, inner), lambda i: (0, i, 0, 0)),
        pl.BlockSpec((1, inner // steps, model), lambda i: (0, i, 0)),
        whole(shapes[2]),
        pl.BlockSpec((1,) + each, lambda i: (0, i, 0, 0)),
        pl.BlockSpec((1,) + each, lambda i: (0, i, 0, 0)),
    ] + [whole(x) for x in shapes[5:]]
    base = model // (inner // steps)
    return pl.pallas_call(
        final_kernel,
        grid=(steps,),
        in_specs=[
            pl.BlockSpec((model // steps, model), lambda i: (i, 0)),
            pl.BlockSpec((inner // steps, model), lambda i: (base + i, 0)),
            pl.BlockSpec((deep, model), lambda i: ((model + inner) // deep, 0)),
            whole(table.shape),
            pl.BlockSpec(each, lambda i: (i, 0, 0)),
            pl.BlockSpec(each, lambda i: (i, 0, 0)),
        ],
        out_specs=specs,
        out_shape=[jax.ShapeDtypeStruct(x, F32) for x in shapes],
        compiler_params=pltpu.CompilerParams(vmem_limit_bytes=LIMIT),
        name="final",
    )(big, big, big, table, lo, ig)


def local(hidden_in, cotangent, segments, padding, norm_gain, w_zx, w_bc, w_dt, conv_x,
          conv_x_bias, conv_bc, conv_bc_bias, dt_bias, a_log, skip_d, gate_gain, w_out):
    s, q, h = place()
    seqs = lax.axis_size(SEQ)
    n = lax.axis_size(HEAD)
    sections = lax.axis_size(SEC)
    batches, tokens, model = hidden_in.shape
    count = batches // sections
    inner = w_out.shape[1]
    heads = w_dt.shape[2]
    state = w_bc.shape[2] // 2
    wide = inner + 2 * state
    wc = jnp.concatenate(
        [w_zx[0].reshape(model, 2 * inner), w_bc[0], pad_lanes(w_dt[0], LANES)], axis=1
    )
    units = 2 * count
    rows = tokens + HALO
    part_rows = tokens // n
    lane_shape = (units, tokens, LANES)
    inner_shape = (units, tokens, inner)
    state_shape = (units, inner, LANES)
    peer_sems = DMA((units, n - 1))
    out_shape = ((batches, tokens, model), F32)
    kept_shapes = [
        ((units, rows, model + LANES), BF),
        ((units, rows, wide), BF),
        (inner_shape, F32),
        (lane_shape, F32),
        (lane_shape, F32),
        (lane_shape, F32),
        ((units, tokens, wide), BF),
        (state_shape, BF),
        (inner_shape, F32),
        (lane_shape, F32),
        ((count, tokens, model), BF),
        ((2,) + wc.shape, BF),
        ((2,) + w_out.shape[1:], BF),
    ]
    car, pr, seg_col, srow, pad, *kept = comm(
        functools.partial(fwd_kernel, seqs, n),
        (hidden_in, segments, padding, norm_gain, conv_x, conv_x_bias, conv_bc, conv_bc_bias,
         dt_bias, a_log, skip_d, gate_gain, wc, w_out[0]),
        [
            ((units, heads, LANES), F32),
            ((2, 16, model), F32),
            ((count, rows, LANES), F32),
            ((count, 8, tokens), F32),
            ((count, tokens, LANES), F32),
        ]
        + kept_shapes,
        [pltpu.VMEM(*x) for x in kept_shapes]
        + [
            pltpu.VMEM((count, HALO, model), F32),
            pltpu.VMEM((count, HALO, LANES), F32),
            pltpu.VMEM((16, model), F32),
            pltpu.VMEM((count, tokens, model), F32),
            pltpu.VMEM((rows, wide), F32),
            pltpu.VMEM((inner, LANES), F32),
            pltpu.VMEM(state_shape, BF),
            pltpu.VMEM((tokens, inner), F32),
            pltpu.VMEM((count, tokens, model), BF),
            pltpu.VMEM((count, n - 1, part_rows, model), BF),
            pltpu.VMEM((units, 8, tokens), F32),
            pltpu.VMEM((units, n - 1, 8, tokens), F32),
            DMA((units, PIECES)), DMA((units, PIECES)),
            peer_sems, peer_sems, peer_sems, peer_sems, peer_sems, peer_sems,
            DMA((count, n)), DMA((count,)), DMA((1,)),
            DMA((5,)), DMA((5,)), DMA((11, units)), DMA((2, 2)),
        ],
        1, "fwd", len(kept_shapes), 1,
    )
    normed, raw, z, dtp, dt, cum, co, st, yn, gsc, part, wc, wo = kept
    total_rows = model + inner + 2 * state
    chunk_sems = DMA((total_rows // CHUNK,))
    more_sems = DMA((units + count, n - 1))
    table_shape = (32, model)
    grad_shape = (tokens, model + 2 * state)
    big, table, input_grad, layer_out = comm(
        functools.partial(bwd_kernel, seqs, n),
        (cotangent, hidden_in, normed, wc, wo, raw, z, dtp, dt, cum, co, st, yn, gsc,
         part, pad, car, seg_col, srow, pr),
        (((total_rows * 3 // 2, model), TOTAL_T), (table_shape, F32), out_shape, out_shape),
        [
            pltpu.VMEM((units, tokens, model), F32),
            pltpu.VMEM((count, tokens, model), F32),
            pltpu.VMEM((units, rows, model + LANES), BF),
            pltpu.VMEM(wc.shape[1:], BF),
            pltpu.VMEM(wo.shape[1:], BF),
            pltpu.VMEM((count, rows, wide), BF),
            pltpu.VMEM((count, tokens, inner), F32),
            pltpu.VMEM((count, tokens, LANES), F32),
            pltpu.VMEM((count, tokens, LANES), F32),
            pltpu.VMEM((count, tokens, LANES), F32),
            pltpu.VMEM((count, tokens, wide), BF),
            pltpu.VMEM((count, inner, LANES), BF),
            pltpu.VMEM((count, tokens, inner), F32),
            pltpu.VMEM((count, tokens, LANES), F32),
            pltpu.VMEM((2, total_rows, model), TOTAL_T),
            pltpu.VMEM((2, total_rows // 2, model), TOTAL_T),
            pltpu.VMEM((2,) + table_shape, F32),
            pltpu.VMEM(table_shape, F32),
            pltpu.VMEM(table_shape, F32),
            pltpu.VMEM(table_shape, F32),
            pltpu.VMEM((rows, wide), F32),
            pltpu.VMEM((rows + HALO, LANES), F32),
            pltpu.VMEM((tokens, wide), F32),
            pltpu.VMEM((count, rows, wide), BF),
            pltpu.VMEM((count, tokens, inner), BF),
            pltpu.VMEM((tokens, inner), BF),
            pltpu.VMEM((count, tokens, inner), BF),
            pltpu.VMEM((count, tokens, LANES), BF),
            pltpu.VMEM((inner, LANES), F32),
            pltpu.VMEM(state_shape, BF),
            pltpu.VMEM((count, inner, LANES), BF),
            pltpu.VMEM((count,) + grad_shape, BF),
            pltpu.VMEM((units, HALO, model + 2 * state), BF),
            pltpu.VMEM((count, n - 1, part_rows, model + 2 * state), BF),
            pltpu.VMEM((units, n, HALO, model + 2 * state), BF),
            pltpu.VMEM((part_rows, model + 2 * state), F32),
            pltpu.VMEM((count,) + grad_shape, BF),
            pltpu.VMEM((model, 2 * state), F32),
            pltpu.VMEM((2, 8, 2 * state), F32),
            pltpu.VMEM((2, n - 1, 8, 2 * state), F32),
            pltpu.VMEM((tokens, inner), F32),
            pltpu.VMEM((units, 8, tokens), F32),
            pltpu.VMEM((units, n - 1, 8, tokens), F32),
            DMA((units, PIECES)), DMA((units, PIECES)),
            more_sems, more_sems, more_sems, more_sems,
            DMA((units,)), DMA((units, n)),
            DMA((2, n - 1)), DMA((2, n - 1)),
            DMA((count,)), DMA((count,)), DMA((count,)), DMA((3,)),
            peer_sems, peer_sems,
            DMA((9, count)), DMA((2,)),
            chunk_sems, chunk_sems, chunk_sems, chunk_sems, chunk_sems, chunk_sems,
            DMA((3,)), DMA((3,)), DMA((count,)), DMA((count,)), DMA((count,)),
            DMA((total_rows // CHUNK // 2,)), DMA((total_rows // CHUNK // 2,)), DMA((count,)),
        ],
        2, "bwd", 2, 15,
    )
    (g_zx, g_wo, g_bc, layer_out, input_grad, rms, g_norm, g_dt, g_cx, g_cxb, g_cb, g_cbb, g_dtb, g_al, g_sk,
     g_gate) = finalize(
        big, table, layer_out, input_grad, inner, heads, state
    )
    return (layer_out, input_grad, rms, g_norm, g_zx, g_bc,
            jnp.transpose(g_dt, (0, 2, 1)), g_cx, g_cxb,
            g_cb, g_cbb, g_dtb, g_al, g_sk, g_gate, g_wo)


def solution(mesh):
    in_specs = (
        P(None, SEQ, None),
        P(None, SEQ, None),
        P(None, SEQ),
        P(None, SEQ),
        P(SEC, None),
        P(SEC, None, None, HEAD),
        P(SEC, None, None),
        P(SEC, None, HEAD),
        P(SEC, None, HEAD),
        P(SEC, HEAD),
        P(SEC, None, None),
        P(SEC, None),
        P(SEC, HEAD),
        P(SEC, HEAD),
        P(SEC, HEAD),
        P(SEC, HEAD),
        P(SEC, HEAD, None),
    )
    out_specs = (
        P(SEC, None, SEQ, None),
        P(SEC, None, SEQ, None),
        P(SEC, None),
        P(SEC, None),
        P(SEC, None, None, HEAD),
        P(SEC, None, None),
        P(SEC, None, HEAD),
        P(SEC, None, HEAD),
        P(SEC, HEAD),
        P(SEC, None, None),
        P(SEC, None),
        P(SEC, HEAD),
        P(SEC, HEAD),
        P(SEC, HEAD),
        P(SEC, HEAD),
        P(SEC, HEAD, None),
    )
    return jax.shard_map(local, mesh=mesh, in_specs=in_specs, out_specs=out_specs, check_vma=False)
```

```python
import functools

import jax
import jax.numpy as jnp
from jax import lax
from jax.experimental import pallas as pl
from jax.experimental.pallas import tpu as pltpu
from jax.sharding import PartitionSpec as P

SEC, SEQ, HEAD = "section", "seq", "head"
F32, BF = jnp.float32, jnp.bfloat16
MESH = pl.DeviceIdType.MESH
HIGH = lax.Precision.HIGHEST
EPS = 1e-05
KC = 4
HALO = 16
LANES = 128
HEAD_SHIFT = 6
LIMIT = 58 << 20
CHUNK = 64
SKEW = 3
LEAD = 2
TICKS = 10
TAIL_TICKS = 4
PIECES = 4
TOTAL_T = jnp.bfloat16


def mm(a, b, precision=None):
    return lax.dot_general(
        a, b, (((1,), (0,)), ((), ())), precision=precision, preferred_element_type=F32
    )


def mm_nt(a, b):
    return lax.dot_general(a, b, (((1,), (1,)), ((), ())), preferred_element_type=F32)


def mm_tn(a, b, precision=None):
    return lax.dot_general(
        a, b, (((0,), (0,)), ((), ())), precision=precision, preferred_element_type=F32
    )


def iota(shape, dim):
    return lax.broadcasted_iota(jnp.int32, shape, dim)


def spread_matrix(width):
    shape = (LANES, width)
    return (iota(shape, 0) == jnp.right_shift(iota(shape, 1), HEAD_SHIFT)).astype(BF)


def split(x):
    high = x.astype(BF)
    return high, (x - high.astype(F32)).astype(BF)


def expand(x, matrix):
    high, low = split(x)
    return mm(high, matrix) + mm(low, matrix)


def head_sums(x, matrix):
    high, low = split(x)
    return mm_nt(high, matrix) + mm_nt(low, matrix)


def fine(product, a, b):
    high, low = split(a)
    return product(high, b) + product(low, b)


def two_lanes(column):
    high = column.astype(BF).astype(F32)
    lane = iota((column.shape[0], LANES), 1)
    return jnp.where(lane == 0, high, jnp.where(lane == 1, column - high, 0.0)).astype(BF)


def sigmoid(v):
    return 1.0 / (1.0 + jnp.exp(-v))


def lower(size):
    return (iota((size, size), 0) >= iota((size, size), 1)).astype(F32)


def same_rows(seg_ref, mb, tokens):
    mine = seg_ref[mb, HALO:]
    first = HALO - KC + 1
    return [
        (seg_ref[mb, first + k : first + k + tokens] == mine).astype(F32) for k in range(KC)
    ]


def convolved(raw_f, same, prm, col, tokens):
    first = HALO - KC + 1
    cols = slice(col, col + LANES)
    pre = jnp.zeros((tokens, LANES), F32) + prm[5:6, cols]
    for k in range(KC):
        pre = pre + prm[1 + k : 2 + k, cols] * raw_f[first + k : first + k + tokens, cols] * same[k]
    return pre


def gains(cum, seg_ref, mb):
    mine = seg_ref[mb, HALO:]
    before = seg_ref[mb, HALO - 1 : HALO]
    last = mine[-1:]
    entry = jnp.exp(cum) * (mine == before).astype(F32)
    decay_end = jnp.exp(cum[-1:] - cum) * (mine == last).astype(F32)
    return entry, decay_end


def place():
    return lax.axis_index(SEC), lax.axis_index(SEQ), lax.axis_index(HEAD)


def remote(src, dst, send, recv, device):
    return pltpu.make_async_remote_copy(
        src_ref=src, dst_ref=dst, send_sem=send, recv_sem=recv, device_id=device,
        device_id_type=MESH,
    )


def greet(device):
    pl.semaphore_signal(
        pltpu.get_barrier_semaphore(), inc=1, device_id=device, device_id_type=MESH
    )


def await_greets(count):
    pl.semaphore_wait(pltpu.get_barrier_semaphore(), count)


def one_if(condition):
    return condition.astype(jnp.int32)


def comm(kernel, ins, outs, scratch, ident, name, in_hbm=0, from_hbm=0):
    sources = [pl.ANY] * from_hbm + [pltpu.VMEM] * (len(ins) - from_hbm)
    spaces = [pltpu.VMEM] * (len(outs) - in_hbm) + [pl.ANY] * in_hbm
    return pl.pallas_call(
        kernel,
        in_specs=[pl.BlockSpec(memory_space=space) for space in sources],
        out_specs=[pl.BlockSpec(memory_space=space) for space in spaces],
        out_shape=[jax.ShapeDtypeStruct(s, d) for s, d in outs],
        scratch_shapes=scratch,
        compiler_params=pltpu.CompilerParams(
            collective_id=ident, has_side_effects=True, vmem_limit_bytes=LIMIT
        ),
        name=name,
    )(*ins)


DMA = pltpu.SemaphoreType.DMA


def wide_copy(x, width):
    return jnp.concatenate([x] * (width // LANES), axis=1)


def causal_mask(seg_ref, srow_ref, mb, tokens, transposed):
    row = iota((tokens, tokens), 0)
    col = iota((tokens, tokens), 1)
    same = wide_copy(seg_ref[mb, HALO:], tokens) == srow_ref[mb, 0:1]
    return same & ((row <= col) if transposed else (row >= col))


def when(condition):
    return pl.when(condition)


def both(a, b):
    return jnp.logical_and(a, b)


def fwd_kernel(seqs, n, source, segments, padding, norm_gain, conv_x, conv_xb, conv_bc, conv_bcb,
               dt_bias, a_log, skip_d, gate_gain, wc_in, wo_in,
               car, pr, seg, srow, pad, normed_o, raw_o, z_o, dtp_o, dt_o, cum_o, co_o, st_o,
               yn_o, gsc_o, part_o, wc_o, wo_o,
               normed, raw, z, dtp, dt, cum, co, st, yn, gsc, part, wc, wo,
               halo, seg_halo, pr_in, hid, raw_f, con, sbuf, gated_s, part0, rbuf0, ssend, srecv,
               c_s, c_r, q_s, q_r, s_s, s_r, g_s, g_r, h_s, h_r, in_s, w_s, w_r, o_s, v_s):
    s, q, h = place()
    count, tokens, model = hid.shape
    inner = wo.shape[1]
    wide = raw.shape[2]
    heads = inner >> HEAD_SHIFT
    rows = tokens // n
    units = 2 * count
    full = inner * n
    piece = inner // PIECES
    other = (1 - s, q, h)
    first_q, last_q = q == 0, q == seqs - 1
    edge_owner = both(h == n - 1, q < seqs - 1)
    peers = [lax.rem(h + j, n) for j in range(1, n)]
    froms = [lax.rem(h + n - j, n) for j in range(1, n)]
    matrix = spread_matrix(inner)
    load = pltpu.make_async_copy(source.at[pl.ds(s * count, count)], hid, in_s.at[0])
    load.start()
    for p in peers:
        greet((s, q, p))
    greet(other)

    @when(q > 0)
    def _():
        greet((s, q - 1, n - 1))

    @when(both(q > 0, h < n - 1))
    def _():
        greet((s, q - 1, h))

    await_greets(n + one_if(q < seqs - 1) * (1 + (n - 1) * one_if(h == n - 1)))

    def at_rows(owner):
        return pl.ds(pl.multiple_of(owner * rows, rows), rows)

    def slot_rows(owner):
        return pl.ds(pl.multiple_of(HALO + owner * rows, HALO), rows)

    def chain(u, k):
        cut = pl.ds(k * piece, piece)
        return remote(
            sbuf.at[u, cut], st.at[u, cut], c_s.at[u, k], c_r.at[u, k], (s, q + 1, h)
        )

    def squares(u, j):
        return remote(
            ssend.at[u], srecv.at[u, j], q_s.at[u, j], q_r.at[u, j], (s, q, peers[j])
        )

    def scatter(u, j):
        return remote(
            part0.at[u, at_rows(peers[j])], rbuf0.at[u, j], s_s.at[u, j], s_r.at[u, j],
            (s, q, peers[j]),
        )

    def gather(u, j, owner):
        where = (u + count, slot_rows(owner))
        return remote(
            normed.at[where], normed.at[where], g_s.at[u, j], g_r.at[u, j], (s, q, peers[j])
        )

    def edge(u, head):
        return remote(
            normed.at[u + count, pl.ds(tokens, HALO)], normed.at[u + count, pl.ds(0, HALO)],
            h_s.at[u, head], h_r.at[u], (s, q + 1, head),
        )

    keeps = (
        (raw, raw_o), (z, z_o), (dtp, dtp_o), (dt, dt_o), (cum, cum_o), (co, co_o), (st, st_o),
        (yn, yn_o), (gsc, gsc_o),
    )

    def keep(u):
        return [
            pltpu.make_async_copy(a.at[u], b.at[u], o_s.at[i, u]) for i, (a, b) in enumerate(keeps)
        ]

    def keep_normed(u):
        return pltpu.make_async_copy(normed.at[u], normed_o.at[u], o_s.at[len(keeps), u])

    def keep_part(mb):
        return pltpu.make_async_copy(
            part.at[mb], part_o.at[mb], o_s.at[len(keeps) + 1, mb]
        )

    def keep_weight(i, layer):
        a, b = ((wc, wc_o), (wo, wo_o))[i]
        return pltpu.make_async_copy(a.at[layer], b.at[layer], v_s.at[i, layer])

    def pass_state(u):
        for k in range(PIECES):
            @when(q > 0)
            def _():
                chain(u, k).wait_recv()

            @when(first_q)
            def _():
                st[u, k * piece : (k + 1) * piece] = jnp.zeros((piece, LANES), BF)

            @when(q < seqs - 1)
            def _():
                per = inner // heads
                for i in range(k * heads // PIECES, (k + 1) * heads // PIECES):
                    cut = slice(i * per, (i + 1) * per)
                    sbuf[u, cut] = (
                        car[u, i : i + 1] * st[u, cut].astype(F32) + con[cut]
                    ).astype(BF)
                chain(u, k).start()

    def weight(i, layer):
        src, dst = ((pr_in, pr), (wc_in, wc), (wo_in, wo))[i]
        return remote(src, dst.at[layer], w_s.at[i], w_r.at[i], other)

    weight(1, s).start()
    weight(2, s).start()
    halo_copy = remote(
        hid.at[:, pl.ds(tokens - HALO, HALO)], halo, w_s.at[3], w_r.at[3], (s, q + 1, h)
    )
    seg_copy = remote(
        seg.at[:, pl.ds(tokens, HALO)], seg_halo, w_s.at[4], w_r.at[4], (s, q + 1, h)
    )
    deep = conv_bc.shape[2]
    pr_in[...] = jnp.zeros_like(pr_in)
    pr_in[0:1] = norm_gain[...]
    pr_in[1:5, :inner] = conv_x[0]
    pr_in[1:5, inner : inner + deep] = conv_bc[0]
    pr_in[5:6, :inner] = conv_xb[...]
    pr_in[5:6, inner : inner + deep] = conv_bcb[...]
    pr_in[6:7, :heads] = dt_bias[...]
    pr_in[7:8, :heads] = -jnp.exp(a_log[...])
    pr_in[9:10, :inner] = gate_gain[...]
    skips = jnp.broadcast_to(
        jnp.concatenate([skip_d[...], jnp.zeros((1, LANES - heads), F32)], axis=1), (8, LANES)
    )
    pr_in[8:9, :inner] = mm(skips, matrix.astype(F32), HIGH)[:1]
    weight(0, s).start()
    batches = segments.shape[0]
    for mb in range(count):
        for given, rows_o in ((segments, srow), (padding, None)):
            row = jnp.zeros((1, tokens), F32)
            for b in range(batches):
                row = jnp.where(b == s * count + mb, given[b : b + 1].astype(F32), row)
            row = jnp.broadcast_to(row, (8, tokens))
            column = mm_tn(row * 0.125, jnp.ones((8, LANES), F32), HIGH)
            if rows_o is None:
                pad[mb] = column
            else:
                rows_o[mb] = row
                seg[mb, HALO:] = column
    load.wait()

    @when(q < seqs - 1)
    def _():
        halo_copy.start()
        seg_copy.start()

    pr[s] = pr_in[...]
    wc[s] = wc_in[...]
    wo[s] = wo_in[...]
    keep_weight(0, s).start()
    keep_weight(1, s).start()

    @when(q > 0)
    def _():
        halo_copy.wait_recv()
        seg_copy.wait_recv()
        seg[:, :HALO] = seg_halo[...]

    @when(first_q)
    def _():
        halo[...] = jnp.zeros_like(halo)
        seg[:, :HALO] = jnp.full((count, HALO, LANES), -1.0, F32)

    weight(0, 1 - s).wait_recv()

    def needs_weights(u):
        return u == count * (1 - s)

    def in_norm(mb, _):
        hx = jnp.concatenate([halo[mb], hid[mb]], axis=0)
        scale = lax.rsqrt(jnp.mean(hx * hx, axis=1, keepdims=True) + EPS)
        normed[mb, :, :model] = (hx * scale * pr[0, 0:1]).astype(BF)
        normed[mb, :, model:] = two_lanes(scale)
        keep_normed(mb).start()

        @when(first_q)
        def _():
            normed[mb + count, :HALO] = jnp.zeros((HALO, model + LANES), BF)

        return 0

    lax.fori_loop(0, count, in_norm, 0)

    def local_part(u):
        layer = u // count
        mb = lax.rem(u, count)
        prm = pr[layer]
        x = normed[u, :, :model]
        new_raw = mm(x, wc[layer, :, inner : inner + wide]).astype(BF)
        raw[u] = new_raw
        raw_f[...] = new_raw.astype(F32)
        x = x[HALO:]
        z[u] = mm(x, wc[layer, :, :inner])
        new_dtp = mm(x, wc[layer, :, inner + wide :]) + prm[6:7, :LANES]
        dtp[u] = new_dtp
        new_dt = jax.nn.softplus(new_dtp)
        dt[u] = new_dt
        new_cum = mm(lower(tokens), new_dt * prm[7:8, :LANES], HIGH)
        cum[u] = new_cum
        cum_t = new_cum.T
        dt_t = new_dt.T
        same = same_rows(seg, mb, tokens)
        pieces = []
        for col in range(0, wide, LANES):
            pre = convolved(raw_f, same, prm, col, tokens)
            piece = (pre * sigmoid(pre)).astype(BF)
            co[u, :, col : col + LANES] = piece
            pieces.append(piece)
        values = jnp.concatenate(pieces[: inner // LANES], axis=1)
        in_b, in_c = pieces[-2], pieces[-1]
        entry, decay_end = gains(new_cum, seg, mb)
        toward = expand(decay_end * new_dt, matrix)
        con[...] = fine(mm_tn, values.astype(F32) * toward, in_b)
        mine = seg[mb, HALO:]
        same_before = (mine[-1:, :] == seg[mb, HALO - 1 : HALO]).astype(F32)
        car[u] = jnp.exp(cum_t[:heads, tokens - 1 :]) * same_before

        @when(first_q)
        def _():
            pass_state(u)

        inner_cb = jnp.where(
            causal_mask(seg, srow, mb, tokens, False), mm_nt(in_c, in_b), 0.0
        )
        mid = tokens // 2
        blocks = [(slice(0, mid), slice(0, mid)), (slice(mid, tokens), slice(0, tokens))]
        for pair in range(heads // 2):
            cols = slice(pair * LANES, (pair + 1) * LANES)
            accs = [jnp.zeros((mid, LANES), F32) for _ in blocks]
            for j in range(2):
                one = slice(2 * pair + j, 2 * pair + j + 1)
                for i, (to, of) in enumerate(blocks):
                    decay = jnp.exp(jnp.minimum(new_cum[to, one] - cum_t[one, of], 0.0))
                    mask = jnp.right_shift(iota((of.stop, LANES), 1), HEAD_SHIFT) == j
                    value = jnp.where(mask, values[of, cols], jnp.zeros((), BF))
                    mixed = (inner_cb[to, of] * decay * dt_t[one, of]).astype(BF)
                    accs[i] = accs[i] + mm(mixed, value)
            for i, (to, of) in enumerate(blocks):
                yn[u, to, cols] = accs[i]

    def gate_part(u):
        layer = u // count
        mb = lax.rem(u, count)
        entry, _ = gains(cum[u], seg, mb)
        in_c = co[u, :, inner + LANES :]
        readout = mm_nt(in_c, st[u])
        y = yn[u] + expand(entry, matrix) * readout
        yn[u] = y
        ssd = y + pr[layer, 8:9, :inner] * co[u, :, :inner].astype(F32)
        gate = z[u]
        gated = ssd * (gate * sigmoid(gate))
        gated_s[...] = gated
        ones = jnp.ones((8, inner), BF)
        ssend[u] = fine(lambda a, b: mm_nt(b, a), gated * gated, ones)

    def out_part(u):
        layer = u // count
        total = ssend[u]
        for j in range(n - 1):
            squares(u, j).wait_recv()
            total = total + srecv[u, j]
        scale_row = lax.rsqrt(total / full + EPS)
        scale = mm_tn(scale_row * 0.125, jnp.ones((8, LANES), F32), HIGH)
        gsc[u] = scale
        x = (gated_s[...] * wide_copy(scale, inner) * pr[layer, 9:10, :inner]).astype(BF)
        product = mm(x, wo[layer])

        @when(u < count)
        def _():
            part0[u] = product.astype(BF)
            for j in range(n - 1):
                scatter(u, j).start()

        @when(u >= count)
        def _():
            part[u - count] = product.astype(BF)
            keep_part(u - count).start()

    def finish(u):
        total = part0[u, at_rows(h)].astype(F32)
        for j in range(n - 1):
            scatter(u, j).wait_recv()
            total = total + rbuf0[u, j].astype(F32)
        h_new = hid[u, at_rows(h)] + total
        scale = lax.rsqrt(jnp.mean(h_new * h_new, axis=1, keepdims=True) + EPS)
        normed[u + count, slot_rows(h), :model] = (h_new * scale * pr[1, 0:1]).astype(BF)
        normed[u + count, slot_rows(h), model:] = two_lanes(scale)
        for j in range(n - 1):
            gather(u, j, h).start()

        @when(edge_owner)
        def _():
            for head in range(n):
                edge(u, head).start()

    def arrived(u):
        for j in range(n - 1):
            gather(u, j, froms[j]).wait_recv()

    def step(u, _):
        @when(both(u >= count, u < units))
        def _():
            mb = u - count
            arrived(mb)

            @when(q > 0)
            def _():
                edge(mb, 0).wait_recv()

            keep_normed(u).start()

        @when(u == count)
        def _():
            finish(u - 1)

        @when(needs_weights(u))
        def _():
            weight(1, 1 - s).wait_recv()
            keep_weight(0, 1 - s).start()

        @when(u < units)
        def _():
            local_part(u)

            @when(q > 0)
            def _():
                pass_state(u)

            gate_part(u)
            for j in range(n - 1):
                squares(u, j).start()

        @when(both(u > 0, u < count))
        def _():
            finish(u - 1)

        @when(needs_weights(u))
        def _():
            weight(2, 1 - s).wait_recv()
            keep_weight(1, 1 - s).start()

        @when(u < units)
        def _():
            out_part(u)
            for copy in keep(u):
                copy.start()

        return 0

    lax.fori_loop(0, units, step, 0)

    def drain(u, _):
        for j in range(n - 1):
            squares(u, j).wait_send()

        @when(q < seqs - 1)
        def _():
            for k in range(PIECES):
                chain(u, k).wait_send()

        @when(u < count)
        def _():
            for j in range(n - 1):
                scatter(u, j).wait_send()
                gather(u, j, h).wait_send()
            keep_part(u).wait()

        @when(both(u < count, edge_owner))
        def _():
            for head in range(n):
                edge(u, head).wait_send()

        for copy in keep(u):
            copy.wait()
        keep_normed(u).wait()
        return 0

    lax.fori_loop(0, units, drain, 0)
    for i in range(3):
        weight(i, s).wait_send()
    for i in range(2):
        for layer in range(2):
            keep_weight(i, layer).wait()

    @when(q < seqs - 1)
    def _():
        halo_copy.wait_send()
        seg_copy.wait_send()


def bwd_kernel(seqs, n, cot, hid, kept, wc_in, wo_in, raw_in, z_in, dtp_in, dt_in, cum_in,
               co_in, st_in, yn_in, gsc_in, part_in, pad, car, seg, srow, pr,
               out, small_o, ig, lo,
               gin, lo_s, normed, wc, wo, raw, z, dtp, dt, cum, co, st, yn, gsc,
               big, pbuf, table, ps, rs_, ts,
               raw_f, shift, gconv, gext, gz, gy_s, ng, gdr, back, nxt, sbuf,
               part, hpart, rbuf, hbuf, acc, ag, gwb, small, srecv, ggn, dsend, drecv,
               c_s, c_r, s_s, s_r, g_s, g_r, h_s, h_r, m_s, m_r, l_c, l_s, l_r, in_s,
               d_s, d_r, f_s, w_s, x_s, x_r, a_s, a_r, b_s, b_r, t_s, t_r,
               k_c, k_s, k_r, e_s, e_r, p_s):
    s, q, h = place()
    count, tokens, model = gin.shape[0] // 2, gin.shape[1], gin.shape[2]
    inner = wo.shape[0]
    state = LANES
    wide = raw.shape[2]
    heads = inner >> HEAD_SHIFT
    rows = tokens // n
    ext = tokens + HALO
    steps = 2 * count
    full = inner * n
    piece = inner // PIECES
    other = (1 - s, q, h)
    edge_owner = both(h == n - 1, q < seqs - 1)
    peers = [lax.rem(h + j, n) for j in range(1, n)]
    froms = [lax.rem(h + n - j, n) for j in range(1, n)]
    matrix = spread_matrix(inner)
    sources = (raw_in, z_in, dtp_in, dt_in, cum_in, co_in, st_in, yn_in, gsc_in)
    targets = (raw, z, dtp, dt, cum, co, st, yn, gsc)

    def unit(w):
        return (1 - w // count) * count + lax.rem(w, count)

    def stream(w):
        k = lax.rem(w, count)
        return [
            pltpu.make_async_copy(a.at[unit(w)], b.at[k], f_s.at[i, k])
            for i, (a, b) in enumerate(zip(sources, targets))
        ]

    def wc_load(layer):
        return pltpu.make_async_copy(wc_in.at[layer], wc, w_s.at[0])

    def wo_load(layer):
        return pltpu.make_async_copy(wo_in.at[layer], wo, w_s.at[1])

    loads = [
        pltpu.make_async_copy(cot.at[pl.ds(s * count, count)], gin.at[pl.ds(0, count)], in_s.at[0]),
        pltpu.make_async_copy(
            hid.at[pl.ds(s * count, count)], gin.at[pl.ds(count, count)], in_s.at[1]
        ),
        pltpu.make_async_copy(kept.at[pl.ds(0, steps)], normed, in_s.at[2]),
    ]
    loads[0].start()
    wo_load(1).start()
    for load in stream(0):
        load.start()
    wc_load(1).start()
    for load in loads[1:]:
        load.start()
    for p in peers:
        greet((s, q, p))
    greet(other)

    @when(q < seqs - 1)
    def _():
        greet((s, q + 1, h))

    @when(edge_owner)
    def _():
        for head in range(n - 1):
            greet((s, q + 1, head))

    @when(q > 0)
    def _():
        greet((s, q - 1, h))

    await_greets(
        n + one_if(q > 0) * (1 + one_if(h < n - 1)) + one_if(q < seqs - 1)
    )

    def at_rows(owner):
        return pl.ds(pl.multiple_of(owner * rows, rows), rows)

    def slot(w):
        return lax.rem(w, count)

    def chain(w, k):
        cut = pl.ds(k * piece, piece)
        return remote(
            sbuf.at[slot(w), cut], nxt.at[w, cut], c_s.at[w, k], c_r.at[w, k], (s, q - 1, h)
        )

    def scatter(w, j):
        return remote(
            part.at[slot(w), at_rows(peers[j])], rbuf.at[slot(w), j], s_s.at[w, j],
            s_r.at[w, j], (s, q, peers[j]),
        )

    def gather(w, j, owner):
        where = (slot(w), at_rows(owner))
        return remote(
            ag.at[where], ag.at[where], g_s.at[w, j], g_r.at[w, j], (s, q, peers[j])
        )

    def branch_scatter(mb, j):
        lanes = pl.ds(0, model)
        return remote(
            part.at[mb, at_rows(peers[j]), lanes], rbuf.at[mb, j, :, lanes],
            s_s.at[steps + mb, j], s_r.at[steps + mb, j], (s, q, peers[j]),
        )

    def branch_gather(mb, j, owner):
        where = (mb, at_rows(owner), pl.ds(0, model))
        return remote(
            ag.at[where], ag.at[where], g_s.at[steps + mb, j], g_r.at[steps + mb, j],
            (s, q, peers[j]),
        )

    def edge(w, head):
        return remote(
            hpart.at[w], hbuf.at[w, head], h_s.at[w], h_r.at[w, head], (s, q - 1, n - 1)
        )

    def little(layer, j):
        return remote(
            small.at[layer], srecv.at[layer, j], m_s.at[layer, j], m_r.at[layer, j],
            (s, q, peers[j]),
        )

    def ship_local(v):
        mb = lax.rem(v, count)
        return pltpu.make_async_copy(gin.at[v], ig.at[s * count + mb], l_c.at[mb])

    def ship(v):
        mb = lax.rem(v, count)
        return remote(gin.at[v], ig.at[s * count + mb], l_s.at[mb], l_r.at[mb], other)

    def out_local(mb):
        return pltpu.make_async_copy(lo_s.at[mb], lo.at[s * count + mb], k_c.at[mb])

    def out_ship(mb):
        return remote(lo_s.at[mb], lo.at[s * count + mb], k_s.at[mb], k_r.at[mb], other)

    def send_layer(layer, mb, h_new, branch):
        lo_s[mb] = h_new
        live = pad[mb]
        for i, x in enumerate((h_new, branch)):
            table[layer, 24 + i : 25 + i, :LANES] += jnp.sum(
                jnp.sum(x * x, axis=1, keepdims=True) * live, axis=0, keepdims=True
            )
        table[layer, 26:27, :LANES] += jnp.sum(live, axis=0, keepdims=True)

        @when(s == layer)
        def _():
            out_local(mb).start()

        @when(s != layer)
        def _():
            out_ship(mb).start()

    def norm_part(v):
        layer = 1 - v // count
        mb = lax.rem(v, count)
        u = layer * count + mb
        for j in range(n - 1):
            gather(v, j, froms[j]).wait_recv()
        gn = ag[mb, :, :model].astype(F32)
        scale = jnp.sum(normed[u, HALO:, model:].astype(F32), axis=1, keepdims=True)
        gain = pr[layer, 0:1]

        def rest(h_in, grad_out):
            x = gn * gain
            dots = jnp.sum(x * h_in, axis=1, keepdims=True)
            gin[v] = grad_out + x * scale - h_in * (scale * scale * scale * dots / model)
            table[layer, 0:1] += jnp.sum(gn * h_in * scale, axis=0, keepdims=True)

        @when(layer == 1)
        def _():
            h_in = normed[u, HALO:, :model].astype(F32) / (scale * gain)
            rest(h_in, gin[mb] * wide_copy(pad[mb], model))
            send_layer(0, mb, h_in, h_in - gin[mb + count])

        @when(layer == 0)
        def _():
            rest(gin[v], gin[mb])

        @when(s == layer)
        def _():
            ship_local(v).start()

        @when(s != layer)
        def _():
            ship(v).start()

        grad_w = mm_tn(normed[u, HALO:, :model], ag[mb, :, model:])

        @when(mb == 0)
        def _():
            gwb[...] = grad_w

        @when(mb > 0)
        def _():
            gwb[...] += grad_w

        @when(mb == count - 1)
        def _():
            base = model + inner
            deep = 2 * state
            for k in range(model // deep):
                cut = slice(k * deep, (k + 1) * deep)
                big[layer, base : base + deep, cut] = gwb[cut].astype(TOTAL_T)

            @when(s == 0)
            def _():
                start_cross(layer, (model + inner) // CHUNK - chunks, chunks)

    def dots(w, j):
        return remote(
            dsend.at[w], drecv.at[w, j], d_s.at[w, j], d_r.at[w, j], (s, q, peers[j])
        )

    def gate_forward(mb, layer):
        gate = z[mb]
        sig = sigmoid(gate)
        silu = gate * sig
        ssd = yn[mb] + pr[layer, 8:9, :inner] * co[mb, :, :inner].astype(F32)
        return gate, sig, silu, ssd, ssd * silu

    def out_b(layer, mb):
        live = jnp.where(layer == 1, pad[mb], jnp.ones((tokens, LANES), F32))
        return (gin[mb] * wide_copy(live, model)).astype(BF)

    def gate_first(w):
        layer = 1 - w // count
        mb = lax.rem(w, count)
        u = layer * count + mb

        grad_gn = mm_nt(out_b(layer, mb), wo[...])
        ggn[...] = grad_gn
        gated = gate_forward(mb, layer)[-1]
        ones = jnp.ones((8, inner), BF)
        dsend[w] = fine(
            lambda a, b: mm_nt(b, a), grad_gn * gated * pr[layer, 9:10, :inner], ones
        )
        for j in range(n - 1):
            dots(w, j).start()

    def conv_slope(w):
        mb = lax.rem(w, count)
        raw_f[...] = raw[mb].astype(F32)
        same = same_rows(seg, mb, tokens)
        prm = pr[1 - w // count]
        for col in range(0, wide, LANES):
            pre = convolved(raw_f, same, prm, col, tokens)
            sig = sigmoid(pre)
            gconv[:, col : col + LANES] = sig * (1.0 + pre * (1.0 - sig))

    def gate_part(w):
        layer = 1 - w // count
        mb = lax.rem(w, count)
        u = layer * count + mb
        total = dsend[w]
        for j in range(n - 1):
            dots(w, j).wait_recv()
            total = total + drecv[w, j]
        across = mm_tn(total * 0.125, jnp.ones((8, LANES), F32), HIGH)
        scale = gsc[mb]
        scale_x = wide_copy(scale, inner)
        gate, sig, silu, ssd, gated = gate_forward(mb, layer)
        grad_gn = ggn[...]
        values = co[mb, :, :inner].astype(F32)
        gain = pr[layer, 9:10, :inner]
        scaled = gated * scale_x
        grad_gated = grad_gn * (gain * scale_x) - scaled * wide_copy(
            scale * scale * across / full, inner
        )
        gy = (grad_gated * silu).astype(BF)
        gy_s[...] = gy
        gz[mb] = (grad_gated * ssd * (sig * (1.0 + gate * (1.0 - sig)))).astype(BF)
        ng[mb] = (scaled * gain).astype(BF)
        gy_f = gy.astype(F32)
        table[layer, 8:9, :inner] += jnp.sum(grad_gn * scaled, axis=0, keepdims=True)
        table[layer, 9:10, :inner] += jnp.sum(gy_f * values, axis=0, keepdims=True)
        entry, _ = gains(cum[mb], seg, mb)
        read = expand(entry, matrix) * gy_f
        back[...] = fine(mm_tn, read, co[mb, :, inner + state :])

        @when(q == seqs - 1)
        def _():
            pass_state(w, u)

    def pass_state(w, u):
        per = inner // heads
        for k in range(PIECES):
            @when(q < seqs - 1)
            def _():
                chain(w, k).wait_recv()

            @when(q == seqs - 1)
            def _():
                nxt[w, k * piece : (k + 1) * piece] = jnp.zeros((piece, LANES), BF)

            @when(q > 0)
            def _():
                @when(w >= count)
                def _():
                    chain(w - count, k).wait_send()

                for i in range(k * heads // PIECES, (k + 1) * heads // PIECES):
                    cut = slice(i * per, (i + 1) * per)
                    sbuf[slot(w), cut] = (
                        car[u, i : i + 1] * nxt[w, cut].astype(F32) + back[cut]
                    ).astype(BF)
                chain(w, k).start()

    def local_part(w):
        layer = 1 - w // count
        mb = lax.rem(w, count)
        u = layer * count + mb
        prm = pr[layer]
        cum_u, dt_u = cum[mb], dt[mb]
        cum_t = cum_u.T
        entry, decay_end = gains(cum_u, seg, mb)
        values = co[mb, :, :inner]
        in_b = co[mb, :, inner : inner + state]
        in_c = co[mb, :, inner + state :]
        gy = gy_s[...]
        gy_f = gy.astype(F32)
        causal = causal_mask(seg, srow, mb, tokens, True)
        inner_bc = jnp.where(causal, mm_nt(in_b, in_c), 0.0)
        lane = iota((tokens, LANES), 1)
        mid = tokens // 2
        blocks = [(slice(0, mid), slice(0, tokens)), (slice(mid, tokens), slice(mid, tokens))]
        grad_inners = [jnp.zeros((mid, to.stop - to.start), F32) for _, to in blocks]
        grad_dts = [jnp.zeros((mid, LANES), F32) for _ in blocks]
        locals_, rows_ = [], []
        for pair in range(heads // 2):
            cols = slice(pair * LANES, (pair + 1) * LANES)
            totals = [jnp.zeros((mid, LANES), F32) for _ in blocks]
            for j in range(2):
                head = 2 * pair + j
                one = slice(head, head + 1)
                mask = jnp.right_shift(lane, HEAD_SHIFT) == j
                gy_one = jnp.where(mask, gy[:, cols], jnp.zeros((), BF))
                downs = []
                for i, (of, to) in enumerate(blocks):
                    dt_col = dt_u[of, one]
                    decay = jnp.exp(jnp.minimum(cum_t[one, to] - cum_u[of, one], 0.0))
                    grad_mix = mm_nt(values[of, cols], gy_one[to])
                    mixed = inner_bc[of, to] * decay
                    totals[i] = totals[i] + mm((mixed * dt_col).astype(BF), gy_one[to])
                    grad_inners[i] = grad_inners[i] + grad_mix * (decay * dt_col)
                    weighted = grad_mix * mixed
                    sums = jnp.sum(weighted, axis=1, keepdims=True)
                    grad_dts[i] = jnp.where(lane[:mid] == head, sums, grad_dts[i])
                    downs.append(jnp.sum(weighted * dt_col, axis=0, keepdims=True))
                rows_.append(
                    jnp.concatenate([downs[0][:, :mid], downs[0][:, mid:] + downs[1]], axis=1)
                )
            locals_.append(jnp.concatenate(totals, axis=0))
            tick(w, 3 + pair, 1)

        @when(w > 0)
        def _():
            finish(w - 1)

        tick(w, 7, 1)

        @when(q < seqs - 1)
        def _():
            pass_state(w, u)

        grad_inners = [
            jnp.where(causal[of, to], x, 0.0) for x, (of, to) in zip(grad_inners, blocks)
        ]
        grad_dt = jnp.concatenate(grad_dts, axis=0)
        toward = decay_end * dt_u
        toward_x = expand(toward, matrix)
        values_f = values.astype(F32)
        pulled = mm_nt(in_b, nxt[w])
        gconv[:, :inner] *= (
            prm[8:9, :inner] * gy_f + jnp.concatenate(locals_, axis=1) + toward_x * pulled
        )
        read = expand(entry, matrix) * gy_f
        from_row = (iota((heads, LANES), 0) == iota((heads, LANES), 1)).astype(F32)
        grad_cum = (
            mm_tn(jnp.concatenate(rows_, axis=0), from_row, HIGH)
            - dt_u * grad_dt
            + head_sums(read * mm_nt(in_c, st[mb]), matrix)
        )
        pulled_sums = head_sums(values_f * pulled, matrix)
        grad_dt = grad_dt + pulled_sums * decay_end
        high, low = split(nxt[w].astype(F32) * st[mb].astype(F32))
        carried = jnp.sum(
            lax.dot_general(high, matrix, (((0,), (1,)), ((), ())), preferred_element_type=F32)
            + lax.dot_general(low, matrix, (((0,), (1,)), ((), ())), preferred_element_type=F32),
            axis=0,
            keepdims=True,
        )
        ahead = (iota((tokens, tokens), 0) > iota((tokens, tokens), 1)).astype(F32)
        grad_rate = (
            mm_tn(lower(tokens), grad_cum, HIGH)
            + mm(ahead, pulled_sums * toward, HIGH)
            + carried * entry[-1:]
        )
        neg = prm[7:8, :LANES]
        grad_pre = (grad_dt + grad_rate * neg) * sigmoid(dtp[mb])
        table[layer, 6:7, :LANES] += jnp.sum(grad_pre, axis=0, keepdims=True)
        table[layer, 7:8, :LANES] += jnp.sum(grad_rate * dt_u * neg, axis=0, keepdims=True)
        grad_raw_dt = grad_pre.astype(BF)
        gdr[mb] = grad_raw_dt
        gconv[:, inner : inner + state] *= jnp.concatenate(
            [fine(mm, x, in_c[to]) for x, (of, to) in zip(grad_inners, blocks)], axis=0
        ) + fine(mm, values_f * toward_x, nxt[w])
        first_c = fine(mm_tn, grad_inners[0], in_b[:mid])
        second_c = first_c[mid:] + fine(mm_tn, grad_inners[1], in_b[mid:])
        gconv[:, inner + state :] *= jnp.concatenate([first_c[:mid], second_c], axis=0) + fine(
            mm, read, st[mb]
        )
        same = same_rows(seg, mb, tokens)
        first = HALO - KC + 1
        shift[:HALO] = jnp.zeros((HALO, LANES), F32)
        shift[ext:] = jnp.zeros((HALO, LANES), F32)
        for col in range(0, wide, LANES):
            cols = slice(col, col + LANES)
            grad = gconv[:, cols]
            target = table if col < inner else small
            off = col if col < inner else col - inner
            tc = slice(off, off + LANES)
            target[layer, 5:6, tc] += jnp.sum(grad, axis=0, keepdims=True)
            total = jnp.zeros((ext, LANES), F32)
            for k in range(KC):
                masked = grad * same[k]
                target[layer, 1 + k : 2 + k, tc] += jnp.sum(
                    masked * raw_f[first + k : first + k + tokens, cols], axis=0, keepdims=True
                )
                shift[HALO:ext] = masked * prm[1 + k : 2 + k, cols]
                total = total + shift[KC - 1 - k : KC - 1 - k + ext]
            gext[mb, :, cols] = total.astype(BF)
            if col == wide // 2:
                tick(w, 8, 1)
        grad_raw = gext[mb]
        main = mm_nt(gz[mb], wc[:, :inner]) + mm_nt(
            grad_raw_dt, wc[:, inner + wide :]
        )
        rest = mm_nt(grad_raw, wc[:, inner : inner + wide])
        part[mb, :, :model] = (main + rest[HALO:]).astype(BF)
        hpart[w, :, :model] = rest[:HALO].astype(BF)
        part[mb, :, model:] = grad_raw[HALO:, inner:]
        hpart[w, :, model:] = grad_raw[:HALO, inner:]

    def finish(w):
        acc[...] = part[slot(w), at_rows(h)].astype(F32)
        for j in range(n - 1):
            scatter(w, j).wait_recv()
            acc[...] += rbuf[slot(w), j].astype(F32)

        @when(both(edge_owner, w < steps))
        def _():
            for head in range(n):
                edge(w, head).wait_recv()
                acc[rows - HALO :] += hbuf[w, head].astype(F32)

        ag[slot(w), at_rows(h)] = acc[...].astype(BF)
        for j in range(n - 1):
            gather(w, j, h).start()

    def weights_part(layer):
        gate_w = jnp.zeros((inner, model), F32)
        z_w = jnp.zeros((model, inner), F32)
        x_w = jnp.zeros((model, inner), F32)
        dt_w = jnp.zeros((LANES, model), F32)
        for mb in range(count):
            x = normed[layer * count + mb, :, :model]
            gate_w = gate_w + mm_tn(ng[mb], out_b(layer, mb))
            z_w = z_w + mm_tn(x[HALO:], gz[mb])
            x_w = x_w + mm_tn(x, gext[mb, :, :inner])
            dt_w = dt_w + mm_tn(gdr[mb], x[HALO:])
        big[layer, :model, :inner] = z_w.astype(TOTAL_T)
        big[layer, :model, inner:] = x_w.astype(TOTAL_T)
        big[layer, model : model + inner] = gate_w.astype(TOTAL_T)
        table[layer, 16:24] = dt_w[:8]
        for j in range(n - 1):
            little(layer, j).start()

        @when(s == 0)
        def _():
            start_cross(layer, 0, (model + inner) // CHUNK - chunks)

        @when(s == 1)
        def _():
            start_cross(layer, 0, chunks)

    chunks = big.shape[1] // (2 * CHUNK)
    spot = s * (seqs - 1) + (1 - 2 * s) * q
    way = 1 - 2 * s
    has_prev, has_next = spot > 0, spot < seqs - 1
    delays = [(SKEW, SKEW), (SKEW + LEAD * (1 - s), SKEW + LEAD * s)]

    def span(base, c):
        return pl.ds(pl.multiple_of(base + c * CHUNK, CHUNK), CHUNK)

    def cross_at(layer, c):
        k = layer * chunks + c
        return remote(
            big.at[layer, span((1 - s) * chunks * CHUNK, c)],
            pbuf.at[layer, span(0, c)], x_s.at[k], x_r.at[k], other,
        )

    def start_cross(layer, low, high):
        def one(c, _):
            cross_at(layer, c).start()
            return 0

        lax.fori_loop(low, high, one, 0)

    def work(layer, c):
        mine = one_if(s == layer)
        return span((mine * s + 2 * (1 - mine)) * chunks * CHUNK, c)

    def along(layer, c):
        k = layer * chunks + c
        return remote(
            big.at[layer, span(s * chunks * CHUNK, c)], out.at[work(layer, c)],
            a_s.at[k], a_r.at[k], (s, q + way, h),
        )

    def home(layer, c):
        k, at = layer * chunks + c, work(layer, c)
        return remote(out.at[at], out.at[at], b_s.at[k], b_r.at[k], (s, q - way, h))

    def deliver(layer, c):
        return remote(
            out.at[work(layer, c)], out.at[span(s * chunks * CHUNK, c)], e_s.at[c], e_r.at[c],
            other,
        )

    def settled(layer, c):
        @when(has_prev)
        def _():
            home(layer, c).start()

        @when(s != layer)
        def _():
            deliver(layer, c).start()

    def advance(layer, t):
        outward, inward = delays[layer]
        c = t - outward * spot

        @when(both(c >= 0, c < chunks))
        def _():
            at = span(s * chunks * CHUNK, c)
            cross_at(layer, c).wait_recv()
            sums = big[layer, at].astype(F32) + pbuf[layer, span(0, c)].astype(F32)

            @when(has_prev)
            def _():
                along(layer, c).wait_recv()
                big[layer, at] = (sums + out[work(layer, c)].astype(F32)).astype(TOTAL_T)

            @when(jnp.logical_not(has_prev))
            def _():
                big[layer, at] = sums.astype(TOTAL_T)

            @when(has_next)
            def _():
                along(layer, c).start()

            @when(jnp.logical_not(has_next))
            def _():
                out[work(layer, c)] = big[layer, at]
                settled(layer, c)

        e = t - outward * (seqs - 1) - inward * (seqs - 1 - spot)

        @when(both(has_next, both(e >= 0, e < chunks)))
        def _():
            home(layer, e).wait_recv()
            settled(layer, e)

    def tick(w, offset, amount):
        @when(w >= count)
        def _():
            def one(i, _):
                advance(1, (w - count) * TICKS + offset + i)
                return 0

            lax.fori_loop(0, amount, one, 0)

    def late_tick(t, _):
        advance(0, t)
        advance(1, t + count * TICKS)
        return 0

    def tail_tick(w, offset, amount):
        first = (w - steps) * TAIL_TICKS + offset
        lax.fori_loop(first, first + amount, late_tick, 0)

    table[...] = jnp.zeros_like(table)
    small[...] = jnp.zeros_like(small)
    loads[0].wait()

    def step(w, _):
        @when(w < steps)
        def _():
            for load in stream(w):
                load.wait()

        @when(w + 1 < steps)
        def _():
            for load in stream(w + 1):
                load.start()

        @when(w == 1)
        def _():
            for load in loads[1:]:
                load.wait()

        @when(w >= count)
        def _():
            norm_part(w - count)

        @when(w >= steps)
        def _():
            tail_tick(w, 0, TAIL_TICKS // 2)

            @when(w == steps)
            def _():
                finish(w - 1)

            tail_tick(w, TAIL_TICKS // 2, TAIL_TICKS - TAIL_TICKS // 2)

        @when(w < steps)
        def _():
            tick(w, 0, 1)

            @when(both(lax.rem(w, count) == 0, w < steps))
            def _():
                wo_load(0).wait()

            gate_first(w)

            @when(w == count - 1)
            def _():
                wo_load(0).start()

            tick(w, 1, 1)
            conv_slope(w)
            tick(w, 2, 1)
            gate_part(w)

            @when(w >= count)
            def _():
                for j in range(n - 1):
                    scatter(w - count, j).wait_send()
                    gather(w - count, j, h).wait_send()

            @when(lax.rem(w, count) == 0)
            def _():
                wc_load(0).wait()

            local_part(w)

            @when(w == count - 1)
            def _():
                wc_load(0).start()

            @when(q > 0)
            def _():
                edge(w, h).start()

            for j in range(n - 1):
                scatter(w, j).start()

            tick(w, 9, 1)

            @when(lax.rem(w, count) == count - 1)
            def _():
                weights_part(1 - w // count)

        return 0

    lax.fori_loop(0, steps + count, step, 0)

    def settle_sends(mb, _):
        for j in range(n - 1):
            scatter(mb + count, j).wait_send()
            gather(mb + count, j, h).wait_send()
        load_part(mb).start()
        return 0

    def load_part(mb):
        return pltpu.make_async_copy(
            part_in.at[mb], part.at[mb, :, pl.ds(0, model)], p_s.at[mb]
        )

    lax.fori_loop(0, count, settle_sends, 0)
    for mb in range(count):
        load_part(mb).wait()
        for j in range(n - 1):
            branch_scatter(mb, j).start()
    tail_tick(steps + count, 0, TAIL_TICKS)

    def finish_branch(mb, _):
        total = part[mb, at_rows(h), :model].astype(F32)
        for j in range(n - 1):
            branch_scatter(mb, j).wait_recv()
            total = total + rbuf[mb, j, :, :model].astype(F32)
        ag[mb, at_rows(h), :model] = total.astype(BF)
        for j in range(n - 1):
            branch_gather(mb, j, h).start()
        return 0

    lax.fori_loop(0, count, finish_branch, 0)
    tail_tick(steps + count + 1, 0, TAIL_TICKS)

    def last_layer(mb, _):
        @when(s == 0)
        def _():
            out_local(mb).wait()

        @when(s == 1)
        def _():
            out_ship(mb).wait_send()

        for j in range(n - 1):
            branch_gather(mb, j, froms[j]).wait_recv()
        u = count + mb
        scale = jnp.sum(normed[u, HALO:, model:].astype(F32), axis=1, keepdims=True)
        h_in = normed[u, HALO:, :model].astype(F32) / (scale * pr[1, 0:1])
        branch = ag[mb, :, :model].astype(F32)
        send_layer(1, mb, h_in + branch, branch)
        return 0

    lax.fori_loop(0, count, last_layer, 0)

    def drain(w, _):
        @when(both(w >= count, q > 0))
        def _():
            for k in range(PIECES):
                chain(w, k).wait_send()

        @when(w < count)
        def _():
            for j in range(n - 1):
                branch_scatter(w, j).wait_send()
                branch_gather(w, j, h).wait_send()

        for j in range(n - 1):
            dots(w, j).wait_send()

        @when(q > 0)
        def _():
            edge(w, h).wait_send()

        return 0

    lax.fori_loop(0, steps, drain, 0)
    for layer in range(2):
        total = small[layer]
        for j in range(n - 1):
            little(layer, j).wait_recv()
            total = total + srecv[layer, j]
        for j in range(n - 1):
            little(layer, j).wait_send()
        table[layer, 1:6, inner : inner + 2 * state] = total[1:6]
    small_cross = remote(table.at[1 - s], ps, t_s.at[0], t_r.at[0], other)
    small_along = remote(ts, rs_, t_s.at[1], t_r.at[1], (s, q + 1, h))
    small_home = remote(small_o, small_o, t_s.at[2], t_r.at[2], (s, q - 1, h))
    small_cross.start()
    done = (count + 2) * TAIL_TICKS
    first_end = chunks + 2 * SKEW * (seqs - 1)
    second_end = chunks + (2 * SKEW + LEAD) * (seqs - 1) - count * TICKS
    last = max(first_end, second_end, done + 2 * SKEW * (seqs - 1) + 1)
    back_at = done + SKEW * (2 * (seqs - 1) - q)

    def last_tick(t, _):
        @when(t == done + SKEW * q)
        def _():
            small_cross.wait_recv()
            ts[...] = table[s] + ps[...]

            @when(q > 0)
            def _():
                small_along.wait_recv()
                ts[...] += rs_[...]

            @when(q < seqs - 1)
            def _():
                small_along.start()

            @when(q == seqs - 1)
            def _():
                small_o[...] = ts[...]

                @when(q > 0)
                def _():
                    small_home.start()

        @when(both(t == back_at, q < seqs - 1))
        def _():
            small_home.wait_recv()

            @when(q > 0)
            def _():
                small_home.start()

        return late_tick(t, _)

    lax.fori_loop(done, last, last_tick, 0)

    def drain_sum(c, _):
        for layer in range(2):
            cross_at(layer, c).wait_send()

            @when(has_next)
            def _():
                along(layer, c).wait_send()

            @when(has_prev)
            def _():
                home(layer, c).wait_send()

            @when(s != layer)
            def _():
                deliver(layer, c).wait_send()

        remote(
            out.at[work(0, c)], out.at[span((1 - s) * chunks * CHUNK, c)], e_s.at[c], e_r.at[c],
            other,
        ).wait_recv()
        return 0

    lax.fori_loop(0, chunks, drain_sum, 0)
    small_cross.wait_send()

    @when(q < seqs - 1)
    def _():
        small_along.wait_send()

    @when(q > 0)
    def _():
        small_home.wait_send()

    def drain_out(mb, _):
        ship_local(mb).wait()
        ship(mb).wait_send()
        remote(
            gin.at[mb], ig.at[(1 - s) * count + mb], l_s.at[mb], l_r.at[mb], other
        ).wait_recv()

        @when(s == 1)
        def _():
            out_local(mb).wait()

        @when(s == 0)
        def _():
            out_ship(mb).wait_send()

        remote(
            lo_s.at[mb], lo.at[(1 - s) * count + mb], k_s.at[mb], k_r.at[mb], other
        ).wait_recv()
        return 0

    lax.fori_loop(0, count, drain_out, 0)


def pad_lanes(a, width):
    return jnp.pad(a, ((0, 0), (0, width - a.shape[1])))


def final_kernel(zx, wo, bc, table, lo, ig, g_zx, g_wo, g_bc, lo_o, ig_o, rms, g_norm, g_dt, g_cx, g_cxb, g_cb, g_cbb,
                 g_dtb, g_al, g_sk, g_gate):
    inner = g_zx.shape[3]
    model = table.shape[1]
    heads = g_dtb.shape[1]
    step = pl.program_id(0)
    g_zx[0, :, 0, :] = zx[:, :inner].astype(F32)
    g_zx[0, :, 1, :] = zx[:, inner:].astype(F32)
    g_wo[0] = wo[...].astype(F32)
    lo_o[0] = lo[...]
    ig_o[0] = ig[...]

    @when(step == 0)
    def _():
        deep = g_bc.shape[2]
        for k in range(model // deep):
            cut = slice(k * deep, (k + 1) * deep)
            g_bc[0, cut] = bc[:, cut].astype(F32)
        live = table[26:27, :LANES] * model
        first = jnp.sqrt(table[24:25, :LANES] / live)
        second = jnp.sqrt(table[25:26, :LANES] / live)
        rms[...] = jnp.where(iota((1, LANES), 1) == 0, first, second)[:, :2]
        g_norm[...] = table[0:1]
        g_dt[0] = table[16 : 16 + heads]
        g_cx[0] = table[1:5, :inner]
        g_cxb[...] = table[5:6, :inner]
        g_cb[0] = table[1:5, inner : inner + deep]
        g_cbb[...] = table[5:6, inner : inner + deep]
        g_dtb[...] = table[6:7, :heads]
        g_al[...] = table[7:8, :heads]
        sums = mm(table[8:16, :inner], spread_matrix(inner).astype(F32).T, HIGH)
        g_sk[...] = sums[1:2, :heads]
        g_gate[...] = table[8:9, :inner]


def finalize(big, table, lo, ig, inner, heads, state):
    model = big.shape[1]
    steps = 2
    each = (lo.shape[0] // steps,) + lo.shape[1:]
    deep = 2 * state

    def whole(shape):
        return pl.BlockSpec(shape, lambda i: (0,) * len(shape))

    shapes = [
        (1, model, 2, inner), (1, inner, model), (1, model, deep), (1,) + lo.shape,
        (1,) + ig.shape, (1, 2), (1, model),
        (1, heads, model), (1, 4, inner), (1, inner), (1, 4, deep), (1, deep),
        (1, heads), (1, heads), (1, heads), (1, inner),
    ]
    specs = [
        pl.BlockSpec((1, model // steps, 2, inner), lambda i: (0, i, 0, 0)),
        pl.BlockSpec((1, inner // steps, model), lambda i: (0, i, 0)),
        whole(shapes[2]),
        pl.BlockSpec((1,) + each, lambda i: (0, i, 0, 0)),
        pl.BlockSpec((1,) + each, lambda i: (0, i, 0, 0)),
    ] + [whole(x) for x in shapes[5:]]
    base = model // (inner // steps)
    return pl.pallas_call(
        final_kernel,
        grid=(steps,),
        in_specs=[
            pl.BlockSpec((model // steps, model), lambda i: (i, 0)),
            pl.BlockSpec((inner // steps, model), lambda i: (base + i, 0)),
            pl.BlockSpec((deep, model), lambda i: ((model + inner) // deep, 0)),
            whole(table.shape),
            pl.BlockSpec(each, lambda i: (i, 0, 0)),
            pl.BlockSpec(each, lambda i: (i, 0, 0)),
        ],
        out_specs=specs,
        out_shape=[jax.ShapeDtypeStruct(x, F32) for x in shapes],
        compiler_params=pltpu.CompilerParams(vmem_limit_bytes=LIMIT),
        name="final",
    )(big, big, big, table, lo, ig)


def local(hidden_in, cotangent, segments, padding, norm_gain, w_zx, w_bc, w_dt, conv_x,
          conv_x_bias, conv_bc, conv_bc_bias, dt_bias, a_log, skip_d, gate_gain, w_out):
    s, q, h = place()
    seqs = lax.axis_size(SEQ)
    n = lax.axis_size(HEAD)
    sections = lax.axis_size(SEC)
    batches, tokens, model = hidden_in.shape
    count = batches // sections
    inner = w_out.shape[1]
    heads = w_dt.shape[2]
    state = w_bc.shape[2] // 2
    wide = inner + 2 * state
    wc = jnp.concatenate(
        [w_zx[0].reshape(model, 2 * inner), w_bc[0], pad_lanes(w_dt[0], LANES)], axis=1
    )
    units = 2 * count
    rows = tokens + HALO
    part_rows = tokens // n
    lane_shape = (units, tokens, LANES)
    inner_shape = (units, tokens, inner)
    state_shape = (units, inner, LANES)
    peer_sems = DMA((units, n - 1))
    out_shape = ((batches, tokens, model), F32)
    kept_shapes = [
        ((units, rows, model + LANES), BF),
        ((units, rows, wide), BF),
        (inner_shape, F32),
        (lane_shape, F32),
        (lane_shape, F32),
        (lane_shape, F32),
        ((units, tokens, wide), BF),
        (state_shape, BF),
        (inner_shape, F32),
        (lane_shape, F32),
        ((count, tokens, model), BF),
        ((2,) + wc.shape, BF),
        ((2,) + w_out.shape[1:], BF),
    ]
    car, pr, seg_col, srow, pad, *kept = comm(
        functools.partial(fwd_kernel, seqs, n),
        (hidden_in, segments, padding, norm_gain, conv_x, conv_x_bias, conv_bc, conv_bc_bias,
         dt_bias, a_log, skip_d, gate_gain, wc, w_out[0]),
        [
            ((units, heads, LANES), F32),
            ((2, 16, model), F32),
            ((count, rows, LANES), F32),
            ((count, 8, tokens), F32),
            ((count, tokens, LANES), F32),
        ]
        + kept_shapes,
        [pltpu.VMEM(*x) for x in kept_shapes]
        + [
            pltpu.VMEM((count, HALO, model), F32),
            pltpu.VMEM((count, HALO, LANES), F32),
            pltpu.VMEM((16, model), F32),
            pltpu.VMEM((count, tokens, model), F32),
            pltpu.VMEM((rows, wide), F32),
            pltpu.VMEM((inner, LANES), F32),
            pltpu.VMEM(state_shape, BF),
            pltpu.VMEM((tokens, inner), F32),
            pltpu.VMEM((count, tokens, model), BF),
            pltpu.VMEM((count, n - 1, part_rows, model), BF),
            pltpu.VMEM((units, 8, tokens), F32),
            pltpu.VMEM((units, n - 1, 8, tokens), F32),
            DMA((units, PIECES)), DMA((units, PIECES)),
            peer_sems, peer_sems, peer_sems, peer_sems, peer_sems, peer_sems,
            DMA((count, n)), DMA((count,)), DMA((1,)),
            DMA((5,)), DMA((5,)), DMA((11, units)), DMA((2, 2)),
        ],
        1, "fwd", len(kept_shapes), 1,
    )
    normed, raw, z, dtp, dt, cum, co, st, yn, gsc, part, wc, wo = kept
    total_rows = model + inner + 2 * state
    chunk_sems = DMA((total_rows // CHUNK,))
    more_sems = DMA((units + count, n - 1))
    table_shape = (32, model)
    grad_shape = (tokens, model + 2 * state)
    big, table, input_grad, layer_out = comm(
        functools.partial(bwd_kernel, seqs, n),
        (cotangent, hidden_in, normed, wc, wo, raw, z, dtp, dt, cum, co, st, yn, gsc,
         part, pad, car, seg_col, srow, pr),
        (((total_rows * 3 // 2, model), TOTAL_T), (table_shape, F32), out_shape, out_shape),
        [
            pltpu.VMEM((units, tokens, model), F32),
            pltpu.VMEM((count, tokens, model), F32),
            pltpu.VMEM((units, rows, model + LANES), BF),
            pltpu.VMEM(wc.shape[1:], BF),
            pltpu.VMEM(wo.shape[1:], BF),
            pltpu.VMEM((count, rows, wide), BF),
            pltpu.VMEM((count, tokens, inner), F32),
            pltpu.VMEM((count, tokens, LANES), F32),
            pltpu.VMEM((count, tokens, LANES), F32),
            pltpu.VMEM((count, tokens, LANES), F32),
            pltpu.VMEM((count, tokens, wide), BF),
            pltpu.VMEM((count, inner, LANES), BF),
            pltpu.VMEM((count, tokens, inner), F32),
            pltpu.VMEM((count, tokens, LANES), F32),
            pltpu.VMEM((2, total_rows, model), TOTAL_T),
            pltpu.VMEM((2, total_rows // 2, model), TOTAL_T),
            pltpu.VMEM((2,) + table_shape, F32),
            pltpu.VMEM(table_shape, F32),
            pltpu.VMEM(table_shape, F32),
            pltpu.VMEM(table_shape, F32),
            pltpu.VMEM((rows, wide), F32),
            pltpu.VMEM((rows + HALO, LANES), F32),
            pltpu.VMEM((tokens, wide), F32),
            pltpu.VMEM((count, rows, wide), BF),
            pltpu.VMEM((count, tokens, inner), BF),
            pltpu.VMEM((tokens, inner), BF),
            pltpu.VMEM((count, tokens, inner), BF),
            pltpu.VMEM((count, tokens, LANES), BF),
            pltpu.VMEM((inner, LANES), F32),
            pltpu.VMEM(state_shape, BF),
            pltpu.VMEM((count, inner, LANES), BF),
            pltpu.VMEM((count,) + grad_shape, BF),
            pltpu.VMEM((units, HALO, model + 2 * state), BF),
            pltpu.VMEM((count, n - 1, part_rows, model + 2 * state), BF),
            pltpu.VMEM((units, n, HALO, model + 2 * state), BF),
            pltpu.VMEM((part_rows, model + 2 * state), F32),
            pltpu.VMEM((count,) + grad_shape, BF),
            pltpu.VMEM((model, 2 * state), F32),
            pltpu.VMEM((2, 8, 2 * state), F32),
            pltpu.VMEM((2, n - 1, 8, 2 * state), F32),
            pltpu.VMEM((tokens, inner), F32),
            pltpu.VMEM((units, 8, tokens), F32),
            pltpu.VMEM((units, n - 1, 8, tokens), F32),
            DMA((units, PIECES)), DMA((units, PIECES)),
            more_sems, more_sems, more_sems, more_sems,
            DMA((units,)), DMA((units, n)),
            DMA((2, n - 1)), DMA((2, n - 1)),
            DMA((count,)), DMA((count,)), DMA((count,)), DMA((3,)),
            peer_sems, peer_sems,
            DMA((9, count)), DMA((2,)),
            chunk_sems, chunk_sems, chunk_sems, chunk_sems, chunk_sems, chunk_sems,
            DMA((3,)), DMA((3,)), DMA((count,)), DMA((count,)), DMA((count,)),
            DMA((total_rows // CHUNK // 2,)), DMA((total_rows // CHUNK // 2,)), DMA((count,)),
        ],
        2, "bwd", 2, 15,
    )
    (g_zx, g_wo, g_bc, layer_out, input_grad, rms, g_norm, g_dt, g_cx, g_cxb, g_cb, g_cbb, g_dtb, g_al, g_sk,
     g_gate) = finalize(
        big, table, layer_out, input_grad, inner, heads, state
    )
    return (layer_out, input_grad, rms, g_norm, g_zx, g_bc,
            jnp.transpose(g_dt, (0, 2, 1)), g_cx, g_cxb,
            g_cb, g_cbb, g_dtb, g_al, g_sk, g_gate, g_wo)


def solution(mesh):
    in_specs = (
        P(None, SEQ, None),
        P(None, SEQ, None),
        P(None, SEQ),
        P(None, SEQ),
        P(SEC, None),
        P(SEC, None, None, HEAD),
        P(SEC, None, None),
        P(SEC, None, HEAD),
        P(SEC, None, HEAD),
        P(SEC, HEAD),
        P(SEC, None, None),
        P(SEC, None),
        P(SEC, HEAD),
        P(SEC, HEAD),
        P(SEC, HEAD),
        P(SEC, HEAD),
        P(SEC, HEAD, None),
    )
    out_specs = (
        P(SEC, None, SEQ, None),
        P(SEC, None, SEQ, None),
        P(SEC, None),
        P(SEC, None),
        P(SEC, None, None, HEAD),
        P(SEC, None, None),
        P(SEC, None, HEAD),
        P(SEC, None, HEAD),
        P(SEC, HEAD),
        P(SEC, None, None),
        P(SEC, None),
        P(SEC, HEAD),
        P(SEC, HEAD),
        P(SEC, HEAD),
        P(SEC, HEAD),
        P(SEC, HEAD, None),
    )
    return jax.shard_map(local, mesh=mesh, in_specs=in_specs, out_specs=out_specs, check_vma=False)
```
